32 devices in a mesh: view: 8 (over z, y), feat: 4 (over x, core).
Axes of the slice: x: 2, y: 2, z: 4, core: 2. Of those that a mesh axis runs over, the one named last changes fastest.
Arguments:
- points: bfloat16 [512, 768, 128], P('view', 'feat'), may hold values from -6 to 6
- head_weight: bfloat16 [768, 768], P('feat'), may hold values from -0.21875 to 0.21875
- teacher: bfloat16 [768, 16, 1369], P('feat', 'view'), may hold values from -6 to 6
- splat_weight: bfloat16 [16, 64, 74, 128], P('view'), may hold values from 0 to 0.19921875
- block_owner: int32 [16, 16, 4], P('view'), may hold values from 0 to 7, all different within a row; in each aligned block of 32 rows (0 to 31, 32 to 63, ..., all dimensions but the last counted through in order) at most 24 rows name the same one
- block_local: int32 [16, 64], P('view'), may hold values from 0 to 63
- block_row: int32 [16, 64], P('view'), may hold values from 0 to 35, as said below
Outputs:
- grad_points: bfloat16 [512, 768, 128], P('view', 'feat')
- head_grad: float32 [768, 768], P('feat')
The draws below stay inside these ranges and needn't reach their ends.
Inputs may be any that keep to these rules, and one draw needn't show every extreme that they name: `block_owner`: over the 128 list entries of the views of one index of view, no owner appears more than 24 times, and some owner appears exactly 24 times. `block_row`: each view's list holds every value from 0 to 35 at least once.
All inputs are finite; a program needn't handle non-finite values.
Results may differ from the reference program's by a relative error of at most 0.0064.
Values may be sent and summed in bfloat16 or wider, within the bound.
No kernel may reach another device: no remote copies, remote signals or barrier semaphores. Data moves between devices by JAX's collectives and lax.ppermute only.
A program may use at most 128 MiB of HBM per device.

```python
import math
import jax
import jax.numpy as jnp
import numpy as np
from jax import lax

D = 768
DT = 768
GRID = 37
BAND = 2
BLOCK = 128
VIEW_DEV = 2
NVIS = 64
BLK_DEV = 64
VIEWS = 16
NBLK = 512
PIX = 1369
CAP = 24
N_VIEW = 8


def draw_block_row(key, part):
    row_range = GRID - BAND + 1
    view_keys = jax.random.split(key, VIEWS)
    leading = jax.vmap(lambda view_key: jax.random.permutation(view_key, row_range))(view_keys).astype(jnp.int32)
    others = jax.random.randint(jax.random.fold_in(key, 7), (VIEWS, NVIS - row_range), 0, row_range, dtype=jnp.int32)
    return jnp.concatenate([leading, others], axis=1)


def plant(entries, stream_key, smallest, largest):
    dims = entries.shape
    place = [jax.random.randint(jax.random.fold_in(stream_key, axis), (), 0, dims[axis]) for axis in range(len(dims))]
    entries = entries.at[tuple(place)].set(smallest)
    longest = dims.index(max(dims))
    place[longest] = (place[longest] + 1) % dims[longest]
    return entries.at[tuple(place)].set(largest)


def steps_of(rng, shape, cuts, low, top_value):
    def one(axis_at, shards_of):
        heights = jax.random.uniform(jax.random.fold_in(jax.random.fold_in(rng, 6), axis_at), (shards_of,), jnp.float32, low / len(cuts), top_value / len(cuts))
        return jnp.repeat(jnp.exp(heights), shape[axis_at] // shards_of).reshape((-1,) + (1,) * (len(shape) - axis_at - 1))

    level = one(*cuts[0])
    for cut in cuts[1:]:
        level = level * one(*cut)
    return level


def shared_out(own_key, own, number, rows, amount, top, most, slope):
    ranking = jax.random.permutation(own_key, amount)
    crowded, ordinary = portions_of(amount, rows * top, most, slope, True), portions_of(amount, rows * top, most, slope, False)
    places = jnp.arange(amount)

    def named(sizes, offset_by):
        used = int((sizes > 0).sum())
        fixed = max(1, used // 4)
        moved = fixed + (places - fixed + offset_by * (used - fixed)) % max(1, amount - fixed)
        return jnp.zeros((amount,), jnp.int32).at[ranking[jnp.where(places < fixed, places, moved)]].set(jnp.asarray(sizes, jnp.int32))

    sizes = jnp.where(number % 4 == 0, named(crowded, number // 4), named(ordinary, number - number // 4 - 1))
    mixed = jax.random.permutation(jax.random.fold_in(own, 3), amount)
    source_of, receiver = mixed[0:amount // 2 * 2:2], mixed[1:amount // 2 * 2:2]
    margin = jnp.minimum(sizes[source_of] - 1, most - sizes[receiver]) // 2
    margin = jnp.where((source_of == ranking[0]) | (receiver == ranking[0]) | (sizes[receiver] == 0), 0, jnp.maximum(margin, 0))
    moved = jax.random.randint(jax.random.fold_in(own, 4), (amount // 2,), 0, 1 << 20) % (margin + 1)
    sizes = sizes.at[source_of].add(-moved).at[receiver].add(moved)
    items = jnp.searchsorted(jnp.cumsum(sizes), jnp.arange(rows * top), side="right").astype(jnp.int32)
    table = items.reshape(top, rows).T
    table = table[jax.random.permutation(jax.random.fold_in(own, 1), rows)]
    offset_by = jax.random.randint(jax.random.fold_in(own, 2), (rows, 1), 0, top)
    return jnp.take_along_axis(table, (jnp.arange(top)[None, :] + offset_by) % top, axis=1)


def portions_of(number_of, total, limit, skew, full):
    weights = [(1 << 20) // math.isqrt(grade ** skew) + 1 for grade in range(1, number_of + 1)]
    largest = limit if full else min(limit, max(-(-total // number_of), total * weights[0] // sum(weights)))
    least = 1 if total - largest >= number_of - 1 else 0
    given, spare = [largest] + [least] * (number_of - 1), total - largest - least * (number_of - 1)
    while spare > 0:
        free = [i for i in range(1, number_of) if given[i] < largest] or [i for i in range(1, number_of) if given[i] < limit]
        pool, remaining = sum([weights[i] for i in free]), spare
        for i in free:
            addition = min(limit - given[i], max(1, remaining * weights[i] // pool), spare)
            given[i] = given[i] + addition
            spare = spare - addition
    return np.array(given)


def scatter_about(key, extent, width, limit, cuts=(), held_as=jnp.bfloat16):
    level = steps_of(key, extent, cuts, -0.22, 0.18) if cuts else 1.0
    result = jax.random.normal(key, extent, jnp.float32) * width * level
    return jnp.minimum(jnp.maximum(result, -limit), limit).astype(held_as)


def setup_inputs(seed: int = 0) -> dict:
    key_of = jax.random.split(jax.random.key(seed), 8)
    points = scatter_about(key_of[0], (NBLK, D, BLOCK), 1.0, 6.0, ((0, 8), (1, 4)))
    head_weight = scatter_about(key_of[1], (D, DT), D ** -0.5, 0.21875, ((0, 4),))
    teacher = scatter_about(key_of[2], (DT, VIEWS, PIX), 1.0, 6.0, ((0, 4), (1, 8)))
    splat_weight = jnp.clip(0.19921875 * jax.random.uniform(key_of[3], (VIEWS, NVIS, BAND * GRID, BLOCK), jnp.float32) ** steps_of(key_of[3], (VIEWS, NVIS, BAND * GRID, BLOCK), ((0, 8),), -0.2, 0.2), 0.0, 0.19921875).astype(jnp.bfloat16)
    block_owner_keys = jax.random.split(jax.random.fold_in(key_of[4], 1), VIEWS * (NVIS // 4) // (VIEW_DEV * NVIS // 4))
    block_owner_turns = jax.random.permutation(jax.random.fold_in(key_of[4], 3), VIEWS * (NVIS // 4) // (VIEW_DEV * NVIS // 4))
    block_owner = jax.vmap(lambda own, number: shared_out(jax.random.fold_in(key_of[4], 2), own, number, VIEW_DEV * NVIS // 4, N_VIEW, 4, CAP, 2))(block_owner_keys, block_owner_turns).reshape((VIEWS, NVIS // 4, 4))
    block_local = plant(jax.random.randint(key_of[5], (VIEWS, NVIS), 0, BLK_DEV), jax.random.fold_in(key_of[5], 1), 0, BLK_DEV - 1).astype(jnp.int32)
    block_row = draw_block_row(jax.random.fold_in(key_of[7], 71), 0)
    return {"points": points, "head_weight": head_weight, "teacher": teacher, "splat_weight": splat_weight, "block_owner": block_owner, "block_local": block_local, "block_row": block_row}


def reference(points, head_weight, teacher, splat_weight, block_owner, block_local, block_row):
    blocks = points
    owners = block_owner.reshape(VIEWS, NVIS)
    global_ids = (owners * BLK_DEV + block_local).astype(jnp.int32)
    teacher_views = jnp.moveaxis(teacher, 1, 0)
    columns = jnp.arange(GRID, dtype=jnp.int32)

    def one_view(state_pair, inputs):
        grad_acc, head_acc = state_pair
        weights, view_ids, top_rows, target_feat = inputs
        fetched = blocks[view_ids]
        contrib = jnp.einsum('jcp,jdp->jcd', weights.astype(jnp.float32), fetched.astype(jnp.float32)).astype(jnp.bfloat16)
        rendered = jnp.zeros((GRID, GRID, D), jnp.float32)
        row_masks = []
        for offset in range(BAND):
            row_mask = (top_rows[:, None] + offset == columns[None, :]).astype(jnp.float32)
            row_masks.append(row_mask)
            band_part = contrib[:, offset * GRID:(offset + 1) * GRID, :].astype(jnp.float32)
            rendered = rendered + jnp.einsum('jr,jcd->rcd', row_mask, band_part)
        rendered = rendered.astype(jnp.bfloat16).reshape(PIX, D)
        projected = jnp.dot(rendered, head_weight, preferred_element_type=jnp.float32)
        scale_rows = jnp.sqrt(lax.optimization_barrier(jnp.mean(projected * projected, axis=1, keepdims=True)) + 1e-06)
        normed = projected / scale_rows
        residual = normed - target_feat.T.astype(jnp.float32)
        row_dot = lax.optimization_barrier(jnp.mean(residual * normed, axis=1, keepdims=True))
        grad_proj = ((residual - normed * row_dot) / scale_rows).astype(jnp.bfloat16)
        grad_image = jnp.dot(grad_proj, head_weight.T, preferred_element_type=jnp.float32).astype(jnp.bfloat16)
        grad_image = grad_image.reshape(GRID, GRID, D).astype(jnp.float32)
        grad_head = jnp.dot(rendered.T, grad_proj, preferred_element_type=jnp.float32)
        pieces = [jnp.einsum('jr,rcd->jcd', row_mask, grad_image) for row_mask in row_masks]
        grad_contrib = jnp.concatenate(pieces, axis=1).astype(jnp.bfloat16)
        grad_block = jnp.einsum('jcp,jcd->jdp', weights.astype(jnp.float32), grad_contrib.astype(jnp.float32)).astype(jnp.bfloat16)
        grad_acc = grad_acc.at[view_ids].add(grad_block.astype(jnp.float32))
        return ((grad_acc, head_acc + grad_head), None)
    start_state = (jnp.zeros((NBLK, D, BLOCK), jnp.float32), jnp.zeros((D, DT), jnp.float32))
    final_state, _ = lax.scan(one_view, start_state, (splat_weight, global_ids, block_row, teacher_views))
    grad_acc, head_acc = final_state
    grad_points = grad_acc.astype(jnp.bfloat16)
    head_grad = head_acc / (VIEWS * GRID)
    return (grad_points, head_grad)
```

```python
import jax
import jax.numpy as jnp
from jax import lax
from jax.experimental import pallas as pl
from jax.experimental.pallas import tpu as pltpu
from jax.sharding import PartitionSpec as P

GRID = 37
BAND = 2
BLOCK = 128
GROUP = 4
VMEM_BYTES = 48 * 1024 * 1024


def slot_plan(owners, peer_count, capacity):
    total_requests = owners.shape[0]
    positions = jnp.arange(total_requests, dtype=jnp.int32)
    earlier = (owners[:, None] == owners[None, :]) & (positions[None, :] < positions[:, None])
    slot_rank = jnp.sum(earlier.astype(jnp.int32), axis=1)
    target = owners * capacity + slot_rank
    slot_ids = jnp.arange(peer_count * capacity, dtype=jnp.int32)
    matches = target[None, :] == slot_ids[:, None]
    source = jnp.sum(jnp.where(matches, positions[None, :], 0), axis=1)
    filled = jnp.any(matches, axis=1)
    return (target, source, filled)


def per_device_listed(points, head_weight, teacher, splat_weight, block_owner, block_local, block_row):
    peer_count = lax.axis_size("view")
    local_width = points.shape[1]
    view_count = splat_weight.shape[0]
    visible = splat_weight.shape[1]
    requests = view_count * visible
    capacity = max(3, (3 * requests + 2 * peer_count - 1) // (2 * peer_count))
    owners = block_owner.reshape(requests)
    local_ids = block_local.reshape(requests)
    target, source, filled = slot_plan(owners, peer_count, capacity)
    wanted = jnp.where(filled, jnp.take(local_ids, source), 0)
    columns = jnp.arange(GRID, dtype=jnp.int32)
    row_masks = [
        (block_row[:, :, None] + offset == columns[None, None, :]).astype(jnp.bfloat16)
        for offset in range(BAND)
    ]
    empty_bf = jnp.zeros((), jnp.bfloat16)
    asked_ids = lax.all_to_all(wanted, "view", split_axis=0, concat_axis=0, tiled=True)
    sent_rows = jnp.take(points, asked_ids, axis=0)
    arrived = lax.all_to_all(sent_rows, "view", split_axis=0, concat_axis=0, tiled=True)
    fetched = jnp.take(arrived, target, axis=0).reshape(view_count, visible, local_width, BLOCK)
    contrib = jnp.einsum(
        "vjcp,vjdp->vjcd", splat_weight, fetched, preferred_element_type=jnp.float32
    ).astype(jnp.bfloat16)
    rendered = jnp.zeros((view_count, GRID, GRID, local_width), jnp.float32)
    for offset in range(BAND):
        band_part = contrib[:, :, offset * GRID : (offset + 1) * GRID, :]
        rendered = rendered + jnp.einsum(
            "vjr,vjcd->vrcd", row_masks[offset], band_part, preferred_element_type=jnp.float32
        )
    rendered_rows = rendered.astype(jnp.bfloat16).reshape(view_count * GRID * GRID, local_width)
    pixel_rows = rendered_rows.shape[0]
    teacher_width = head_weight.shape[1]
    local_teacher = teacher.shape[0]
    contract_first = (((0,), (1,)), ((), ()))
    head_full = lax.all_gather(head_weight, "feat", axis=0, tiled=True)
    head_cols = lax.dynamic_slice_in_dim(
        head_full, lax.axis_index("feat") * local_teacher, local_teacher, 1
    )
    head_part = head_cols
    projected = lax.dot_general(
        head_part,
        lax.all_gather(rendered_rows, "feat", axis=1, tiled=True),
        contract_first,
        preferred_element_type=jnp.float32,
    )
    square_sum = lax.psum(jnp.sum(projected * projected, axis=0), "feat")
    scale_rows = jnp.sqrt(square_sum / teacher_width + 1e-06)
    normed = projected / scale_rows[None, :]
    target_feat = teacher.reshape(local_teacher, pixel_rows).astype(jnp.float32)
    residual = normed - target_feat
    row_dot = lax.psum(jnp.sum(residual * normed, axis=0), "feat")
    grad_proj = (
        (residual - normed * (row_dot / teacher_width)[None, :]) / scale_rows[None, :]
    ).astype(jnp.bfloat16)
    shard_part = lax.all_gather(grad_proj, "feat", axis=0, tiled=True)
    head_part = head_weight
    grad_image = lax.dot_general(
        shard_part, head_part, contract_first, preferred_element_type=jnp.float32
    )
    column_part = lax.dot_general(
        rendered_rows, shard_part, contract_first, preferred_element_type=jnp.float32
    )
    grad_head = column_part
    grad_image, grad_head = (grad_image, grad_head)
    head_grad = lax.psum(grad_head, "view") / (view_count * peer_count * GRID)
    grad_image = grad_image.astype(jnp.bfloat16).reshape(view_count, GRID, GRID, local_width)
    pieces = [
        jnp.einsum("vjr,vrcd->vjcd", row_mask, grad_image, preferred_element_type=jnp.float32)
        for row_mask in row_masks
    ]
    grad_contrib = jnp.concatenate(pieces, axis=2).astype(jnp.bfloat16)
    grad_block = jnp.einsum(
        "vjcp,vjcd->vjdp", splat_weight, grad_contrib, preferred_element_type=jnp.float32
    ).astype(jnp.bfloat16)
    grad_block = grad_block.reshape(requests, local_width, BLOCK)
    packed = jnp.where(filled[:, None, None], jnp.take(grad_block, source, axis=0), empty_bf)
    landed = lax.all_to_all(packed, "view", split_axis=0, concat_axis=0, tiled=True)
    summed = jax.ops.segment_sum(
        landed.astype(jnp.float32), asked_ids, num_segments=points.shape[0]
    )
    grad_points = summed.astype(jnp.bfloat16)
    return (grad_points, head_grad)


def shifted(weight, start):
    rows = jnp.concatenate([weight.astype(jnp.float32), jnp.zeros((8, BLOCK), jnp.float32)], axis=0)
    return pltpu.roll(rows, lax.rem(start, 8), 0).astype(jnp.bfloat16)


def rows_at(start, band_rows):
    return pl.ds(pl.multiple_of((start // 8) * 8, 8), band_rows + 8)


def render_kernel(
    half_rows, band_rows, count_ref, block_ref, place_ref, where_ref, weight_ref, points_ref, *rest
):
    outs, acc = rest[:-1], rest[-1]
    width = points_ref.shape[1]
    acc[...] = jnp.zeros_like(acc)

    def group(step, carry):
        parts = []
        for t in range(GROUP):
            slot = step * GROUP + t
            parts.append(
                lax.dot_general(
                    shifted(weight_ref[where_ref[slot]], place_ref[slot]),
                    points_ref[block_ref[slot]],
                    (((1,), (1,)), ((), ())),
                    preferred_element_type=jnp.float32,
                )
            )
        for t in range(GROUP):
            rows = rows_at(place_ref[step * GROUP + t], band_rows)
            acc[rows, 0:width] += parts[t]
        return carry

    lax.fori_loop(0, (count_ref[0] + GROUP - 1) // GROUP, group, 0)
    lane = lax.broadcasted_iota(jnp.int32, (half_rows, 128), 1)
    for u, out in enumerate(outs):
        first = acc[2 * u * half_rows : (2 * u + 1) * half_rows, :]
        second = pltpu.roll(acc[(2 * u + 1) * half_rows : (2 * u + 2) * half_rows, :], 64, 1)
        out[:, 0:128] = first[:, 0:128].astype(out.dtype)
        out[:, 128:256] = jnp.where(lane < 64, first[:, 128:256], second[:, 0:128]).astype(out.dtype)
        out[:, 256:384] = second[:, 128:256].astype(out.dtype)


def render(count, block, place, where, weight, points, view_count, half_rows):
    width = points.shape[1]
    band_rows = weight.shape[1]
    smem = pl.BlockSpec(memory_space=pltpu.SMEM)
    vmem = pl.BlockSpec(memory_space=pltpu.VMEM)
    image = jax.ShapeDtypeStruct((half_rows, 2 * width), jnp.bfloat16)
    return pl.pallas_call(
        lambda *refs: render_kernel(half_rows, band_rows, *refs),
        out_shape=[image] * view_count,
        in_specs=[smem] * 4 + [vmem] * 2,
        out_specs=[vmem] * view_count,
        scratch_shapes=[pltpu.VMEM((2 * view_count * half_rows + band_rows + 8, 256), jnp.float32)],
        compiler_params=pltpu.CompilerParams(vmem_limit_bytes=VMEM_BYTES),
        name="render_blocks",
    )(count, block, place, where, weight, points)


def loss_kernel(teacher_width, parts_ref, head_ref, teacher_ref, image_ref, grad_ref):
    rows, packed = parts_ref.shape[1], parts_ref.shape[2]
    width = packed // 2
    lane = lax.broadcasted_iota(jnp.int32, (rows, packed), 1)
    head = head_ref[...]
    halves = [[], []]
    for pair in range(2):
        one = parts_ref[2 * pair].astype(jnp.float32)
        two = parts_ref[2 * pair + 1].astype(jnp.float32)
        halves[0].append(jnp.where(lane < width, one, pltpu.roll(two, width, 1)))
        halves[1].append(jnp.where(lane < width, pltpu.roll(one, width, 1), two))
    rendered_all, grad_all, images = [], [], []
    for half in range(2):
        rendered = jnp.concatenate(halves[half], axis=1).astype(jnp.bfloat16)
        projected = jnp.dot(rendered, head, preferred_element_type=jnp.float32)
        square = jnp.sum(projected * projected, axis=1, keepdims=True)
        scale = jnp.sqrt(square / teacher_width + 1e-06)
        normed = projected / scale
        residual = normed - teacher_ref[half].astype(jnp.float32)
        inner = jnp.sum(residual * normed, axis=1, keepdims=True) / teacher_width
        grad_proj = ((residual - normed * inner) / scale).astype(jnp.bfloat16)
        images.append(
            lax.dot_general(
                grad_proj, head, (((1,), (1,)), ((), ())), preferred_element_type=jnp.float32
            )
        )
        rendered_all.append(rendered)
        grad_all.append(grad_proj)
    for pair in range(2):
        cols = slice(2 * pair * width, 2 * (pair + 1) * width)
        first, second = images[0][:, cols], images[1][:, cols]
        image_ref[2 * pair] = jnp.where(lane < width, first, pltpu.roll(second, width, 1)).astype(
            image_ref.dtype
        )
        image_ref[2 * pair + 1] = jnp.where(
            lane < width, pltpu.roll(first, width, 1), second
        ).astype(image_ref.dtype)
    grad_ref[...] = lax.dot_general(
        jnp.concatenate(rendered_all, axis=0),
        jnp.concatenate(grad_all, axis=0),
        (((0,), (0,)), ((), ())),
        preferred_element_type=jnp.float32,
    )


def loss(parts, head, teacher):
    vmem = pl.BlockSpec(memory_space=pltpu.VMEM)
    teacher_width = head.shape[1]
    return pl.pallas_call(
        lambda *refs: loss_kernel(teacher_width, *refs),
        out_shape=[
            jax.ShapeDtypeStruct(parts.shape, jnp.bfloat16),
            jax.ShapeDtypeStruct(head.shape, jnp.float32),
        ],
        in_specs=[vmem] * 3,
        out_specs=[vmem] * 2,
        compiler_params=pltpu.CompilerParams(vmem_limit_bytes=VMEM_BYTES),
        name="loss_rows",
    )(parts, head, teacher)


def pull_kernel(
    half_rows, band_rows, view_count, first, last,
    count_ref, block_ref, place_ref, where_ref, weight_ref, image_refs, old_ref, out_ref, image, acc
):
    step_of = pl.program_id(0)
    width = acc.shape[1]
    blocks = out_ref.shape[0]

    @pl.when(step_of == 0)
    def _():
        if first:
            acc[...] = jnp.zeros_like(acc)
        else:
            acc[0:blocks] = old_ref[...]

    for u in range(view_count):
        packed = image_refs[u][0].astype(jnp.float32)
        image[2 * u * half_rows : (2 * u + 1) * half_rows, :] = packed[:, 0:256]
        tail = jnp.concatenate([packed[:, 128:384]], axis=1)
        image[(2 * u + 1) * half_rows : (2 * u + 2) * half_rows, :] = pltpu.roll(tail, 192, 1)

    slots = weight_ref.shape[1]
    base = step_of * slots

    def group(step, carry):
        parts = []
        for t in range(GROUP):
            slot = base + step * GROUP + t
            rows = rows_at(place_ref[slot], band_rows)
            parts.append(
                lax.dot_general(
                    image[rows, 0:width].astype(jnp.bfloat16),
                    shifted(weight_ref[0, where_ref[slot]], place_ref[slot]),
                    (((0,), (0,)), ((), ())),
                    preferred_element_type=jnp.float32,
                )
            )
        for t in range(GROUP):
            slot = base + step * GROUP + t
            acc[block_ref[slot]] += parts[t]
        return carry

    lax.fori_loop(0, (count_ref[step_of] + GROUP - 1) // GROUP, group, 0)

    @pl.when(step_of == pl.num_programs(0) - 1)
    def _():
        out_ref[...] = acc[0:blocks].astype(out_ref.dtype)


def pull(count, block, place, where, weight, images, old, blocks, width, last):
    view_count = len(images)
    peers, slots, band_rows, points = weight.shape
    half_rows = images[0].shape[1]
    first = old is None
    smem = pl.BlockSpec(memory_space=pltpu.SMEM)
    vmem = pl.BlockSpec(memory_space=pltpu.VMEM)

    def body(count_ref, block_ref, place_ref, where_ref, weight_ref, *rest):
        image_refs, rest = rest[:view_count], rest[view_count:]
        if first:
            rest = (None,) + rest
        pull_kernel(
            half_rows, band_rows, view_count, first, last,
            count_ref, block_ref, place_ref, where_ref, weight_ref, image_refs, *rest
        )

    args = [count, block, place, where, weight] + list(images)
    in_specs = [smem] * 4 + [pl.BlockSpec((1, slots, band_rows, points), lambda i: (i, 0, 0, 0))]
    in_specs += [pl.BlockSpec((1,) + images[0].shape[1:], lambda i: (i, 0, 0))] * view_count
    if not first:
        args.append(old)
        in_specs.append(vmem)
    return pl.pallas_call(
        body,
        grid=(peers,),
        out_shape=jax.ShapeDtypeStruct((blocks, width, points), jnp.bfloat16 if last else jnp.float32),
        in_specs=in_specs,
        out_specs=vmem,
        scratch_shapes=[
            pltpu.VMEM((2 * view_count * half_rows + band_rows + 8, 256), jnp.float32),
            pltpu.VMEM((blocks + 1, width, points), jnp.float32),
        ],
        compiler_params=pltpu.CompilerParams(vmem_limit_bytes=VMEM_BYTES),
        name="pull_blocks",
    )(*args)


def total(*terms):
    acc = terms[0].astype(jnp.float32)
    for term in terms[1:]:
        acc = acc + term.astype(jnp.float32)
    return acc.astype(jnp.bfloat16)


def in_order(own_first, other):
    index, mine = own_first
    return jnp.where(
        index == 0, jnp.concatenate([mine, other], 0), jnp.concatenate([other, mine], 0)
    )


def per_device(points, head_weight, teacher, splat_weight, block_owner, block_local, block_row):
    peers, sides = lax.axis_size("view"), lax.axis_size("feat")
    blocks, width = points.shape[0], points.shape[1]
    view_count, visible, band_rows = splat_weight.shape[:3]
    requests = view_count * visible
    capacity = max(3, (3 * requests + 2 * peers - 1) // (2 * peers))
    quarter = -(-capacity // sides)
    slots = quarter * sides
    pixels = teacher.shape[2]
    unit = 2 * sides * 16
    padded = -(-pixels // unit) * unit
    half_rows = padded // 2
    me, side = lax.axis_index("view"), lax.axis_index("feat")
    line, across, core = me // 2, side // 2, side % 2

    def hop(value, axis, pairs):
        return lax.ppermute(value, axis, pairs)

    def swap(value, axis, k):
        size = peers if axis == "view" else sides
        return hop(value, axis, [(i, i ^ k) for i in range(size)])

    def along(value, moves):
        return hop(value, "view", [(2 * a + y, 2 * b + y) for a, b in moves for y in range(2)])

    ints = jnp.int32
    owners = block_owner.reshape(requests)
    positions = jnp.arange(requests, dtype=ints)
    earlier = (owners[:, None] == owners[None, :]) & (positions[None, :] < positions[:, None])
    rank = jnp.sum(earlier.astype(ints), axis=1)
    peer_ids = me ^ jnp.arange(peers, dtype=ints)
    send_ranks = side * quarter + jnp.arange(quarter, dtype=ints)
    match = (owners[None, None, :] == peer_ids[:, None, None]) & (
        rank[None, None, :] == send_ranks[None, :, None]
    )
    source = jnp.sum(jnp.where(match, positions[None, None, :], 0), axis=2)
    aligned = -(-band_rows // 16) * 16
    listed = splat_weight.reshape(requests, band_rows, BLOCK)
    listed = jnp.pad(listed, ((0, 0), (0, aligned - band_rows), (0, 0)))
    packed = jnp.take(listed, source.reshape(peers * quarter), axis=0).reshape(
        peers, quarter, aligned, BLOCK
    )

    view_of = positions // visible
    start = view_of * padded + block_row.reshape(requests) * GRID
    told = jnp.stack([owners, rank, block_local.reshape(requests), start])
    heard = lax.all_gather(told, "view", axis=0)
    heard = jnp.take(heard, peer_ids, axis=0)
    slot_ids = jnp.arange(slots, dtype=ints)
    asked = (heard[:, None, 0, :] == me) & (heard[:, None, 1, :] == slot_ids[None, :, None])
    filled = jnp.any(asked, axis=2)
    counts = jnp.sum(filled.astype(ints), axis=1)
    block_of = jnp.sum(jnp.where(asked, heard[:, None, 2, :], 0), axis=2)
    place_of = jnp.where(
        filled, jnp.sum(jnp.where(asked, heard[:, None, 3, :], 0), axis=2), view_count * padded
    )
    pull_of = jnp.where(filled, block_of, blocks)
    turn = (slot_ids // quarter) ^ side
    turn = (turn % 2) * 2 + turn // 2
    where_of = turn * quarter + slot_ids % quarter

    weights = {}
    for j in (3, 2, 1, 0):
        got = jnp.stack([swap(packed[k], "view", k) if k else packed[k] for k in (2 * j, 2 * j + 1)])
        got = jnp.concatenate([got, swap(got, "feat", 2)], axis=1)
        weights[j] = jnp.concatenate([got, swap(got, "feat", 1)], axis=1)

    head = jnp.concatenate([head_weight, swap(head_weight, "feat", 2)], axis=0)
    head = jnp.concatenate([head, swap(head, "feat", 1)], axis=0)
    seventh = half_rows // sides
    target = jnp.pad(teacher, ((0, 0), (0, 0), (0, padded - pixels)))
    target = target.reshape(width, view_count, 2, sides, seventh).transpose(3, 1, 2, 4, 0)
    order = side ^ jnp.arange(sides, dtype=ints)
    target = jnp.take(target, order, axis=0)
    target = [swap(target[d], "feat", d) if d else target[d] for d in range(sides)]
    target = jnp.take(jnp.stack(target), order, axis=0)
    target = target.transpose(1, 2, 3, 0, 4).reshape(view_count, 2, seventh, sides * width)

    kept, sent = {}, {}
    for j in (3, 2, 1, 0):
        for k, into in ((2 * j + 1, sent), (2 * j, kept)):
            into[j] = render(
                counts[k : k + 1], block_of[k], place_of[k], where_of, weights[j][k - 2 * j], points,
                view_count, half_rows,
            )
    rendered = []
    for u in range(view_count):
        pair = {j: (kept[j][u], swap(sent[j][u], "view", 1)) for j in (3, 2, 1, 0)}
        far = along(total(*pair[3]), [(0, 1), (3, 2)])
        mid = total(*pair[2], far)
        inward = along(mid, [(0, 1), (3, 2)])
        between = along(mid, [(1, 2), (2, 1)])
        near = along(total(*pair[1], between), [(0, 1), (1, 0), (2, 3), (3, 2)])
        centre = along(total(*pair[3], inward), [(1, 2), (2, 1)])
        rendered.append(total(*pair[0], near, centre))

    grads, images = [], []
    side_rows = half_rows // 2
    for u in range(view_count):
        whole = rendered[u]
        mine = lax.dynamic_slice_in_dim(whole, across * side_rows, side_rows, 0)
        other = lax.dynamic_slice_in_dim(whole, (1 - across) * side_rows, side_rows, 0)
        both = jnp.stack([mine, swap(other, "feat", 2)])
        mine = lax.dynamic_slice_in_dim(both, core * seventh, seventh, 1)
        other = lax.dynamic_slice_in_dim(both, (1 - core) * seventh, seventh, 1)
        parts = jnp.concatenate([mine, swap(other, "feat", 1)], axis=0)
        image, grad = loss(parts, head, target[u])
        grads.append(grad)
        back = swap(image[2:4], "feat", 1)
        rows = [in_order((core, image[i]), back[i]) for i in range(2)]
        images.append(in_order((across, rows[0]), swap(rows[1], "feat", 2)))

    grad = grads[0]
    for more in grads[1:]:
        grad = grad + more
    grad = grad.reshape(2, 2, width, grad.shape[1])
    grad = grad[0] + swap(grad[1], "feat", 1)
    grad = grad[0] + swap(grad[1], "feat", 2)
    grad = lax.psum(grad, "view")
    head_grad = grad / (view_count * peers * GRID)

    middle = (line == 1) | (line == 2)
    chunks = {j: [] for j in range(4)}
    for u in range(view_count):
        own = images[u]
        near = along(own, [(0, 1), (1, 0), (2, 3), (3, 2)])
        centre = along(own, [(1, 2), (2, 1)])
        out_near = along(centre, [(1, 0), (2, 3)])
        cross = along(near, [(1, 2), (2, 1)])
        out_far = along(cross, [(1, 0), (2, 3)])
        for j, value in enumerate(
            (own, near, jnp.where(middle, cross, out_near), jnp.where(middle, centre, out_far))
        ):
            chunks[j].append(jnp.stack([value, swap(value, "view", 1)]))
    acc = None
    for j in range(4):
        ks = slice(2 * j, 2 * j + 2)
        acc = pull(
            counts[ks], pull_of[ks].reshape(-1), place_of[ks].reshape(-1), jnp.tile(where_of, 2),
            weights[j], chunks[j], acc, blocks, width, j == 3,
        )
    return (acc, head_grad)


def solution(mesh):
    size = mesh.shape
    paired = size["view"] == 8 and size["feat"] == 4
    placed = (
        P("view", "feat", None),
        P("feat", None),
        P("feat", "view", None),
        P("view", None, None, None),
        P("view", None, None),
        P("view", None),
        P("view", None),
    )
    return jax.shard_map(
        per_device if paired else per_device_listed,
        mesh=mesh,
        in_specs=placed,
        out_specs=(P("view", "feat", None), P("feat", None)),
        check_vma=False,
    )
```

```python
import jax
import jax.numpy as jnp
from jax import lax
from jax.experimental import pallas as pl
from jax.experimental.pallas import tpu as pltpu
from jax.sharding import PartitionSpec as P

GRID = 37
BAND = 2
BLOCK = 128
GROUP = 4
VMEM_BYTES = 48 * 1024 * 1024


def slot_plan(owners, peer_count, capacity):
    total_requests = owners.shape[0]
    positions = jnp.arange(total_requests, dtype=jnp.int32)
    earlier = (owners[:, None] == owners[None, :]) & (positions[None, :] < positions[:, None])
    slot_rank = jnp.sum(earlier.astype(jnp.int32), axis=1)
    target = owners * capacity + slot_rank
    slot_ids = jnp.arange(peer_count * capacity, dtype=jnp.int32)
    matches = target[None, :] == slot_ids[:, None]
    source = jnp.sum(jnp.where(matches, positions[None, :], 0), axis=1)
    filled = jnp.any(matches, axis=1)
    return (target, source, filled)


def per_device_listed(points, head_weight, teacher, splat_weight, block_owner, block_local, block_row):
    peer_count = lax.axis_size("view")
    local_width = points.shape[1]
    view_count = splat_weight.shape[0]
    visible = splat_weight.shape[1]
    requests = view_count * visible
    capacity = max(3, (3 * requests + 2 * peer_count - 1) // (2 * peer_count))
    owners = block_owner.reshape(requests)
    local_ids = block_local.reshape(requests)
    target, source, filled = slot_plan(owners, peer_count, capacity)
    wanted = jnp.where(filled, jnp.take(local_ids, source), 0)
    columns = jnp.arange(GRID, dtype=jnp.int32)
    row_masks = [
        (block_row[:, :, None] + offset == columns[None, None, :]).astype(jnp.bfloat16)
        for offset in range(BAND)
    ]
    empty_bf = jnp.zeros((), jnp.bfloat16)
    asked_ids = lax.all_to_all(wanted, "view", split_axis=0, concat_axis=0, tiled=True)
    sent_rows = jnp.take(points, asked_ids, axis=0)
    arrived = lax.all_to_all(sent_rows, "view", split_axis=0, concat_axis=0, tiled=True)
    fetched = jnp.take(arrived, target, axis=0).reshape(view_count, visible, local_width, BLOCK)
    contrib = jnp.einsum(
        "vjcp,vjdp->vjcd", splat_weight, fetched, preferred_element_type=jnp.float32
    ).astype(jnp.bfloat16)
    rendered = jnp.zeros((view_count, GRID, GRID, local_width), jnp.float32)
    for offset in range(BAND):
        band_part = contrib[:, :, offset * GRID : (offset + 1) * GRID, :]
        rendered = rendered + jnp.einsum(
            "vjr,vjcd->vrcd", row_masks[offset], band_part, preferred_element_type=jnp.float32
        )
    rendered_rows = rendered.astype(jnp.bfloat16).reshape(view_count * GRID * GRID, local_width)
    pixel_rows = rendered_rows.shape[0]
    teacher_width = head_weight.shape[1]
    local_teacher = teacher.shape[0]
    contract_first = (((0,), (1,)), ((), ()))
    head_full = lax.all_gather(head_weight, "feat", axis=0, tiled=True)
    head_cols = lax.dynamic_slice_in_dim(
        head_full, lax.axis_index("feat") * local_teacher, local_teacher, 1
    )
    head_part = head_cols
    projected = lax.dot_general(
        head_part,
        lax.all_gather(rendered_rows, "feat", axis=1, tiled=True),
        contract_first,
        preferred_element_type=jnp.float32,
    )
    square_sum = lax.psum(jnp.sum(projected * projected, axis=0), "feat")
    scale_rows = jnp.sqrt(square_sum / teacher_width + 1e-06)
    normed = projected / scale_rows[None, :]
    target_feat = teacher.reshape(local_teacher, pixel_rows).astype(jnp.float32)
    residual = normed - target_feat
    row_dot = lax.psum(jnp.sum(residual * normed, axis=0), "feat")
    grad_proj = (
        (residual - normed * (row_dot / teacher_width)[None, :]) / scale_rows[None, :]
    ).astype(jnp.bfloat16)
    shard_part = lax.all_gather(grad_proj, "feat", axis=0, tiled=True)
    head_part = head_weight
    grad_image = lax.dot_general(
        shard_part, head_part, contract_first, preferred_element_type=jnp.float32
    )
    column_part = lax.dot_general(
        rendered_rows, shard_part, contract_first, preferred_element_type=jnp.float32
    )
    grad_head = column_part
    grad_image, grad_head = (grad_image, grad_head)
    head_grad = lax.psum(grad_head, "view") / (view_count * peer_count * GRID)
    grad_image = grad_image.astype(jnp.bfloat16).reshape(view_count, GRID, GRID, local_width)
    pieces = [
        jnp.einsum("vjr,vrcd->vjcd", row_mask, grad_image, preferred_element_type=jnp.float32)
        for row_mask in row_masks
    ]
    grad_contrib = jnp.concatenate(pieces, axis=2).astype(jnp.bfloat16)
    grad_block = jnp.einsum(
        "vjcp,vjcd->vjdp", splat_weight, grad_contrib, preferred_element_type=jnp.float32
    ).astype(jnp.bfloat16)
    grad_block = grad_block.reshape(requests, local_width, BLOCK)
    packed = jnp.where(filled[:, None, None], jnp.take(grad_block, source, axis=0), empty_bf)
    landed = lax.all_to_all(packed, "view", split_axis=0, concat_axis=0, tiled=True)
    summed = jax.ops.segment_sum(
        landed.astype(jnp.float32), asked_ids, num_segments=points.shape[0]
    )
    grad_points = summed.astype(jnp.bfloat16)
    return (grad_points, head_grad)


def shifted(weight, start):
    rows = jnp.concatenate([weight.astype(jnp.float32), jnp.zeros((8, BLOCK), jnp.float32)], axis=0)
    return pltpu.roll(rows, lax.rem(start, 8), 0).astype(jnp.bfloat16)


def rows_at(start, band_rows):
    return pl.ds(pl.multiple_of((start // 8) * 8, 8), band_rows + 8)


def render_kernel(
    half_rows, band_rows, count_ref, block_ref, place_ref, where_ref, weight_ref, points_ref, *rest
):
    outs, acc = rest[:-1], rest[-1]
    width = points_ref.shape[1]
    acc[...] = jnp.zeros_like(acc)

    def group(step, carry):
        parts = []
        for t in range(GROUP):
            slot = step * GROUP + t
            parts.append(
                lax.dot_general(
                    shifted(weight_ref[where_ref[slot]], place_ref[slot]),
                    points_ref[block_ref[slot]],
                    (((1,), (1,)), ((), ())),
                    preferred_element_type=jnp.float32,
                )
            )
        for t in range(GROUP):
            rows = rows_at(place_ref[step * GROUP + t], band_rows)
            acc[rows, 0:width] += parts[t]
        return carry

    lax.fori_loop(0, (count_ref[0] + GROUP - 1) // GROUP, group, 0)
    lane = lax.broadcasted_iota(jnp.int32, (half_rows, 128), 1)
    for u, out in enumerate(outs):
        first = acc[2 * u * half_rows : (2 * u + 1) * half_rows, :]
        second = pltpu.roll(acc[(2 * u + 1) * half_rows : (2 * u + 2) * half_rows, :], 64, 1)
        out[:, 0:128] = first[:, 0:128].astype(out.dtype)
        out[:, 128:256] = jnp.where(lane < 64, first[:, 128:256], second[:, 0:128]).astype(out.dtype)
        out[:, 256:384] = second[:, 128:256].astype(out.dtype)


def render(count, block, place, where, weight, points, view_count, half_rows):
    width = points.shape[1]
    band_rows = weight.shape[1]
    smem = pl.BlockSpec(memory_space=pltpu.SMEM)
    vmem = pl.BlockSpec(memory_space=pltpu.VMEM)
    image = jax.ShapeDtypeStruct((half_rows, 2 * width), jnp.bfloat16)
    return pl.pallas_call(
        lambda *refs: render_kernel(half_rows, band_rows, *refs),
        out_shape=[image] * view_count,
        in_specs=[smem] * 4 + [vmem] * 2,
        out_specs=[vmem] * view_count,
        scratch_shapes=[pltpu.VMEM((2 * view_count * half_rows + band_rows + 8, 256), jnp.float32)],
        compiler_params=pltpu.CompilerParams(vmem_limit_bytes=VMEM_BYTES),
        name="render_blocks",
    )(count, block, place, where, weight, points)


def loss_kernel(teacher_width, parts_ref, head_ref, teacher_ref, image_ref, grad_ref):
    rows, packed = parts_ref.shape[1], parts_ref.shape[2]
    width = packed // 2
    lane = lax.broadcasted_iota(jnp.int32, (rows, packed), 1)
    head = head_ref[...]
    halves = [[], []]
    for pair in range(2):
        one = parts_ref[2 * pair].astype(jnp.float32)
        two = parts_ref[2 * pair + 1].astype(jnp.float32)
        halves[0].append(jnp.where(lane < width, one, pltpu.roll(two, width, 1)))
        halves[1].append(jnp.where(lane < width, pltpu.roll(one, width, 1), two))
    rendered_all, grad_all, images = [], [], []
    for half in range(2):
        rendered = jnp.concatenate(halves[half], axis=1).astype(jnp.bfloat16)
        projected = jnp.dot(rendered, head, preferred_element_type=jnp.float32)
        square = jnp.sum(projected * projected, axis=1, keepdims=True)
        scale = jnp.sqrt(square / teacher_width + 1e-06)
        normed = projected / scale
        residual = normed - teacher_ref[half].astype(jnp.float32)
        inner = jnp.sum(residual * normed, axis=1, keepdims=True) / teacher_width
        grad_proj = ((residual - normed * inner) / scale).astype(jnp.bfloat16)
        images.append(
            lax.dot_general(
                grad_proj, head, (((1,), (1,)), ((), ())), preferred_element_type=jnp.float32
            )
        )
        rendered_all.append(rendered)
        grad_all.append(grad_proj)
    for pair in range(2):
        cols = slice(2 * pair * width, 2 * (pair + 1) * width)
        first, second = images[0][:, cols], images[1][:, cols]
        image_ref[2 * pair] = jnp.where(lane < width, first, pltpu.roll(second, width, 1)).astype(
            image_ref.dtype
        )
        image_ref[2 * pair + 1] = jnp.where(
            lane < width, pltpu.roll(first, width, 1), second
        ).astype(image_ref.dtype)
    grad_ref[...] = lax.dot_general(
        jnp.concatenate(rendered_all, axis=0),
        jnp.concatenate(grad_all, axis=0),
        (((0,), (0,)), ((), ())),
        preferred_element_type=jnp.float32,
    )


def loss(parts, head, teacher):
    vmem = pl.BlockSpec(memory_space=pltpu.VMEM)
    teacher_width = head.shape[1]
    return pl.pallas_call(
        lambda *refs: loss_kernel(teacher_width, *refs),
        out_shape=[
            jax.ShapeDtypeStruct(parts.shape, jnp.bfloat16),
            jax.ShapeDtypeStruct(head.shape, jnp.float32),
        ],
        in_specs=[vmem] * 3,
        out_specs=[vmem] * 2,
        compiler_params=pltpu.CompilerParams(vmem_limit_bytes=VMEM_BYTES),
        name="loss_rows",
    )(parts, head, teacher)


def pull_kernel(
    half_rows, band_rows, view_count, first, last,
    count_ref, block_ref, place_ref, where_ref, weight_ref, image_refs, old_ref, out_ref, image, acc
):
    step_of = pl.program_id(0)
    width = acc.shape[1]
    blocks = out_ref.shape[0]

    @pl.when(step_of == 0)
    def _():
        if first:
            acc[...] = jnp.zeros_like(acc)
        else:
            acc[0:blocks] = old_ref[...]

    for u in range(view_count):
        packed = image_refs[u][0].astype(jnp.float32)
        image[2 * u * half_rows : (2 * u + 1) * half_rows, :] = packed[:, 0:256]
        tail = jnp.concatenate([packed[:, 128:384]], axis=1)
        image[(2 * u + 1) * half_rows : (2 * u + 2) * half_rows, :] = pltpu.roll(tail, 192, 1)

    slots = weight_ref.shape[1]
    base = step_of * slots

    def group(step, carry):
        parts = []
        for t in range(GROUP):
            slot = base + step * GROUP + t
            rows = rows_at(place_ref[slot], band_rows)
            parts.append(
                lax.dot_general(
                    image[rows, 0:width].astype(jnp.bfloat16),
                    shifted(weight_ref[0, where_ref[slot]], place_ref[slot]),
                    (((0,), (0,)), ((), ())),
                    preferred_element_type=jnp.float32,
                )
            )
        for t in range(GROUP):
            slot = base + step * GROUP + t
            acc[block_ref[slot]] += parts[t]
        return carry

    lax.fori_loop(0, (count_ref[step_of] + GROUP - 1) // GROUP, group, 0)

    @pl.when(step_of == pl.num_programs(0) - 1)
    def _():
        out_ref[...] = acc[0:blocks].astype(out_ref.dtype)


def pull(count, block, place, where, weight, images, old, blocks, width, last):
    view_count = len(images)
    peers, slots, band_rows, points = weight.shape
    half_rows = images[0].shape[1]
    first = old is None
    smem = pl.BlockSpec(memory_space=pltpu.SMEM)
    vmem = pl.BlockSpec(memory_space=pltpu.VMEM)

    def body(count_ref, block_ref, place_ref, where_ref, weight_ref, *rest):
        image_refs, rest = rest[:view_count], rest[view_count:]
        if first:
            rest = (None,) + rest
        pull_kernel(
            half_rows, band_rows, view_count, first, last,
            count_ref, block_ref, place_ref, where_ref, weight_ref, image_refs, *rest
        )

    args = [count, block, place, where, weight] + list(images)
    in_specs = [smem] * 4 + [pl.BlockSpec((1, slots, band_rows, points), lambda i: (i, 0, 0, 0))]
    in_specs += [pl.BlockSpec((1,) + images[0].shape[1:], lambda i: (i, 0, 0))] * view_count
    if not first:
        args.append(old)
        in_specs.append(vmem)
    return pl.pallas_call(
        body,
        grid=(peers,),
        out_shape=jax.ShapeDtypeStruct((blocks, width, points), jnp.bfloat16 if last else jnp.float32),
        in_specs=in_specs,
        out_specs=vmem,
        scratch_shapes=[
            pltpu.VMEM((2 * view_count * half_rows + band_rows + 8, 256), jnp.float32),
            pltpu.VMEM((blocks + 1, width, points), jnp.float32),
        ],
        compiler_params=pltpu.CompilerParams(vmem_limit_bytes=VMEM_BYTES),
        name="pull_blocks",
    )(*args)


def total(*terms):
    acc = terms[0].astype(jnp.float32)
    for term in terms[1:]:
        acc = acc + term.astype(jnp.float32)
    return acc.astype(jnp.bfloat16)


def in_order(own_first, other):
    index, mine = own_first
    return jnp.where(
        index == 0, jnp.concatenate([mine, other], 0), jnp.concatenate([other, mine], 0)
    )


def per_device(points, head_weight, teacher, splat_weight, block_owner, block_local, block_row):
    peers, sides = lax.axis_size("view"), lax.axis_size("feat")
    blocks, width = points.shape[0], points.shape[1]
    view_count, visible, band_rows = splat_weight.shape[:3]
    requests = view_count * visible
    capacity = max(3, (3 * requests + 2 * peers - 1) // (2 * peers))
    quarter = -(-capacity // sides)
    slots = quarter * sides
    pixels = teacher.shape[2]
    unit = 2 * sides * 16
    padded = -(-pixels // unit) * unit
    half_rows = padded // 2
    me, side = lax.axis_index("view"), lax.axis_index("feat")
    line, across, core = me // 2, side // 2, side % 2

    def hop(value, axis, pairs):
        return lax.ppermute(value, axis, pairs)

    def swap(value, axis, k):
        size = peers if axis == "view" else sides
        return hop(value, axis, [(i, i ^ k) for i in range(size)])

    def along(value, moves):
        return hop(value, "view", [(2 * a + y, 2 * b + y) for a, b in moves for y in range(2)])

    ints = jnp.int32
    owners = block_owner.reshape(requests)
    positions = jnp.arange(requests, dtype=ints)
    earlier = (owners[:, None] == owners[None, :]) & (positions[None, :] < positions[:, None])
    rank = jnp.sum(earlier.astype(ints), axis=1)
    peer_ids = me ^ jnp.arange(peers, dtype=ints)
    send_ranks = side * quarter + jnp.arange(quarter, dtype=ints)
    match = (owners[None, None, :] == peer_ids[:, None, None]) & (
        rank[None, None, :] == send_ranks[None, :, None]
    )
    source = jnp.sum(jnp.where(match, positions[None, None, :], 0), axis=2)
    aligned = -(-band_rows // 16) * 16
    listed = splat_weight.reshape(requests, band_rows, BLOCK)
    listed = jnp.pad(listed, ((0, 0), (0, aligned - band_rows), (0, 0)))
    packed = jnp.take(listed, source.reshape(peers * quarter), axis=0).reshape(
        peers, quarter, aligned, BLOCK
    )

    view_of = positions // visible
    start = view_of * padded + block_row.reshape(requests) * GRID
    told = jnp.stack([owners, rank, block_local.reshape(requests), start])
    heard = told[None]
    for k in (1, 2, 4):
        heard = jnp.concatenate([heard, swap(heard, "view", k)], axis=0)
    slot_ids = jnp.arange(slots, dtype=ints)
    asked = (heard[:, None, 0, :] == me) & (heard[:, None, 1, :] == slot_ids[None, :, None])
    filled = jnp.any(asked, axis=2)
    counts = jnp.sum(filled.astype(ints), axis=1)
    block_of = jnp.sum(jnp.where(asked, heard[:, None, 2, :], 0), axis=2)
    place_of = jnp.where(
        filled, jnp.sum(jnp.where(asked, heard[:, None, 3, :], 0), axis=2), view_count * padded
    )
    pull_of = jnp.where(filled, block_of, blocks)
    turn = (slot_ids // quarter) ^ side
    turn = (turn % 2) * 2 + turn // 2
    where_of = turn * quarter + slot_ids % quarter

    weights = {}
    for j in (3, 2, 1, 0):
        got = jnp.stack([swap(packed[k], "view", k) if k else packed[k] for k in (2 * j, 2 * j + 1)])
        got = jnp.concatenate([got, swap(got, "feat", 2)], axis=1)
        weights[j] = jnp.concatenate([got, swap(got, "feat", 1)], axis=1)

    head = jnp.concatenate([head_weight, swap(head_weight, "feat", 2)], axis=0)
    head = jnp.concatenate([head, swap(head, "feat", 1)], axis=0)
    seventh = half_rows // sides
    target = jnp.pad(teacher, ((0, 0), (0, 0), (0, padded - pixels)))
    target = target.reshape(width, view_count, 2, sides, seventh).transpose(3, 1, 2, 4, 0)
    order = side ^ jnp.arange(sides, dtype=ints)
    target = jnp.take(target, order, axis=0)
    target = [swap(target[d], "feat", d) if d else target[d] for d in range(sides)]
    target = jnp.take(jnp.stack(target), order, axis=0)
    target = target.transpose(1, 2, 3, 0, 4).reshape(view_count, 2, seventh, sides * width)

    kept, sent = {}, {}
    for j in (3, 2, 1, 0):
        for k, into in ((2 * j + 1, sent), (2 * j, kept)):
            into[j] = render(
                counts[k : k + 1], block_of[k], place_of[k], where_of, weights[j][k - 2 * j], points,
                view_count, half_rows,
            )
    rendered = []
    for u in range(view_count):
        pair = {j: (kept[j][u], swap(sent[j][u], "view", 1)) for j in (3, 2, 1, 0)}
        far = along(total(*pair[3]), [(0, 1), (3, 2)])
        mid = total(*pair[2], far)
        inward = along(mid, [(0, 1), (3, 2)])
        between = along(mid, [(1, 2), (2, 1)])
        near = along(total(*pair[1], between), [(0, 1), (1, 0), (2, 3), (3, 2)])
        centre = along(total(*pair[3], inward), [(1, 2), (2, 1)])
        rendered.append(total(*pair[0], near, centre))

    grads, images = [], []
    side_rows = half_rows // 2
    for u in range(view_count):
        whole = rendered[u]
        mine = lax.dynamic_slice_in_dim(whole, across * side_rows, side_rows, 0)
        other = lax.dynamic_slice_in_dim(whole, (1 - across) * side_rows, side_rows, 0)
        both = jnp.stack([mine, swap(other, "feat", 2)])
        mine = lax.dynamic_slice_in_dim(both, core * seventh, seventh, 1)
        other = lax.dynamic_slice_in_dim(both, (1 - core) * seventh, seventh, 1)
        parts = jnp.concatenate([mine, swap(other, "feat", 1)], axis=0)
        image, grad = loss(parts, head, target[u])
        grads.append(grad)
        back = swap(image[2:4], "feat", 1)
        rows = [in_order((core, image[i]), back[i]) for i in range(2)]
        images.append(in_order((across, rows[0]), swap(rows[1], "feat", 2)))

    grad = grads[0]
    for more in grads[1:]:
        grad = grad + more
    grad = grad.reshape(2, 2, width, grad.shape[1])
    grad = grad[0] + swap(grad[1], "feat", 1)
    grad = grad[0] + swap(grad[1], "feat", 2)
    bits = [(1, me % 2), (4, me // 4), (2, line % 2)]
    for k, bit in bits:
        rows = grad.shape[0] // 2
        mine = lax.dynamic_slice_in_dim(grad, bit * rows, rows, 0)
        other = lax.dynamic_slice_in_dim(grad, (1 - bit) * rows, rows, 0)
        grad = mine + swap(other, "view", k)
    grad = grad / (view_count * peers * GRID)
    for k, bit in bits[::-1]:
        grad = in_order((bit, grad), swap(grad, "view", k))
    head_grad = grad

    middle = (line == 1) | (line == 2)
    chunks = {j: [] for j in range(4)}
    for u in range(view_count):
        own = images[u]
        near = along(own, [(0, 1), (1, 0), (2, 3), (3, 2)])
        centre = along(own, [(1, 2), (2, 1)])
        out_near = along(centre, [(1, 0), (2, 3)])
        cross = along(near, [(1, 2), (2, 1)])
        out_far = along(cross, [(1, 0), (2, 3)])
        for j, value in enumerate(
            (own, near, jnp.where(middle, cross, out_near), jnp.where(middle, centre, out_far))
        ):
            chunks[j].append(jnp.stack([value, swap(value, "view", 1)]))
    acc = None
    for j in range(4):
        ks = slice(2 * j, 2 * j + 2)
        acc = pull(
            counts[ks], pull_of[ks].reshape(-1), place_of[ks].reshape(-1), jnp.tile(where_of, 2),
            weights[j], chunks[j], acc, blocks, width, j == 3,
        )
    return (acc, head_grad)


def solution(mesh):
    size = mesh.shape
    paired = size["view"] == 8 and size["feat"] == 4
    placed = (
        P("view", "feat", None),
        P("feat", None),
        P("feat", "view", None),
        P("view", None, None, None),
        P("view", None, None),
        P("view", None),
        P("view", None),
    )
    return jax.shard_map(
        per_device if paired else per_device_listed,
        mesh=mesh,
        in_specs=placed,
        out_specs=(P("view", "feat", None), P("feat", None)),
        check_vma=False,
    )
```

```python
import jax
import jax.numpy as jnp
from jax import lax
from jax.experimental import pallas as pl
from jax.experimental.pallas import tpu as pltpu
from jax.sharding import PartitionSpec as P

GRID = 37
BAND = 2
BLOCK = 128
GROUP = 4
VMEM_BYTES = 48 * 1024 * 1024


def slot_plan(owners, peer_count, capacity):
    total_requests = owners.shape[0]
    positions = jnp.arange(total_requests, dtype=jnp.int32)
    earlier = (owners[:, None] == owners[None, :]) & (positions[None, :] < positions[:, None])
    slot_rank = jnp.sum(earlier.astype(jnp.int32), axis=1)
    target = owners * capacity + slot_rank
    slot_ids = jnp.arange(peer_count * capacity, dtype=jnp.int32)
    matches = target[None, :] == slot_ids[:, None]
    source = jnp.sum(jnp.where(matches, positions[None, :], 0), axis=1)
    filled = jnp.any(matches, axis=1)
    return (target, source, filled)


def per_device_listed(points, head_weight, teacher, splat_weight, block_owner, block_local, block_row):
    peer_count = lax.axis_size("view")
    local_width = points.shape[1]
    view_count = splat_weight.shape[0]
    visible = splat_weight.shape[1]
    requests = view_count * visible
    capacity = max(3, (3 * requests + 2 * peer_count - 1) // (2 * peer_count))
    owners = block_owner.reshape(requests)
    local_ids = block_local.reshape(requests)
    target, source, filled = slot_plan(owners, peer_count, capacity)
    wanted = jnp.where(filled, jnp.take(local_ids, source), 0)
    columns = jnp.arange(GRID, dtype=jnp.int32)
    row_masks = [
        (block_row[:, :, None] + offset == columns[None, None, :]).astype(jnp.bfloat16)
        for offset in range(BAND)
    ]
    empty_bf = jnp.zeros((), jnp.bfloat16)
    asked_ids = lax.all_to_all(wanted, "view", split_axis=0, concat_axis=0, tiled=True)
    sent_rows = jnp.take(points, asked_ids, axis=0)
    arrived = lax.all_to_all(sent_rows, "view", split_axis=0, concat_axis=0, tiled=True)
    fetched = jnp.take(arrived, target, axis=0).reshape(view_count, visible, local_width, BLOCK)
    contrib = jnp.einsum(
        "vjcp,vjdp->vjcd", splat_weight, fetched, preferred_element_type=jnp.float32
    ).astype(jnp.bfloat16)
    rendered = jnp.zeros((view_count, GRID, GRID, local_width), jnp.float32)
    for offset in range(BAND):
        band_part = contrib[:, :, offset * GRID : (offset + 1) * GRID, :]
        rendered = rendered + jnp.einsum(
            "vjr,vjcd->vrcd", row_masks[offset], band_part, preferred_element_type=jnp.float32
        )
    rendered_rows = rendered.astype(jnp.bfloat16).reshape(view_count * GRID * GRID, local_width)
    pixel_rows = rendered_rows.shape[0]
    teacher_width = head_weight.shape[1]
    local_teacher = teacher.shape[0]
    contract_first = (((0,), (1,)), ((), ()))
    head_full = lax.all_gather(head_weight, "feat", axis=0, tiled=True)
    head_cols = lax.dynamic_slice_in_dim(
        head_full, lax.axis_index("feat") * local_teacher, local_teacher, 1
    )
    head_part = head_cols
    projected = lax.dot_general(
        head_part,
        lax.all_gather(rendered_rows, "feat", axis=1, tiled=True),
        contract_first,
        preferred_element_type=jnp.float32,
    )
    square_sum = lax.psum(jnp.sum(projected * projected, axis=0), "feat")
    scale_rows = jnp.sqrt(square_sum / teacher_width + 1e-06)
    normed = projected / scale_rows[None, :]
    target_feat = teacher.reshape(local_teacher, pixel_rows).astype(jnp.float32)
    residual = normed - target_feat
    row_dot = lax.psum(jnp.sum(residual * normed, axis=0), "feat")
    grad_proj = (
        (residual - normed * (row_dot / teacher_width)[None, :]) / scale_rows[None, :]
    ).astype(jnp.bfloat16)
    shard_part = lax.all_gather(grad_proj, "feat", axis=0, tiled=True)
    head_part = head_weight
    grad_image = lax.dot_general(
        shard_part, head_part, contract_first, preferred_element_type=jnp.float32
    )
    column_part = lax.dot_general(
        rendered_rows, shard_part, contract_first, preferred_element_type=jnp.float32
    )
    grad_head = column_part
    grad_image, grad_head = (grad_image, grad_head)
    head_grad = lax.psum(grad_head, "view") / (view_count * peer_count * GRID)
    grad_image = grad_image.astype(jnp.bfloat16).reshape(view_count, GRID, GRID, local_width)
    pieces = [
        jnp.einsum("vjr,vrcd->vjcd", row_mask, grad_image, preferred_element_type=jnp.float32)
        for row_mask in row_masks
    ]
    grad_contrib = jnp.concatenate(pieces, axis=2).astype(jnp.bfloat16)
    grad_block = jnp.einsum(
        "vjcp,vjcd->vjdp", splat_weight, grad_contrib, preferred_element_type=jnp.float32
    ).astype(jnp.bfloat16)
    grad_block = grad_block.reshape(requests, local_width, BLOCK)
    packed = jnp.where(filled[:, None, None], jnp.take(grad_block, source, axis=0), empty_bf)
    landed = lax.all_to_all(packed, "view", split_axis=0, concat_axis=0, tiled=True)
    summed = jax.ops.segment_sum(
        landed.astype(jnp.float32), asked_ids, num_segments=points.shape[0]
    )
    grad_points = summed.astype(jnp.bfloat16)
    return (grad_points, head_grad)


def price(us):
    return pl.CostEstimate(flops=int(us * 1e9), bytes_accessed=int(us * 2e6), transcendentals=0)


def call(body, out_shape, args, n_scalars, us, name, scratch=(), aliases=None):
    smem = pl.BlockSpec(memory_space=pltpu.SMEM)
    vmem = pl.BlockSpec(memory_space=pltpu.VMEM)
    many = isinstance(out_shape, list)
    return pl.pallas_call(
        body,
        out_shape=out_shape,
        in_specs=[smem] * n_scalars + [vmem] * (len(args) - n_scalars),
        out_specs=[vmem] * len(out_shape) if many else vmem,
        scratch_shapes=list(scratch),
        compiler_params=pltpu.CompilerParams(vmem_limit_bytes=VMEM_BYTES),
        cost_estimate=price(us),
        name=name,
    )(*args)


def pack_weights(source, listed, peers, aligned):
    quarter = source.shape[0] // peers
    band_rows = listed.shape[1]
    tail = aligned - 16

    def body(source_ref, listed_ref, *outs):
        for k in range(peers):
            for i in range(quarter):
                outs[k][i, tail:aligned, :] = jnp.zeros((16, BLOCK), jnp.bfloat16)
                outs[k][i, 0:band_rows, :] = listed_ref[source_ref[k * quarter + i]]

    out = jax.ShapeDtypeStruct((quarter, aligned, BLOCK), jnp.bfloat16)
    return call(body, [out] * peers, (source, listed), 1, 3, "pack_weights")


def shifted(rows, start):
    rows = rows.astype(jnp.float32)
    rows = jnp.concatenate([rows, jnp.zeros((8, rows.shape[1]), jnp.float32)], axis=0)
    return pltpu.roll(rows, lax.rem(start, 8), 0)


def rows_at(start, band_rows):
    return pl.ds(pl.multiple_of((start // 8) * 8, 8), band_rows + 8)


def beside(first, second):
    lane = lax.broadcasted_iota(jnp.int32, (first.shape[0], 128), 1)
    second = pltpu.roll(second, 64, 1)
    middle = jnp.where(lane < 64, first[:, 128:256], second[:, 0:128])
    return jnp.concatenate([first[:, 0:128], middle, second[:, 128:256]], axis=1)


def apart(packed):
    return packed[:, 0:256], pltpu.roll(packed[:, 128:384], 192, 1)


def rounds(count, group):
    return (count + group - 1) // group


def spread(count, block, where, weight, points):
    slots, band_rows = weight.shape[:2]
    width = points.shape[1]

    def body(count_ref, block_ref, where_ref, weight_ref, points_ref, out_ref):
        blank = jnp.zeros((width, BLOCK), jnp.bfloat16)

        def group(step, carry):
            for t in range(2):
                pair = 2 * step + t
                one, two = 2 * pair, 2 * pair + 1
                weights = jnp.concatenate(
                    [weight_ref[where_ref[one]], weight_ref[where_ref[two]]], axis=1
                )
                blocks = jnp.concatenate(
                    [
                        jnp.concatenate([points_ref[block_ref[one]], blank], axis=1),
                        jnp.concatenate([blank, points_ref[block_ref[two]]], axis=1),
                    ],
                    axis=0,
                )
                out_ref[pair] = lax.dot_general(
                    weights, blocks, (((1,), (1,)), ((), ())), preferred_element_type=jnp.float32
                ).astype(jnp.bfloat16)
            return carry

        lax.fori_loop(0, rounds(count_ref[0], 4), group, 0)

    out = jax.ShapeDtypeStruct((slots // 2, band_rows, 2 * width), jnp.bfloat16)
    return call(body, out, (count, block, where, weight, points), 3, 3, "spread_blocks")


def render(count, block, place, where, other_count, other_place, weight, points, other, views, half_rows):
    width = points.shape[1]
    band_rows = weight.shape[1]

    def body(
        count_ref, block_ref, place_ref, where_ref, other_count_ref, other_place_ref,
        weight_ref, points_ref, other_ref, *rest
    ):
        outs, acc = rest[:-1], rest[-1]
        acc[...] = jnp.zeros_like(acc)

        def group(step, carry):
            parts = []
            for t in range(GROUP):
                slot = step * GROUP + t
                parts.append(
                    lax.dot_general(
                        shifted(weight_ref[where_ref[slot]], place_ref[slot]).astype(jnp.bfloat16),
                        points_ref[block_ref[slot]],
                        (((1,), (1,)), ((), ())),
                        preferred_element_type=jnp.float32,
                    )
                )
            for t in range(GROUP):
                acc[rows_at(place_ref[step * GROUP + t], band_rows), 0:width] += parts[t]
            return carry

        def other_group(step, carry):
            for t in range(2):
                pair = 2 * step + t
                for value, slot in zip(apart(other_ref[pair].astype(jnp.float32)), (2 * pair, 2 * pair + 1)):
                    start = other_place_ref[slot]
                    acc[rows_at(start, band_rows), :] += shifted(value, start)
            return carry

        lax.fori_loop(0, rounds(count_ref[0], GROUP), group, 0)
        lax.fori_loop(0, rounds(other_count_ref[0], 4), other_group, 0)
        for u, out in enumerate(outs):
            first = acc[2 * u * half_rows : (2 * u + 1) * half_rows, :]
            second = acc[(2 * u + 1) * half_rows : (2 * u + 2) * half_rows, :]
            out[...] = beside(first, second).astype(out.dtype)

    image = jax.ShapeDtypeStruct((half_rows, 2 * width), jnp.bfloat16)
    args = (count, block, place, where, other_count, other_place, weight, points, other)
    scratch = [pltpu.VMEM((2 * views * half_rows + band_rows + 8, 256), jnp.float32)]
    return call(body, [image] * views, args, 6, 5, "render_blocks", scratch)


def unpack_images(image_refs, image, half_rows):
    for u, ref in enumerate(image_refs):
        first, second = apart(ref[...].astype(jnp.float32))
        image[2 * u * half_rows : (2 * u + 1) * half_rows, :] = first
        image[(2 * u + 1) * half_rows : (2 * u + 2) * half_rows, :] = second


def pick(count, place, images, slots, band_rows):
    half_rows, packed = images[0].shape
    views = len(images)

    def body(count_ref, place_ref, *rest):
        image_refs, (out_ref, image) = rest[:views], rest[views:]
        unpack_images(image_refs, image, half_rows)
        image[2 * views * half_rows :, :] = jnp.zeros((band_rows + 8, 256), jnp.float32)

        def group(step, carry):
            for t in range(2):
                pair = 2 * step + t
                bands = []
                for slot in (2 * pair, 2 * pair + 1):
                    start = place_ref[slot]
                    rows = image[rows_at(start, band_rows), :]
                    back = lax.rem(band_rows + 8 - lax.rem(start, 8), band_rows + 8)
                    bands.append(pltpu.roll(rows, back, 0)[0:band_rows])
                out_ref[pair] = beside(*bands).astype(out_ref.dtype)
            return carry

        lax.fori_loop(0, rounds(count_ref[0], 4), group, 0)

    out = jax.ShapeDtypeStruct((slots // 2, band_rows, packed), jnp.bfloat16)
    scratch = [pltpu.VMEM((2 * views * half_rows + band_rows + 8, 256), jnp.float32)]
    return call(body, out, (count, place) + tuple(images), 2, 4, "pick_bands", scratch)


def pull(
    count, block, place, where, other_count, other_block, weights, images, other, old, blocks, last
):
    views = len(images)
    half_rows, packed = images[0].shape
    width = packed // 2
    band_rows = weights.shape[2]
    first = old is None

    def body(
        count_ref, block_ref, place_ref, where_ref, other_count_ref, other_block_ref, weight_ref, *rest
    ):
        image_refs, rest = rest[:views], rest[views:]
        other_ref, rest = rest[0], rest[1:]
        old_ref, rest = (None, rest) if first else (rest[0], rest[1:])
        out_ref, image, acc = rest
        if first:
            acc[...] = jnp.zeros_like(acc)
        else:
            acc[0:blocks] = old_ref[...]
        unpack_images(image_refs, image, half_rows)

        def group(step, carry):
            parts = []
            for t in range(GROUP):
                slot = step * GROUP + t
                start = place_ref[slot]
                parts.append(
                    lax.dot_general(
                        image[rows_at(start, band_rows), 0:width].astype(jnp.bfloat16),
                        shifted(weight_ref[0, where_ref[slot]], start).astype(jnp.bfloat16),
                        (((0,), (0,)), ((), ())),
                        preferred_element_type=jnp.float32,
                    )
                )
            for t in range(GROUP):
                acc[block_ref[step * GROUP + t]] += parts[t]
            return carry

        def other_group(step, carry):
            parts = []
            for t in range(2):
                pair = 2 * step + t
                both = jnp.concatenate(
                    [weight_ref[1, where_ref[2 * pair]], weight_ref[1, where_ref[2 * pair + 1]]], axis=1
                )
                parts.append(
                    lax.dot_general(
                        other_ref[pair], both, (((0,), (0,)), ((), ())), preferred_element_type=jnp.float32
                    )
                )
            for t in range(2):
                pair = 2 * step + t
                acc[other_block_ref[2 * pair]] += parts[t][0:width, 0:BLOCK]
                acc[other_block_ref[2 * pair + 1]] += parts[t][width:, BLOCK:]
            return carry

        lax.fori_loop(0, rounds(count_ref[0], GROUP), group, 0)
        lax.fori_loop(0, rounds(other_count_ref[0], 4), other_group, 0)
        out_ref[...] = acc[0:blocks].astype(out_ref.dtype)

    args = (count, block, place, where, other_count, other_block, weights) + tuple(images) + (other,)
    args += () if first else (old,)
    out = jax.ShapeDtypeStruct((blocks, width, BLOCK), jnp.bfloat16 if last else jnp.float32)
    scratch = [
        pltpu.VMEM((2 * views * half_rows + band_rows + 8, 256), jnp.float32),
        pltpu.VMEM((blocks + 1, width, BLOCK), jnp.float32),
    ]
    return call(body, out, args, 6, 8, "pull_blocks", scratch)


def loss_kernel(teacher_width, parts_ref, head_ref, teacher_ref, image_ref, grad_ref):
    rows, packed = parts_ref.shape[1], parts_ref.shape[2]
    width = packed // 2
    lane = lax.broadcasted_iota(jnp.int32, (rows, packed), 1)
    head = head_ref[...]
    halves = [[], []]
    for pair in range(2):
        one = parts_ref[2 * pair].astype(jnp.float32)
        two = parts_ref[2 * pair + 1].astype(jnp.float32)
        halves[0].append(jnp.where(lane < width, one, pltpu.roll(two, width, 1)))
        halves[1].append(jnp.where(lane < width, pltpu.roll(one, width, 1), two))
    rendered_all, grad_all, images = [], [], []
    for half in range(2):
        rendered = jnp.concatenate(halves[half], axis=1).astype(jnp.bfloat16)
        projected = jnp.dot(rendered, head, preferred_element_type=jnp.float32)
        square = jnp.sum(projected * projected, axis=1, keepdims=True)
        scale = jnp.sqrt(square / teacher_width + 1e-06)
        normed = projected / scale
        residual = normed - teacher_ref[half].astype(jnp.float32)
        inner = jnp.sum(residual * normed, axis=1, keepdims=True) / teacher_width
        grad_proj = ((residual - normed * inner) / scale).astype(jnp.bfloat16)
        images.append(
            lax.dot_general(
                grad_proj, head, (((1,), (1,)), ((), ())), preferred_element_type=jnp.float32
            )
        )
        rendered_all.append(rendered)
        grad_all.append(grad_proj)
    for pair in range(2):
        cols = slice(2 * pair * width, 2 * (pair + 1) * width)
        first, second = images[0][:, cols], images[1][:, cols]
        image_ref[2 * pair] = jnp.where(lane < width, first, pltpu.roll(second, width, 1)).astype(
            image_ref.dtype
        )
        image_ref[2 * pair + 1] = jnp.where(
            lane < width, pltpu.roll(first, width, 1), second
        ).astype(image_ref.dtype)
    grad_ref[...] = lax.dot_general(
        jnp.concatenate(rendered_all, axis=0),
        jnp.concatenate(grad_all, axis=0),
        (((0,), (0,)), ((), ())),
        preferred_element_type=jnp.float32,
    )


def loss(parts, head, teacher):
    teacher_width = head.shape[1]
    outs = [
        jax.ShapeDtypeStruct(parts.shape, jnp.bfloat16),
        jax.ShapeDtypeStruct(head.shape, jnp.float32),
    ]
    body = lambda *refs: loss_kernel(teacher_width, *refs)
    return call(body, outs, (parts, head, teacher), 0, 3, "loss_rows")


def after(value, *earlier):
    return lax.optimization_barrier((value,) + earlier)[0]


def total(*terms):
    acc = terms[0].astype(jnp.float32)
    for term in terms[1:]:
        acc = acc + term.astype(jnp.float32)
    return acc.astype(jnp.bfloat16)


def in_order(own_first, other):
    index, mine = own_first
    return jnp.where(
        index == 0, jnp.concatenate([mine, other], 0), jnp.concatenate([other, mine], 0)
    )


def per_device(points, head_weight, teacher, splat_weight, block_owner, block_local, block_row):
    peers, sides = lax.axis_size("view"), lax.axis_size("feat")
    blocks, width = points.shape[0], points.shape[1]
    view_count, visible, band_rows = splat_weight.shape[:3]
    requests = view_count * visible
    capacity = max(3, (3 * requests + 2 * peers - 1) // (2 * peers))
    quarter = -(-capacity // sides)
    slots = quarter * sides
    pixels = teacher.shape[2]
    unit = 2 * sides * 16
    padded = -(-pixels // unit) * unit
    half_rows = padded // 2
    me, side = lax.axis_index("view"), lax.axis_index("feat")
    line, across, core = me // 2, side // 2, side % 2

    def hop(value, axis, pairs):
        return lax.ppermute(value, axis, pairs)

    def swap(value, axis, k):
        size = peers if axis == "view" else sides
        return hop(value, axis, [(i, i ^ k) for i in range(size)])

    def along(value, moves):
        return hop(value, "view", [(2 * a + y, 2 * b + y) for a, b in moves for y in range(2)])

    ints = jnp.int32
    owners = block_owner.reshape(requests)
    positions = jnp.arange(requests, dtype=ints)
    earlier = (owners[:, None] == owners[None, :]) & (positions[None, :] < positions[:, None])
    rank = jnp.sum(earlier.astype(ints), axis=1)
    peer_ids = me ^ jnp.arange(peers, dtype=ints)
    send_ranks = side * quarter + jnp.arange(quarter, dtype=ints)
    match = (owners[None, None, :] == peer_ids[:, None, None]) & (
        rank[None, None, :] == send_ranks[None, :, None]
    )
    source = jnp.sum(jnp.where(match, positions[None, None, :], 0), axis=2)
    aligned = -(-band_rows // 16) * 16
    listed = splat_weight.reshape(requests, band_rows, BLOCK)
    packed = pack_weights(source.reshape(peers * quarter), listed, peers, aligned)

    view_of = positions // visible
    start = view_of * padded + block_row.reshape(requests) * GRID
    told = jnp.stack([owners, rank, block_local.reshape(requests), start])
    heard = told[None]
    for k in (1, 2, 4):
        heard = jnp.concatenate([heard, swap(heard, "view", k)], axis=0)
    slot_ids = jnp.arange(slots, dtype=ints)

    def asked_of(owner, told):
        asked = (told[:, None, 0, :] == owner) & (told[:, None, 1, :] == slot_ids[None, :, None])
        filled = jnp.any(asked, axis=2)
        block = jnp.sum(jnp.where(asked, told[:, None, 2, :], 0), axis=2)
        place = jnp.sum(jnp.where(asked, told[:, None, 3, :], 0), axis=2)
        place = jnp.where(filled, place, view_count * padded)
        return jnp.sum(filled.astype(ints), axis=1), block, jnp.where(filled, block, blocks), place

    counts, block_of, pull_of, place_of = asked_of(me, heard)
    pair_counts, _, _, pair_places = asked_of(me ^ 1, heard[::2])
    turn = (slot_ids // quarter) ^ side
    turn = (turn % 2) * 2 + turn // 2
    where_of = turn * quarter + slot_ids % quarter

    weights = {}
    for j in (3, 2, 1, 0):
        got = jnp.stack([swap(packed[k], "view", k) if k else packed[k] for k in (2 * j, 2 * j + 1)])
        got = jnp.concatenate([got, swap(got, "feat", 2)], axis=1)
        weights[j] = jnp.concatenate([got, swap(got, "feat", 1)], axis=1)

    head_weight, teacher = after((head_weight, teacher), weights[1])
    head = jnp.concatenate([head_weight, swap(head_weight, "feat", 2)], axis=0)
    head = jnp.concatenate([head, swap(head, "feat", 1)], axis=0)
    seventh = half_rows // sides
    target = jnp.pad(teacher, ((0, 0), (0, 0), (0, padded - pixels)))
    target = target.reshape(width, view_count, 2, sides, seventh).transpose(3, 1, 2, 4, 0)
    order = side ^ jnp.arange(sides, dtype=ints)
    target = jnp.take(target, order, axis=0)
    target = [swap(target[d], "feat", d) if d else target[d] for d in range(sides)]
    target = jnp.take(jnp.stack(target), order, axis=0)
    target = target.transpose(1, 2, 3, 0, 4).reshape(view_count, 2, seventh, sides * width)

    kept = {}
    for j in (3, 2, 1, 0):
        k = 2 * j + 1
        given = spread(counts[k : k + 1], block_of[k], where_of, weights[j][1], points)
        k = 2 * j
        kept[j] = render(
            counts[k : k + 1], block_of[k], place_of[k], where_of,
            pair_counts[j : j + 1], pair_places[j], weights[j][0], points, swap(given, "view", 1),
            view_count, half_rows,
        )
    rendered = []
    for u in range(view_count):
        far = along(kept[3][u], [(0, 1), (3, 2)])
        mid = total(kept[2][u], far)
        inward = along(mid, [(0, 1), (3, 2)])
        between = along(mid, [(1, 2), (2, 1)])
        near = along(total(kept[1][u], between), [(0, 1), (1, 0), (2, 3), (3, 2)])
        centre = along(total(kept[3][u], inward), [(1, 2), (2, 1)])
        rendered.append(total(kept[0][u], near, centre))

    grads, images = [], []
    side_rows = half_rows // 2
    for u in range(view_count):
        whole = rendered[u]
        mine = lax.dynamic_slice_in_dim(whole, across * side_rows, side_rows, 0)
        other = lax.dynamic_slice_in_dim(whole, (1 - across) * side_rows, side_rows, 0)
        both = jnp.stack([mine, swap(other, "feat", 2)])
        mine = lax.dynamic_slice_in_dim(both, core * seventh, seventh, 1)
        other = lax.dynamic_slice_in_dim(both, (1 - core) * seventh, seventh, 1)
        parts = jnp.concatenate([mine, swap(other, "feat", 1)], axis=0)
        image, grad = loss(parts, head, target[u])
        grads.append(grad)
        back = swap(image[2:4], "feat", 1)
        rows = [in_order((core, image[i]), back[i]) for i in range(2)]
        images.append(in_order((across, rows[0]), swap(rows[1], "feat", 2)))

    grad = grads[0]
    for more in grads[1:]:
        grad = grad + more
    grad = grad.reshape(2, 2, width, grad.shape[1])
    grad = grad[0] + swap(grad[1], "feat", 1)
    grad = grad[0] + swap(grad[1], "feat", 2)
    bits = [(1, me % 2), (4, me // 4), (2, line % 2)]
    for k, bit in bits:
        rows = grad.shape[0] // 2
        mine = lax.dynamic_slice_in_dim(grad, bit * rows, rows, 0)
        other = lax.dynamic_slice_in_dim(grad, (1 - bit) * rows, rows, 0)
        grad = mine + swap(other, "view", k)
    grad = grad / (view_count * peers * GRID)
    for k, bit in bits[::-1]:
        grad = in_order((bit, grad), swap(grad, "view", k))
    head_grad = grad

    middle = (line == 1) | (line == 2)
    chunks = {j: [] for j in range(4)}
    for u in range(view_count):
        own = images[u]
        near = along(own, [(0, 1), (1, 0), (2, 3), (3, 2)])
        centre = along(own, [(1, 2), (2, 1)])
        out_near = along(centre, [(1, 0), (2, 3)])
        cross = along(near, [(1, 2), (2, 1)])
        out_far = along(cross, [(1, 0), (2, 3)])
        for j, value in enumerate(
            (own, near, jnp.where(middle, cross, out_near), jnp.where(middle, centre, out_far))
        ):
            chunks[j].append(value)
    acc = None
    for j in range(4):
        own, other = 2 * j, 2 * j + 1
        bands = pick(pair_counts[j : j + 1], pair_places[j], chunks[j], slots, aligned)
        acc = pull(
            counts[own : own + 1], pull_of[own], place_of[own], where_of, counts[other : other + 1],
            pull_of[other], weights[j], chunks[j], swap(bands, "view", 1), acc, blocks, j == 3,
        )
    return (acc, head_grad)


def solution(mesh):
    size = mesh.shape
    paired = size["view"] == 8 and size["feat"] == 4
    placed = (
        P("view", "feat", None),
        P("feat", None),
        P("feat", "view", None),
        P("view", None, None, None),
        P("view", None, None),
        P("view", None),
        P("view", None),
    )
    return jax.shard_map(
        per_device if paired else per_device_listed,
        mesh=mesh,
        in_specs=placed,
        out_specs=(P("view", "feat", None), P("feat", None)),
        check_vma=False,
    )
```

```python
import jax
import jax.numpy as jnp
from jax import lax
from jax.experimental import pallas as pl
from jax.experimental.pallas import tpu as pltpu
from jax.sharding import PartitionSpec as P

GRID = 37
BAND = 2
BLOCK = 128
GROUP = 4
VMEM_BYTES = 48 * 1024 * 1024


def slot_plan(owners, peer_count, capacity):
    total_requests = owners.shape[0]
    positions = jnp.arange(total_requests, dtype=jnp.int32)
    earlier = (owners[:, None] == owners[None, :]) & (positions[None, :] < positions[:, None])
    slot_rank = jnp.sum(earlier.astype(jnp.int32), axis=1)
    target = owners * capacity + slot_rank
    slot_ids = jnp.arange(peer_count * capacity, dtype=jnp.int32)
    matches = target[None, :] == slot_ids[:, None]
    source = jnp.sum(jnp.where(matches, positions[None, :], 0), axis=1)
    filled = jnp.any(matches, axis=1)
    return (target, source, filled)


def per_device_listed(points, head_weight, teacher, splat_weight, block_owner, block_local, block_row):
    peer_count = lax.axis_size("view")
    local_width = points.shape[1]
    view_count = splat_weight.shape[0]
    visible = splat_weight.shape[1]
    requests = view_count * visible
    capacity = max(3, (3 * requests + 2 * peer_count - 1) // (2 * peer_count))
    owners = block_owner.reshape(requests)
    local_ids = block_local.reshape(requests)
    target, source, filled = slot_plan(owners, peer_count, capacity)
    wanted = jnp.where(filled, jnp.take(local_ids, source), 0)
    columns = jnp.arange(GRID, dtype=jnp.int32)
    row_masks = [
        (block_row[:, :, None] + offset == columns[None, None, :]).astype(jnp.bfloat16)
        for offset in range(BAND)
    ]
    empty_bf = jnp.zeros((), jnp.bfloat16)
    asked_ids = lax.all_to_all(wanted, "view", split_axis=0, concat_axis=0, tiled=True)
    sent_rows = jnp.take(points, asked_ids, axis=0)
    arrived = lax.all_to_all(sent_rows, "view", split_axis=0, concat_axis=0, tiled=True)
    fetched = jnp.take(arrived, target, axis=0).reshape(view_count, visible, local_width, BLOCK)
    contrib = jnp.einsum(
        "vjcp,vjdp->vjcd", splat_weight, fetched, preferred_element_type=jnp.float32
    ).astype(jnp.bfloat16)
    rendered = jnp.zeros((view_count, GRID, GRID, local_width), jnp.float32)
    for offset in range(BAND):
        band_part = contrib[:, :, offset * GRID : (offset + 1) * GRID, :]
        rendered = rendered + jnp.einsum(
            "vjr,vjcd->vrcd", row_masks[offset], band_part, preferred_element_type=jnp.float32
        )
    rendered_rows = rendered.astype(jnp.bfloat16).reshape(view_count * GRID * GRID, local_width)
    pixel_rows = rendered_rows.shape[0]
    teacher_width = head_weight.shape[1]
    local_teacher = teacher.shape[0]
    contract_first = (((0,), (1,)), ((), ()))
    head_full = lax.all_gather(head_weight, "feat", axis=0, tiled=True)
    head_cols = lax.dynamic_slice_in_dim(
        head_full, lax.axis_index("feat") * local_teacher, local_teacher, 1
    )
    head_part = head_cols
    projected = lax.dot_general(
        head_part,
        lax.all_gather(rendered_rows, "feat", axis=1, tiled=True),
        contract_first,
        preferred_element_type=jnp.float32,
    )
    square_sum = lax.psum(jnp.sum(projected * projected, axis=0), "feat")
    scale_rows = jnp.sqrt(square_sum / teacher_width + 1e-06)
    normed = projected / scale_rows[None, :]
    target_feat = teacher.reshape(local_teacher, pixel_rows).astype(jnp.float32)
    residual = normed - target_feat
    row_dot = lax.psum(jnp.sum(residual * normed, axis=0), "feat")
    grad_proj = (
        (residual - normed * (row_dot / teacher_width)[None, :]) / scale_rows[None, :]
    ).astype(jnp.bfloat16)
    shard_part = lax.all_gather(grad_proj, "feat", axis=0, tiled=True)
    head_part = head_weight
    grad_image = lax.dot_general(
        shard_part, head_part, contract_first, preferred_element_type=jnp.float32
    )
    column_part = lax.dot_general(
        rendered_rows, shard_part, contract_first, preferred_element_type=jnp.float32
    )
    grad_head = column_part
    grad_image, grad_head = (grad_image, grad_head)
    head_grad = lax.psum(grad_head, "view") / (view_count * peer_count * GRID)
    grad_image = grad_image.astype(jnp.bfloat16).reshape(view_count, GRID, GRID, local_width)
    pieces = [
        jnp.einsum("vjr,vrcd->vjcd", row_mask, grad_image, preferred_element_type=jnp.float32)
        for row_mask in row_masks
    ]
    grad_contrib = jnp.concatenate(pieces, axis=2).astype(jnp.bfloat16)
    grad_block = jnp.einsum(
        "vjcp,vjcd->vjdp", splat_weight, grad_contrib, preferred_element_type=jnp.float32
    ).astype(jnp.bfloat16)
    grad_block = grad_block.reshape(requests, local_width, BLOCK)
    packed = jnp.where(filled[:, None, None], jnp.take(grad_block, source, axis=0), empty_bf)
    landed = lax.all_to_all(packed, "view", split_axis=0, concat_axis=0, tiled=True)
    summed = jax.ops.segment_sum(
        landed.astype(jnp.float32), asked_ids, num_segments=points.shape[0]
    )
    grad_points = summed.astype(jnp.bfloat16)
    return (grad_points, head_grad)


def price(us):
    return pl.CostEstimate(flops=int(us * 1e9), bytes_accessed=int(us * 2e6), transcendentals=0)


def call(body, out_shape, args, n_scalars, us, name, scratch=(), aliases=None):
    smem = pl.BlockSpec(memory_space=pltpu.SMEM)
    vmem = pl.BlockSpec(memory_space=pltpu.VMEM)
    many = isinstance(out_shape, list)
    return pl.pallas_call(
        body,
        out_shape=out_shape,
        in_specs=[smem] * n_scalars + [vmem] * (len(args) - n_scalars),
        out_specs=[vmem] * len(out_shape) if many else vmem,
        scratch_shapes=list(scratch),
        compiler_params=pltpu.CompilerParams(vmem_limit_bytes=VMEM_BYTES),
        cost_estimate=price(us),
        name=name,
    )(*args)


def pack_weights(source, listed, peers, aligned):
    quarter = source.shape[0] // peers
    band_rows = listed.shape[1]
    tail = aligned - 16

    def body(source_ref, listed_ref, *outs):
        for k in range(peers):
            for i in range(quarter):
                outs[k][i, tail:aligned, :] = jnp.zeros((16, BLOCK), jnp.bfloat16)
                outs[k][i, 0:band_rows, :] = listed_ref[source_ref[k * quarter + i]]

    out = jax.ShapeDtypeStruct((quarter, aligned, BLOCK), jnp.bfloat16)
    return call(body, [out] * peers, (source, listed), 1, 3, "pack_weights")


def shifted(rows, start):
    rows = rows.astype(jnp.float32)
    rows = jnp.concatenate([rows, jnp.zeros((8, rows.shape[1]), jnp.float32)], axis=0)
    return pltpu.roll(rows, lax.rem(start, 8), 0)


def rows_at(start, band_rows):
    return pl.ds(pl.multiple_of((start // 8) * 8, 8), band_rows + 8)


def beside(first, second):
    lane = lax.broadcasted_iota(jnp.int32, (first.shape[0], 128), 1)
    second = pltpu.roll(second, 64, 1)
    middle = jnp.where(lane < 64, first[:, 128:256], second[:, 0:128])
    return jnp.concatenate([first[:, 0:128], middle, second[:, 128:256]], axis=1)


def apart(packed):
    return packed[:, 0:256], pltpu.roll(packed[:, 128:384], 192, 1)


def rounds(count, group):
    return (count + group - 1) // group


def spread(count, block, where, weight, points):
    slots, band_rows = weight.shape[:2]
    width = points.shape[1]

    def body(count_ref, block_ref, where_ref, weight_ref, points_ref, out_ref):
        blank = jnp.zeros((width, BLOCK), jnp.bfloat16)

        def group(step, carry):
            for t in range(2):
                pair = 2 * step + t
                one, two = 2 * pair, 2 * pair + 1
                weights = jnp.concatenate(
                    [weight_ref[where_ref[one]], weight_ref[where_ref[two]]], axis=1
                )
                blocks = jnp.concatenate(
                    [
                        jnp.concatenate([points_ref[block_ref[one]], blank], axis=1),
                        jnp.concatenate([blank, points_ref[block_ref[two]]], axis=1),
                    ],
                    axis=0,
                )
                out_ref[pair] = lax.dot_general(
                    weights, blocks, (((1,), (1,)), ((), ())), preferred_element_type=jnp.float32
                ).astype(jnp.bfloat16)
            return carry

        lax.fori_loop(0, rounds(count_ref[0], 4), group, 0)

    out = jax.ShapeDtypeStruct((slots // 2, band_rows, 2 * width), jnp.bfloat16)
    return call(body, out, (count, block, where, weight, points), 3, 3, "spread_blocks")


def render(count, block, place, where, other_count, other_place, weight, points, other, views, half_rows):
    width = points.shape[1]
    band_rows = weight.shape[1]

    def body(
        count_ref, block_ref, place_ref, where_ref, other_count_ref, other_place_ref,
        weight_ref, points_ref, other_ref, *rest
    ):
        outs, acc = rest[:-1], rest[-1]
        acc[...] = jnp.zeros_like(acc)

        def group(step, carry):
            parts = []
            for t in range(GROUP):
                slot = step * GROUP + t
                parts.append(
                    lax.dot_general(
                        shifted(weight_ref[where_ref[slot]], place_ref[slot]).astype(jnp.bfloat16),
                        points_ref[block_ref[slot]],
                        (((1,), (1,)), ((), ())),
                        preferred_element_type=jnp.float32,
                    )
                )
            for t in range(GROUP):
                acc[rows_at(place_ref[step * GROUP + t], band_rows), 0:width] += parts[t]
            return carry

        def other_group(step, carry):
            for t in range(2):
                pair = 2 * step + t
                for value, slot in zip(apart(other_ref[pair].astype(jnp.float32)), (2 * pair, 2 * pair + 1)):
                    start = other_place_ref[slot]
                    acc[rows_at(start, band_rows), :] += shifted(value, start)
            return carry

        lax.fori_loop(0, rounds(count_ref[0], GROUP), group, 0)
        lax.fori_loop(0, rounds(other_count_ref[0], 4), other_group, 0)
        for u, out in enumerate(outs):
            first = acc[2 * u * half_rows : (2 * u + 1) * half_rows, :]
            second = acc[(2 * u + 1) * half_rows : (2 * u + 2) * half_rows, :]
            out[...] = beside(first, second).astype(out.dtype)

    image = jax.ShapeDtypeStruct((half_rows, 2 * width), jnp.bfloat16)
    args = (count, block, place, where, other_count, other_place, weight, points, other)
    scratch = [pltpu.VMEM((2 * views * half_rows + band_rows + 8, 256), jnp.float32)]
    return call(body, [image] * views, args, 6, 5, "render_blocks", scratch)


def unpack_images(image_refs, image, half_rows):
    for u, ref in enumerate(image_refs):
        first, second = apart(ref[...].astype(jnp.float32))
        image[2 * u * half_rows : (2 * u + 1) * half_rows, :] = first
        image[(2 * u + 1) * half_rows : (2 * u + 2) * half_rows, :] = second


def pick(count, place, images, slots, band_rows):
    half_rows, packed = images[0].shape
    views = len(images)

    def body(count_ref, place_ref, *rest):
        image_refs, (out_ref, image) = rest[:views], rest[views:]
        unpack_images(image_refs, image, half_rows)
        image[2 * views * half_rows :, :] = jnp.zeros((band_rows + 8, 256), jnp.float32)

        def group(step, carry):
            for t in range(2):
                pair = 2 * step + t
                bands = []
                for slot in (2 * pair, 2 * pair + 1):
                    start = place_ref[slot]
                    rows = image[rows_at(start, band_rows), :]
                    back = lax.rem(band_rows + 8 - lax.rem(start, 8), band_rows + 8)
                    bands.append(pltpu.roll(rows, back, 0)[0:band_rows])
                out_ref[pair] = beside(*bands).astype(out_ref.dtype)
            return carry

        lax.fori_loop(0, rounds(count_ref[0], 4), group, 0)

    out = jax.ShapeDtypeStruct((slots // 2, band_rows, packed), jnp.bfloat16)
    scratch = [pltpu.VMEM((2 * views * half_rows + band_rows + 8, 256), jnp.float32)]
    return call(body, out, (count, place) + tuple(images), 2, 4, "pick_bands", scratch)


def pull(parts, where, old, blocks, last):
    views = len(parts[0]["images"])
    half_rows, packed = parts[0]["images"][0].shape
    width = packed // 2
    band_rows = parts[0]["weights"].shape[2]
    first = old is None
    scalars = ("count", "block", "place", "other_count", "other_block")
    tables, arrays = [where], []
    for part in parts:
        tables += [part[name] for name in scalars]
        arrays += [part["weights"], part["bands"]] + list(part["images"])
    arrays += [] if first else [old]

    def body(*refs):
        where_ref, table_refs = refs[0], refs[1 : len(tables)]
        array_refs = refs[len(tables) : len(tables) + len(arrays)]
        out_ref, image, acc = refs[len(tables) + len(arrays) :]
        if first:
            acc[...] = jnp.zeros_like(acc)
        else:
            acc[0:blocks] = array_refs[-1][...]

        for i in range(len(parts)):
            count_ref, block_ref, place_ref, other_count_ref, other_block_ref = table_refs[5 * i : 5 * i + 5]
            weight_ref, other_ref, *image_refs = array_refs[(2 + views) * i : (2 + views) * (i + 1)]
            unpack_images(image_refs, image, half_rows)

            def group(step, carry):
                terms = []
                for t in range(GROUP):
                    slot = step * GROUP + t
                    start = place_ref[slot]
                    terms.append(
                        lax.dot_general(
                            image[rows_at(start, band_rows), 0:width].astype(jnp.bfloat16),
                            shifted(weight_ref[0, where_ref[slot]], start).astype(jnp.bfloat16),
                            (((0,), (0,)), ((), ())),
                            preferred_element_type=jnp.float32,
                        )
                    )
                for t in range(GROUP):
                    acc[block_ref[step * GROUP + t]] += terms[t]
                return carry

            def other_group(step, carry):
                terms = []
                for t in range(2):
                    pair = 2 * step + t
                    both = [weight_ref[1, where_ref[2 * pair + s]] for s in range(2)]
                    terms.append(
                        lax.dot_general(
                            other_ref[pair],
                            jnp.concatenate(both, axis=1),
                            (((0,), (0,)), ((), ())),
                            preferred_element_type=jnp.float32,
                        )
                    )
                for t in range(2):
                    pair = 2 * step + t
                    acc[other_block_ref[2 * pair]] += terms[t][0:width, 0:BLOCK]
                    acc[other_block_ref[2 * pair + 1]] += terms[t][width:, BLOCK:]
                return carry

            lax.fori_loop(0, rounds(count_ref[0], GROUP), group, 0)
            lax.fori_loop(0, rounds(other_count_ref[0], 4), other_group, 0)
        out_ref[...] = acc[0:blocks].astype(out_ref.dtype)

    out = jax.ShapeDtypeStruct((blocks, width, BLOCK), jnp.bfloat16 if last else jnp.float32)
    scratch = [
        pltpu.VMEM((2 * views * half_rows + band_rows + 8, 256), jnp.float32),
        pltpu.VMEM((blocks + 1, width, BLOCK), jnp.float32),
    ]
    us = 3 + 5 * len(parts)
    return call(body, out, tuple(tables + arrays), len(tables), us, "pull_blocks", scratch)


def loss_kernel(u, teacher_width, side_ref, parts_ref, head_ref, teacher_ref, image_ref, grad_ref):
    rows, packed = parts_ref.shape[1], parts_ref.shape[2]
    width = packed // 2
    lane = lax.broadcasted_iota(jnp.int32, (rows, packed), 1)
    head = head_ref[...]

    def halves_of(parts):
        halves = [[], []]
        for pair in range(2):
            one, two = (part.astype(jnp.float32) for part in parts[2 * pair : 2 * pair + 2])
            halves[0].append(jnp.where(lane < width, one, pltpu.roll(two, width, 1)))
            halves[1].append(jnp.where(lane < width, pltpu.roll(one, width, 1), two))
        return [jnp.concatenate(half, axis=1) for half in halves]

    halves = halves_of([parts_ref[d] for d in range(4)])
    targets = halves_of([teacher_ref[side_ref[0] ^ g, u] for g in range(4)])
    rendered_all, grad_all, images = [], [], []
    for half in range(2):
        rendered = halves[half].astype(jnp.bfloat16)
        projected = jnp.dot(rendered, head, preferred_element_type=jnp.float32)
        square = jnp.sum(projected * projected, axis=1, keepdims=True)
        scale = jnp.sqrt(square / teacher_width + 1e-06)
        normed = projected / scale
        residual = normed - targets[half]
        inner = jnp.sum(residual * normed, axis=1, keepdims=True) / teacher_width
        grad_proj = ((residual - normed * inner) / scale).astype(jnp.bfloat16)
        images.append(
            lax.dot_general(
                grad_proj, head, (((1,), (1,)), ((), ())), preferred_element_type=jnp.float32
            )
        )
        rendered_all.append(rendered)
        grad_all.append(grad_proj)
    for pair in range(2):
        cols = slice(2 * pair * width, 2 * (pair + 1) * width)
        first, second = images[0][:, cols], images[1][:, cols]
        image_ref[2 * pair] = jnp.where(lane < width, first, pltpu.roll(second, width, 1)).astype(
            image_ref.dtype
        )
        image_ref[2 * pair + 1] = jnp.where(
            lane < width, pltpu.roll(first, width, 1), second
        ).astype(image_ref.dtype)
    grad_ref[...] = lax.dot_general(
        jnp.concatenate(rendered_all, axis=0),
        jnp.concatenate(grad_all, axis=0),
        (((0,), (0,)), ((), ())),
        preferred_element_type=jnp.float32,
    )


def loss(u, side, parts, head, teacher):
    teacher_width = head.shape[1]
    outs = [
        jax.ShapeDtypeStruct(parts.shape, jnp.bfloat16),
        jax.ShapeDtypeStruct(head.shape, jnp.float32),
    ]
    body = lambda *refs: loss_kernel(u, teacher_width, *refs)
    return call(body, outs, (side, parts, head, teacher), 1, 3, "loss_rows")


def turn_teacher(side, teacher, sides, padded):
    views, width, pixels = teacher.shape
    half_rows = padded // 2
    rows = half_rows // sides
    whole = pixels // 128 * 128

    def body(side_ref, teacher_ref, *rest):
        outs, (across, turned) = rest[:sides], rest[sides:]
        for u in range(views):
            across[width:, :] = jnp.zeros((256 - width, padded), jnp.float32)
            across[0:width, whole:] = jnp.zeros((width, padded - whole), jnp.float32)
            across[0:width, 0:pixels] = teacher_ref[u].astype(jnp.float32)
            turned[...] = across[...].T
            for d in range(sides):
                start = pl.multiple_of((side_ref[0] ^ d) * rows, 16)
                first = turned[pl.ds(start, rows), :]
                second = turned[pl.ds(half_rows + start, rows), :]
                outs[d][u] = beside(first, second).astype(jnp.bfloat16)

    out = jax.ShapeDtypeStruct((views, rows, 2 * width), jnp.bfloat16)
    scratch = [pltpu.VMEM((256, padded), jnp.float32), pltpu.VMEM((padded, 256), jnp.float32)]
    return call(body, [out] * sides, (side, teacher), 1, 6, "turn_teacher", scratch)


def after(value, *earlier):
    return lax.optimization_barrier((value,) + earlier)[0]


def total(*terms):
    acc = terms[0].astype(jnp.float32)
    for term in terms[1:]:
        acc = acc + term.astype(jnp.float32)
    return acc.astype(jnp.bfloat16)


def in_order(own_first, other):
    index, mine = own_first
    return jnp.where(
        index == 0, jnp.concatenate([mine, other], 0), jnp.concatenate([other, mine], 0)
    )


def per_device(points, head_weight, teacher, splat_weight, block_owner, block_local, block_row):
    peers, sides = lax.axis_size("view"), lax.axis_size("feat")
    blocks, width = points.shape[0], points.shape[1]
    view_count, visible, band_rows = splat_weight.shape[:3]
    requests = view_count * visible
    capacity = max(3, (3 * requests + 2 * peers - 1) // (2 * peers))
    quarter = -(-capacity // sides)
    slots = quarter * sides
    pixels = teacher.shape[2]
    unit = 2 * sides * 16
    padded = -(-pixels // unit) * unit
    half_rows = padded // 2
    me, side = lax.axis_index("view"), lax.axis_index("feat")
    line, across, core = me // 2, side // 2, side % 2

    def hop(value, axis, pairs):
        return lax.ppermute(value, axis, pairs)

    def swap(value, axis, k):
        size = peers if axis == "view" else sides
        return hop(value, axis, [(i, i ^ k) for i in range(size)])

    def along(value, moves):
        return hop(value, "view", [(2 * a + y, 2 * b + y) for a, b in moves for y in range(2)])

    ints = jnp.int32
    owners = block_owner.reshape(requests)
    positions = jnp.arange(requests, dtype=ints)
    earlier = (owners[:, None] == owners[None, :]) & (positions[None, :] < positions[:, None])
    rank = jnp.sum(earlier.astype(ints), axis=1)
    peer_ids = me ^ jnp.arange(peers, dtype=ints)
    send_ranks = side * quarter + jnp.arange(quarter, dtype=ints)
    match = (owners[None, None, :] == peer_ids[:, None, None]) & (
        rank[None, None, :] == send_ranks[None, :, None]
    )
    source = jnp.sum(jnp.where(match, positions[None, None, :], 0), axis=2)
    aligned = -(-band_rows // 16) * 16
    listed = splat_weight.reshape(requests, band_rows, BLOCK)
    packed = pack_weights(source.reshape(peers * quarter), listed, peers, aligned)

    view_of = positions // visible
    start = view_of * padded + block_row.reshape(requests) * GRID
    told = jnp.stack([owners, rank, block_local.reshape(requests), start])
    heard = told[None]
    for k in (4, 2, 1):
        heard = jnp.concatenate([heard, swap(heard, "view", k)], axis=0)
    heard = heard.reshape((2, 2, 2) + told.shape).transpose(2, 1, 0, 3, 4).reshape((peers,) + told.shape)
    slot_ids = jnp.arange(slots, dtype=ints)

    def asked_of(owner, told):
        asked = (told[:, None, 0, :] == owner) & (told[:, None, 1, :] == slot_ids[None, :, None])
        filled = jnp.any(asked, axis=2)
        block = jnp.sum(jnp.where(asked, told[:, None, 2, :], 0), axis=2)
        place = jnp.sum(jnp.where(asked, told[:, None, 3, :], 0), axis=2)
        place = jnp.where(filled, place, view_count * padded)
        return jnp.sum(filled.astype(ints), axis=1), block, jnp.where(filled, block, blocks), place

    counts, block_of, pull_of, place_of = asked_of(me, heard)
    pair_counts, _, _, pair_places = asked_of(me ^ 1, heard[::2])
    turn = (slot_ids // quarter) ^ side
    turn = (turn % 2) * 2 + turn // 2
    where_of = turn * quarter + slot_ids % quarter

    weights, hops = {}, None
    for j in (3, 2, 1, 0):
        got = []
        for k in (2 * j + 1, 2 * j):
            value = packed[k] if hops is None else after(packed[k], hops)
            got.append(swap(value, "view", k) if k else value)
        got = hops = jnp.stack(got[::-1])
        got = jnp.concatenate([got, swap(got, "feat", 2)], axis=1)
        weights[j] = jnp.concatenate([got, swap(got, "feat", 1)], axis=1)

    kept, arrived = {}, None
    for j in (3, 2, 1, 0):
        k = 2 * j + 1
        given = spread(counts[k : k + 1], block_of[k], where_of, weights[j][1], points)
        arrived = swap(given if arrived is None else after(given, arrived), "view", 1)
        k = 2 * j
        kept[j] = render(
            counts[k : k + 1], block_of[k], place_of[k], where_of,
            pair_counts[j : j + 1], pair_places[j], weights[j][0], points, arrived, view_count, half_rows,
        )

    side_id = side.reshape(1).astype(ints)
    teacher = after(teacher.transpose(1, 0, 2), weights[0])
    target = turn_teacher(side_id, teacher, sides, padded)
    target = jnp.stack([swap(target[d], "feat", d) if d else target[d] for d in range(sides)])
    head_weight = after(head_weight, weights[0])
    head = jnp.concatenate([head_weight, swap(head_weight, "feat", 2)], axis=0)
    head = jnp.concatenate([head, swap(head, "feat", 1)], axis=0)

    rendered = []
    for u in range(view_count):
        far = along(kept[3][u], [(0, 1), (3, 2)])
        mid = total(kept[2][u], far)
        inward = along(mid, [(0, 1), (3, 2)])
        between = along(mid, [(1, 2), (2, 1)])
        near = along(total(kept[1][u], between), [(0, 1), (1, 0), (2, 3), (3, 2)])
        centre = along(total(kept[3][u], inward), [(1, 2), (2, 1)])
        rendered.append(total(kept[0][u], near, centre))

    grads, images = [], []
    side_rows, seventh = half_rows // 2, half_rows // sides
    for u in range(view_count):
        whole = rendered[u]
        mine = lax.dynamic_slice_in_dim(whole, across * side_rows, side_rows, 0)
        other = lax.dynamic_slice_in_dim(whole, (1 - across) * side_rows, side_rows, 0)
        both = jnp.stack([mine, swap(other, "feat", 2)])
        mine = lax.dynamic_slice_in_dim(both, core * seventh, seventh, 1)
        other = lax.dynamic_slice_in_dim(both, (1 - core) * seventh, seventh, 1)
        parts = jnp.concatenate([mine, swap(other, "feat", 1)], axis=0)
        image, grad = loss(u, side_id, parts, head, target)
        grads.append(grad)
        back = swap(image[2:4], "feat", 1)
        rows = [in_order((core, image[i]), back[i]) for i in range(2)]
        images.append(in_order((across, rows[0]), swap(rows[1], "feat", 2)))

    middle = (line == 1) | (line == 2)
    chunks = {j: [] for j in range(4)}
    marks = []
    for u in range(view_count):
        own = images[u]
        near = along(own, [(0, 1), (1, 0), (2, 3), (3, 2)])
        centre = along(own, [(1, 2), (2, 1)])
        out_near = along(centre, [(1, 0), (2, 3)])
        cross = along(near, [(1, 2), (2, 1)])
        out_far = along(cross, [(1, 0), (2, 3)])
        marks.append((near, cross, out_far))
        for j, value in enumerate(
            (own, near, jnp.where(middle, cross, out_near), jnp.where(middle, centre, out_far))
        ):
            chunks[j].append(value)
    parts, bands = [], None
    for j in range(4):
        bands = pick(pair_counts[j : j + 1], pair_places[j], chunks[j], slots, aligned)
        bands = swap(bands if not parts else after(bands, parts[-1]["bands"]), "view", 1)
        own, other = 2 * j, 2 * j + 1
        parts.append(
            dict(
                count=counts[own : own + 1], block=pull_of[own], place=place_of[own],
                other_count=counts[other : other + 1], other_block=pull_of[other],
                weights=weights[j], images=chunks[j], bands=bands,
            )
        )
    early = pull(parts[:3], where_of, None, blocks, False)
    grad_points = pull(parts[3:], where_of, early, blocks, True)

    grad = grads[0]
    for more in grads[1:]:
        grad = grad + more
    grad = grad.reshape(2, 2, width, grad.shape[1])
    grad = grad[0] + swap(grad[1], "feat", 1)
    grad = grad[0] + swap(grad[1], "feat", 2)
    marks = [marks[u][i] for i in range(3) for u in range(view_count)]
    bits = [(1, me % 2), (4, me // 4), (2, line % 2)]
    for (k, bit), mark in zip(bits, marks):
        rows = grad.shape[0] // 2
        grad = after(grad, mark)
        mine = lax.dynamic_slice_in_dim(grad, bit * rows, rows, 0)
        other = lax.dynamic_slice_in_dim(grad, (1 - bit) * rows, rows, 0)
        grad = mine + swap(other, "view", k)
    grad = grad / (view_count * peers * GRID)
    for (k, bit), mark in zip(bits[::-1], marks[3:]):
        grad = after(grad, mark)
        grad = in_order((bit, grad), swap(grad, "view", k))
    return (grad_points, grad)


def solution(mesh):
    size = mesh.shape
    paired = size["view"] == 8 and size["feat"] == 4
    placed = (
        P("view", "feat", None),
        P("feat", None),
        P("feat", "view", None),
        P("view", None, None, None),
        P("view", None, None),
        P("view", None),
        P("view", None),
    )
    return jax.shard_map(
        per_device if paired else per_device_listed,
        mesh=mesh,
        in_specs=placed,
        out_specs=(P("view", "feat", None), P("feat", None)),
        check_vma=False,
    )
```

```python
import jax
import jax.numpy as jnp
from jax import lax
from jax.experimental import pallas as pl
from jax.experimental.pallas import tpu as pltpu
from jax.sharding import PartitionSpec as P

GRID = 37
BAND = 2
BLOCK = 128
GROUP = 4
VMEM_BYTES = 48 * 1024 * 1024


def slot_plan(owners, peer_count, capacity):
    total_requests = owners.shape[0]
    positions = jnp.arange(total_requests, dtype=jnp.int32)
    earlier = (owners[:, None] == owners[None, :]) & (positions[None, :] < positions[:, None])
    slot_rank = jnp.sum(earlier.astype(jnp.int32), axis=1)
    target = owners * capacity + slot_rank
    slot_ids = jnp.arange(peer_count * capacity, dtype=jnp.int32)
    matches = target[None, :] == slot_ids[:, None]
    source = jnp.sum(jnp.where(matches, positions[None, :], 0), axis=1)
    filled = jnp.any(matches, axis=1)
    return (target, source, filled)


def per_device_listed(points, head_weight, teacher, splat_weight, block_owner, block_local, block_row):
    peer_count = lax.axis_size("view")
    local_width = points.shape[1]
    view_count = splat_weight.shape[0]
    visible = splat_weight.shape[1]
    requests = view_count * visible
    capacity = max(3, (3 * requests + 2 * peer_count - 1) // (2 * peer_count))
    owners = block_owner.reshape(requests)
    local_ids = block_local.reshape(requests)
    target, source, filled = slot_plan(owners, peer_count, capacity)
    wanted = jnp.where(filled, jnp.take(local_ids, source), 0)
    columns = jnp.arange(GRID, dtype=jnp.int32)
    row_masks = [
        (block_row[:, :, None] + offset == columns[None, None, :]).astype(jnp.bfloat16)
        for offset in range(BAND)
    ]
    empty_bf = jnp.zeros((), jnp.bfloat16)
    asked_ids = lax.all_to_all(wanted, "view", split_axis=0, concat_axis=0, tiled=True)
    sent_rows = jnp.take(points, asked_ids, axis=0)
    arrived = lax.all_to_all(sent_rows, "view", split_axis=0, concat_axis=0, tiled=True)
    fetched = jnp.take(arrived, target, axis=0).reshape(view_count, visible, local_width, BLOCK)
    contrib = jnp.einsum(
        "vjcp,vjdp->vjcd", splat_weight, fetched, preferred_element_type=jnp.float32
    ).astype(jnp.bfloat16)
    rendered = jnp.zeros((view_count, GRID, GRID, local_width), jnp.float32)
    for offset in range(BAND):
        band_part = contrib[:, :, offset * GRID : (offset + 1) * GRID, :]
        rendered = rendered + jnp.einsum(
            "vjr,vjcd->vrcd", row_masks[offset], band_part, preferred_element_type=jnp.float32
        )
    rendered_rows = rendered.astype(jnp.bfloat16).reshape(view_count * GRID * GRID, local_width)
    pixel_rows = rendered_rows.shape[0]
    teacher_width = head_weight.shape[1]
    local_teacher = teacher.shape[0]
    contract_first = (((0,), (1,)), ((), ()))
    head_full = lax.all_gather(head_weight, "feat", axis=0, tiled=True)
    head_cols = lax.dynamic_slice_in_dim(
        head_full, lax.axis_index("feat") * local_teacher, local_teacher, 1
    )
    head_part = head_cols
    projected = lax.dot_general(
        head_part,
        lax.all_gather(rendered_rows, "feat", axis=1, tiled=True),
        contract_first,
        preferred_element_type=jnp.float32,
    )
    square_sum = lax.psum(jnp.sum(projected * projected, axis=0), "feat")
    scale_rows = jnp.sqrt(square_sum / teacher_width + 1e-06)
    normed = projected / scale_rows[None, :]
    target_feat = teacher.reshape(local_teacher, pixel_rows).astype(jnp.float32)
    residual = normed - target_feat
    row_dot = lax.psum(jnp.sum(residual * normed, axis=0), "feat")
    grad_proj = (
        (residual - normed * (row_dot / teacher_width)[None, :]) / scale_rows[None, :]
    ).astype(jnp.bfloat16)
    shard_part = lax.all_gather(grad_proj, "feat", axis=0, tiled=True)
    head_part = head_weight
    grad_image = lax.dot_general(
        shard_part, head_part, contract_first, preferred_element_type=jnp.float32
    )
    column_part = lax.dot_general(
        rendered_rows, shard_part, contract_first, preferred_element_type=jnp.float32
    )
    grad_head = column_part
    grad_image, grad_head = (grad_image, grad_head)
    head_grad = lax.psum(grad_head, "view") / (view_count * peer_count * GRID)
    grad_image = grad_image.astype(jnp.bfloat16).reshape(view_count, GRID, GRID, local_width)
    pieces = [
        jnp.einsum("vjr,vrcd->vjcd", row_mask, grad_image, preferred_element_type=jnp.float32)
        for row_mask in row_masks
    ]
    grad_contrib = jnp.concatenate(pieces, axis=2).astype(jnp.bfloat16)
    grad_block = jnp.einsum(
        "vjcp,vjcd->vjdp", splat_weight, grad_contrib, preferred_element_type=jnp.float32
    ).astype(jnp.bfloat16)
    grad_block = grad_block.reshape(requests, local_width, BLOCK)
    packed = jnp.where(filled[:, None, None], jnp.take(grad_block, source, axis=0), empty_bf)
    landed = lax.all_to_all(packed, "view", split_axis=0, concat_axis=0, tiled=True)
    summed = jax.ops.segment_sum(
        landed.astype(jnp.float32), asked_ids, num_segments=points.shape[0]
    )
    grad_points = summed.astype(jnp.bfloat16)
    return (grad_points, head_grad)


def price(us):
    return pl.CostEstimate(flops=int(us * 1e9), bytes_accessed=int(us * 2e6), transcendentals=0)


def call(body, out_shape, args, n_scalars, us, name, scratch=(), aliases=None):
    smem = pl.BlockSpec(memory_space=pltpu.SMEM)
    vmem = pl.BlockSpec(memory_space=pltpu.VMEM)
    many = isinstance(out_shape, list)
    return pl.pallas_call(
        body,
        out_shape=out_shape,
        in_specs=[smem] * n_scalars + [vmem] * (len(args) - n_scalars),
        out_specs=[vmem] * len(out_shape) if many else vmem,
        scratch_shapes=list(scratch),
        compiler_params=pltpu.CompilerParams(vmem_limit_bytes=VMEM_BYTES),
        cost_estimate=price(us),
        name=name,
    )(*args)


def pack_weights(source, listed, peers, aligned):
    quarter = source.shape[0] // peers
    band_rows = listed.shape[1]
    tail = aligned - 16

    def body(source_ref, listed_ref, *outs):
        for k in range(peers):
            for i in range(quarter):
                outs[k][i, tail:aligned, :] = jnp.zeros((16, BLOCK), jnp.bfloat16)
                outs[k][i, 0:band_rows, :] = listed_ref[source_ref[k * quarter + i]]

    out = jax.ShapeDtypeStruct((quarter, aligned, BLOCK), jnp.bfloat16)
    return call(body, [out] * peers, (source, listed), 1, 3, "pack_weights")


def shifted(rows, start):
    rows = rows.astype(jnp.float32)
    rows = jnp.concatenate([rows, jnp.zeros((8, rows.shape[1]), jnp.float32)], axis=0)
    return pltpu.roll(rows, lax.rem(start, 8), 0)


def rows_at(start, band_rows):
    return pl.ds(pl.multiple_of((start // 8) * 8, 8), band_rows + 8)


def beside(first, second):
    lane = lax.broadcasted_iota(jnp.int32, (first.shape[0], 128), 1)
    second = pltpu.roll(second, 64, 1)
    middle = jnp.where(lane < 64, first[:, 128:256], second[:, 0:128])
    return jnp.concatenate([first[:, 0:128], middle, second[:, 128:256]], axis=1)


def apart(packed):
    return packed[:, 0:256], pltpu.roll(packed[:, 128:384], 192, 1)


def rounds(count, group):
    return (count + group - 1) // group


def spread(count, block, where, weight, points):
    slots, band_rows = weight.shape[:2]
    width = points.shape[1]

    def body(count_ref, block_ref, where_ref, weight_ref, points_ref, out_ref):
        blank = jnp.zeros((width, BLOCK), jnp.bfloat16)

        def group(step, carry):
            for t in range(2):
                pair = 2 * step + t
                one, two = 2 * pair, 2 * pair + 1
                weights = jnp.concatenate(
                    [weight_ref[where_ref[one]], weight_ref[where_ref[two]]], axis=1
                )
                blocks = jnp.concatenate(
                    [
                        jnp.concatenate([points_ref[block_ref[one]], blank], axis=1),
                        jnp.concatenate([blank, points_ref[block_ref[two]]], axis=1),
                    ],
                    axis=0,
                )
                out_ref[pair] = lax.dot_general(
                    weights, blocks, (((1,), (1,)), ((), ())), preferred_element_type=jnp.float32
                ).astype(jnp.bfloat16)
            return carry

        lax.fori_loop(0, rounds(count_ref[0], 4), group, 0)

    out = jax.ShapeDtypeStruct((slots // 2, band_rows, 2 * width), jnp.bfloat16)
    return call(body, out, (count, block, where, weight, points), 3, 0.1, "spread_blocks")


def render(count, block, place, where, other_count, other_place, weight, points, other, views, half_rows):
    width = points.shape[1]
    band_rows = weight.shape[1]

    def body(
        count_ref, block_ref, place_ref, where_ref, other_count_ref, other_place_ref,
        weight_ref, points_ref, other_ref, *rest
    ):
        out, acc = rest
        acc[...] = jnp.zeros_like(acc)

        def group(step, carry):
            parts = []
            for t in range(GROUP):
                slot = step * GROUP + t
                parts.append(
                    lax.dot_general(
                        shifted(weight_ref[where_ref[slot]], place_ref[slot]).astype(jnp.bfloat16),
                        points_ref[block_ref[slot]],
                        (((1,), (1,)), ((), ())),
                        preferred_element_type=jnp.float32,
                    )
                )
            for t in range(GROUP):
                acc[rows_at(place_ref[step * GROUP + t], band_rows), 0:width] += parts[t]
            return carry

        def other_group(step, carry):
            for t in range(2):
                pair = 2 * step + t
                for value, slot in zip(apart(other_ref[pair].astype(jnp.float32)), (2 * pair, 2 * pair + 1)):
                    start = other_place_ref[slot]
                    acc[rows_at(start, band_rows), :] += shifted(value, start)
            return carry

        lax.fori_loop(0, rounds(count_ref[0], GROUP), group, 0)
        lax.fori_loop(0, rounds(other_count_ref[0], 4), other_group, 0)
        for u in range(views):
            first = acc[2 * u * half_rows : (2 * u + 1) * half_rows, :]
            second = acc[(2 * u + 1) * half_rows : (2 * u + 2) * half_rows, :]
            out[u * half_rows : (u + 1) * half_rows, :] = beside(first, second).astype(out.dtype)

    images = jax.ShapeDtypeStruct((views * half_rows, 2 * width), jnp.bfloat16)
    args = (count, block, place, where, other_count, other_place, weight, points, other)
    scratch = [pltpu.VMEM((2 * views * half_rows + band_rows + 8, 256), jnp.float32)]
    return call(body, images, args, 6, 5, "render_blocks", scratch)


def unpack_images(images_ref, image, half_rows):
    for u in range(images_ref.shape[0] // half_rows):
        first, second = apart(images_ref[u * half_rows : (u + 1) * half_rows, :].astype(jnp.float32))
        image[2 * u * half_rows : (2 * u + 1) * half_rows, :] = first
        image[(2 * u + 1) * half_rows : (2 * u + 2) * half_rows, :] = second


def pick(count, place, images, slots, band_rows, half_rows):
    pixels, packed = 2 * images.shape[0], images.shape[1]

    def body(count_ref, place_ref, images_ref, out_ref, image):
        unpack_images(images_ref, image, half_rows)
        image[pixels:, :] = jnp.zeros((band_rows + 8, 256), jnp.float32)

        def group(step, carry):
            for t in range(2):
                pair = 2 * step + t
                bands = []
                for slot in (2 * pair, 2 * pair + 1):
                    start = place_ref[slot]
                    rows = image[rows_at(start, band_rows), :]
                    back = lax.rem(band_rows + 8 - lax.rem(start, 8), band_rows + 8)
                    bands.append(pltpu.roll(rows, back, 0)[0:band_rows])
                out_ref[pair] = beside(*bands).astype(out_ref.dtype)
            return carry

        lax.fori_loop(0, rounds(count_ref[0], 4), group, 0)

    out = jax.ShapeDtypeStruct((slots // 2, band_rows, packed), jnp.bfloat16)
    scratch = [pltpu.VMEM((pixels + band_rows + 8, 256), jnp.float32)]
    return call(body, out, (count, place, images), 2, 1, "pick_bands", scratch)


def pull(jobs, where, old, blocks, half_rows, last):
    band_rows = jobs[0]["weights"].shape[1]
    pixels = max([2 * job["images"].shape[0] for job in jobs if "place" in job], default=0)
    width = jobs[0]["width"]
    first = old is None
    tables, arrays, layout = [where], [], []
    for job in jobs:
        layout.append((len(tables), len(arrays), "place" in job))
        tables += [job["count"], job["block"]] + ([job["place"]] if "place" in job else [])
        arrays += [job["weights"], job["images"] if "place" in job else job["bands"]]
    arrays += [] if first else [old]

    def body(*refs):
        where_ref = refs[0]
        array_refs = refs[len(tables) : len(tables) + len(arrays)]
        out_ref, image, acc = refs[len(tables) + len(arrays) :]
        if first:
            acc[...] = jnp.zeros_like(acc)
        else:
            acc[0:blocks] = array_refs[-1][...]

        for table, array, own in layout:
            count_ref, block_ref, weight_ref = refs[table], refs[table + 1], array_refs[array]
            place_ref, other_ref = refs[table + 2], array_refs[array + 1]
            if own:
                unpack_images(other_ref, image, half_rows)

            def group(step, carry):
                terms = []
                for t in range(GROUP):
                    slot = step * GROUP + t
                    start = place_ref[slot]
                    terms.append(
                        lax.dot_general(
                            image[rows_at(start, band_rows), 0:width].astype(jnp.bfloat16),
                            shifted(weight_ref[where_ref[slot]], start).astype(jnp.bfloat16),
                            (((0,), (0,)), ((), ())),
                            preferred_element_type=jnp.float32,
                        )
                    )
                for t in range(GROUP):
                    acc[block_ref[step * GROUP + t]] += terms[t]
                return carry

            def other_group(step, carry):
                terms = []
                for t in range(2):
                    pair = 2 * step + t
                    both = [weight_ref[where_ref[2 * pair + s]] for s in range(2)]
                    terms.append(
                        lax.dot_general(
                            other_ref[pair],
                            jnp.concatenate(both, axis=1),
                            (((0,), (0,)), ((), ())),
                            preferred_element_type=jnp.float32,
                        )
                    )
                for t in range(2):
                    pair = 2 * step + t
                    acc[block_ref[2 * pair]] += terms[t][0:width, 0:BLOCK]
                    acc[block_ref[2 * pair + 1]] += terms[t][width:, BLOCK:]
                return carry

            lax.fori_loop(0, rounds(count_ref[0], GROUP), group if own else other_group, 0)
        out_ref[...] = acc[0:blocks].astype(out_ref.dtype)

    out = jax.ShapeDtypeStruct((blocks, width, BLOCK), jnp.bfloat16 if last else jnp.float32)
    scratch = [
        pltpu.VMEM((pixels + band_rows + 8, 256), jnp.float32),
        pltpu.VMEM((blocks + 1, width, BLOCK), jnp.float32),
    ]
    us = 1
    return call(body, out, tuple(tables + arrays), len(tables), us, "pull_blocks", scratch)


def loss_kernel(u, teacher_width, side_ref, head_ref, teacher_ref, *rest):
    parts_refs, image_refs, grad_ref = rest[0:4], rest[-5:-1], rest[-1]
    rows, packed = parts_refs[0].shape
    width = packed // 2
    lane = lax.broadcasted_iota(jnp.int32, (rows, packed), 1)
    head = head_ref[...]

    def halves_of(parts):
        halves = [[], []]
        for pair in range(2):
            one, two = (part.astype(jnp.float32) for part in parts[2 * pair : 2 * pair + 2])
            halves[0].append(jnp.where(lane < width, one, pltpu.roll(two, width, 1)))
            halves[1].append(jnp.where(lane < width, pltpu.roll(one, width, 1), two))
        return [jnp.concatenate(half, axis=1) for half in halves]

    halves = halves_of([ref[...] for ref in parts_refs])
    targets = halves_of([teacher_ref[side_ref[0] ^ g, u] for g in range(4)])
    rendered_all, grad_all, images = [], [], []
    for half in range(2):
        rendered = halves[half].astype(jnp.bfloat16)
        projected = jnp.dot(rendered, head, preferred_element_type=jnp.float32)
        square = jnp.sum(projected * projected, axis=1, keepdims=True)
        scale = jnp.sqrt(square / teacher_width + 1e-06)
        normed = projected / scale
        residual = normed - targets[half]
        inner = jnp.sum(residual * normed, axis=1, keepdims=True) / teacher_width
        grad_proj = ((residual - normed * inner) / scale).astype(jnp.bfloat16)
        images.append(
            lax.dot_general(grad_proj, head, (((1,), (1,)), ((), ())), preferred_element_type=jnp.float32)
        )
        rendered_all.append(rendered)
        grad_all.append(grad_proj)
    for pair in range(2):
        cols = slice(2 * pair * width, 2 * (pair + 1) * width)
        first, second = images[0][:, cols], images[1][:, cols]
        one = jnp.where(lane < width, first, pltpu.roll(second, width, 1))
        two = jnp.where(lane < width, pltpu.roll(first, width, 1), second)
        image_refs[2 * pair][...] = one.astype(jnp.bfloat16)
        image_refs[2 * pair + 1][...] = two.astype(jnp.bfloat16)
    grad = lax.dot_general(
        jnp.concatenate(rendered_all, axis=0),
        jnp.concatenate(grad_all, axis=0),
        (((0,), (0,)), ((), ())),
        preferred_element_type=jnp.float32,
    )
    grad_ref[...] = grad if len(rest) == 9 else grad + rest[4][...]


def loss(u, side, parts, head, teacher, grad):
    teacher_width = head.shape[1]
    outs = [jax.ShapeDtypeStruct(parts[0].shape, jnp.bfloat16)] * len(parts)
    outs += [jax.ShapeDtypeStruct(head.shape, jnp.float32)]
    body = lambda *refs: loss_kernel(u, teacher_width, *refs)
    args = (side, head, teacher) + tuple(parts) + (() if grad is None else (grad,))
    *images, grad = call(body, outs, args, 1, 3, "loss_rows")
    return images, grad


def deal(side, terms, sides, half_rows):
    rows = half_rows // sides
    views = terms[0].shape[0] // half_rows

    def body(side_ref, *refs):
        for u in range(views):
            for d in range(sides):
                start = pl.multiple_of(u * half_rows + (side_ref[0] ^ d) * rows, 16)
                value = refs[0][pl.ds(start, rows), :].astype(jnp.float32)
                for ref in refs[1 : len(terms)]:
                    value = value + ref[pl.ds(start, rows), :].astype(jnp.float32)
                refs[len(terms) + u * sides + d][...] = value.astype(jnp.bfloat16)

    out = jax.ShapeDtypeStruct((rows, terms[0].shape[1]), jnp.bfloat16)
    parts = call(body, [out] * (views * sides), (side,) + tuple(terms), 1, 2, "deal_rows")
    return [parts[u * sides : (u + 1) * sides] for u in range(views)]


def gather(side, parts, half_rows):
    views, sides = len(parts), len(parts[0])
    rows, lanes = parts[0][0].shape

    def body(side_ref, *refs):
        for u in range(views):
            for d in range(sides):
                start = pl.multiple_of(u * half_rows + (side_ref[0] ^ d) * rows, 16)
                refs[-1][pl.ds(start, rows), :] = refs[u * sides + d][...]

    out = jax.ShapeDtypeStruct((views * half_rows, lanes), jnp.bfloat16)
    return call(body, out, (side,) + tuple(sum(parts, [])), 1, 2, "gather_rows")


def turn_teacher(side, teacher, sides, padded):
    views, width, pixels = teacher.shape
    half_rows = padded // 2
    rows = half_rows // sides
    whole = pixels // 128 * 128

    def body(side_ref, teacher_ref, *rest):
        outs, (across, turned) = rest[:sides], rest[sides:]
        for u in range(views):
            across[width:, :] = jnp.zeros((256 - width, padded), jnp.float32)
            across[0:width, whole:] = jnp.zeros((width, padded - whole), jnp.float32)
            across[0:width, 0:pixels] = teacher_ref[u].astype(jnp.float32)
            turned[...] = across[...].T
            for d in range(sides):
                start = pl.multiple_of((side_ref[0] ^ d) * rows, 16)
                first = turned[pl.ds(start, rows), :]
                second = turned[pl.ds(half_rows + start, rows), :]
                outs[d][u] = beside(first, second).astype(jnp.bfloat16)

    out = jax.ShapeDtypeStruct((views, rows, 2 * width), jnp.bfloat16)
    scratch = [pltpu.VMEM((256, padded), jnp.float32), pltpu.VMEM((padded, 256), jnp.float32)]
    return call(body, [out] * sides, (side, teacher), 1, 6, "turn_teacher", scratch)


def after(value, *earlier):
    return lax.optimization_barrier((value,) + earlier)[0]


def total(*terms):
    acc = terms[0].astype(jnp.float32)
    for term in terms[1:]:
        acc = acc + term.astype(jnp.float32)
    return acc.astype(jnp.bfloat16)


def in_order(own_first, other):
    index, mine = own_first
    return jnp.where(
        index == 0, jnp.concatenate([mine, other], 0), jnp.concatenate([other, mine], 0)
    )


def per_device(points, head_weight, teacher, splat_weight, block_owner, block_local, block_row):
    peers, sides = lax.axis_size("view"), lax.axis_size("feat")
    blocks, width = points.shape[0], points.shape[1]
    view_count, visible, band_rows = splat_weight.shape[:3]
    requests = view_count * visible
    capacity = max(3, (3 * requests + 2 * peers - 1) // (2 * peers))
    quarter = -(-capacity // sides)
    slots = quarter * sides
    pixels = teacher.shape[2]
    unit = 2 * sides * 16
    padded = -(-pixels // unit) * unit
    half_rows = padded // 2
    me, side = lax.axis_index("view"), lax.axis_index("feat")
    line, across, core = me // 2, side // 2, side % 2

    def hop(value, axis, pairs):
        return lax.ppermute(value, axis, pairs)

    def swap(value, axis, k):
        size = peers if axis == "view" else sides
        return hop(value, axis, [(i, i ^ k) for i in range(size)])

    def along(value, moves):
        return hop(value, "view", [(2 * a + y, 2 * b + y) for a, b in moves for y in range(2)])

    ints = jnp.int32
    owners = block_owner.reshape(requests)
    positions = jnp.arange(requests, dtype=ints)
    earlier = (owners[:, None] == owners[None, :]) & (positions[None, :] < positions[:, None])
    rank = jnp.sum(earlier.astype(ints), axis=1)
    peer_ids = me ^ jnp.arange(peers, dtype=ints)
    send_ranks = side * quarter + jnp.arange(quarter, dtype=ints)
    match = (owners[None, None, :] == peer_ids[:, None, None]) & (
        rank[None, None, :] == send_ranks[None, :, None]
    )
    source = jnp.sum(jnp.where(match, positions[None, None, :], 0), axis=2)
    aligned = -(-band_rows // 16) * 16
    listed = splat_weight.reshape(requests, band_rows, BLOCK)
    packed = pack_weights(source.reshape(peers * quarter), listed, peers, aligned)

    view_of = positions // visible
    start = view_of * padded + block_row.reshape(requests) * GRID
    told = jnp.stack([owners, rank, block_local.reshape(requests), start])
    heard = told[None]
    for k in (4, 2, 1):
        heard = jnp.concatenate([heard, swap(heard, "view", k)], axis=0)
    heard = heard.reshape((2, 2, 2) + told.shape).transpose(2, 1, 0, 3, 4).reshape((peers,) + told.shape)
    slot_ids = jnp.arange(slots, dtype=ints)

    def asked_of(owner, told):
        asked = (told[:, None, 0, :] == owner) & (told[:, None, 1, :] == slot_ids[None, :, None])
        filled = jnp.any(asked, axis=2)
        block = jnp.sum(jnp.where(asked, told[:, None, 2, :], 0), axis=2)
        place = jnp.sum(jnp.where(asked, told[:, None, 3, :], 0), axis=2)
        place = jnp.where(filled, place, view_count * padded)
        return jnp.sum(filled.astype(ints), axis=1), block, jnp.where(filled, block, blocks), place

    counts, block_of, pull_of, place_of = asked_of(me, heard)
    pair_counts, _, _, pair_places = asked_of(me ^ 1, heard[::2])
    turn = (slot_ids // quarter) ^ side
    turn = (turn % 2) * 2 + turn // 2
    where_of = turn * quarter + slot_ids % quarter

    weights, kept, given, arrived = {}, {}, {}, {}
    hops = []
    for j in (3, 2, 1, 0):
        got = []
        for k in (2 * j + 1, 2 * j):
            value = packed[k]
            got.append(swap(value, "view", k) if k else value)
        got = jnp.stack(got[::-1])
        if j >= 2:
            hops.append(got)
        else:
            got = after(got, given[3])
        got = jnp.concatenate([got, swap(got, "feat", 2)], axis=1)
        weights[j] = jnp.concatenate([got, swap(got, "feat", 1)], axis=1)
        k = 2 * j + 1
        given[j] = spread(counts[k : k + 1], block_of[k], where_of, weights[j][1], points)
        arrived[j] = given[j]
    arrived[3] = after(swap(given[3], "view", 1), given[2], weights[1], weights[0])
    for j in (3, 2, 1, 0):
        if j < 3:
            arrived[j] = swap(after(given[j], arrived[j + 1]), "view", 1)
        k = 2 * j
        kept[j] = render(
            counts[k : k + 1], block_of[k], place_of[k], where_of, pair_counts[j : j + 1], pair_places[j],
            weights[j][0], points, arrived[j], view_count, half_rows,
        )

    side_id = side.reshape(1).astype(ints)
    teacher = after(teacher.transpose(1, 0, 2), weights[0])
    target = turn_teacher(side_id, teacher, sides, padded)
    target = jnp.stack([swap(target[d], "feat", d) if d else target[d] for d in range(sides)])
    head_weight = after(head_weight, weights[0])
    head = jnp.concatenate([head_weight, swap(head_weight, "feat", 2)], axis=0)
    head = jnp.concatenate([head, swap(head, "feat", 1)], axis=0)

    far = along(kept[3], [(0, 1), (3, 2)])
    mid = total(kept[2], far)
    inward = along(mid, [(0, 1), (3, 2)])
    between = along(mid, [(1, 2), (2, 1)])
    near = along(total(kept[1], between), [(0, 1), (1, 0), (2, 3), (3, 2)])
    centre = along(total(kept[3], inward), [(1, 2), (2, 1)])

    parts = deal(side_id, (kept[0], near, centre), sides, half_rows)
    parts = [[swap(of[d], "feat", d) if d else of[d] for d in (0, 2, 1, 3)] for of in parts]
    back, grad = [], None
    for u in range(view_count):
        images, grad = loss(u, side_id, parts[u], head, target, grad)
        images = [swap(image, "feat", d) if d else image for d, image in zip((0, 2, 1, 3), images)]
        back.append([images[i] for i in (0, 2, 1, 3)])
    own = gather(side_id, back, half_rows)

    middle = (line == 1) | (line == 2)
    near = along(own, [(0, 1), (1, 0), (2, 3), (3, 2)])
    centre = along(own, [(1, 2), (2, 1)])
    out_near = along(centre, [(1, 0), (2, 3)])
    cross = along(near, [(1, 2), (2, 1)])
    out_far = along(cross, [(1, 0), (2, 3)])
    chunks = [own, near, jnp.where(middle, cross, out_near), jnp.where(middle, centre, out_far)]
    jobs, marks, bands, sums = {}, [], None, None
    for j in range(4):
        if j >= 2:
            ready = [jobs[k] for k in ((0, 1, 2), (3, 4))[j - 2]]
            sums = pull(ready, after(where_of, picked), sums, blocks, half_rows, False)
            if j == 3:
                chunks[j] = after(chunks[j], sums)
        picked = pick(pair_counts[j : j + 1], pair_places[j], chunks[j], slots, aligned, half_rows)
        marks.append(picked)
        bands = swap(picked if bands is None else after(picked, bands), "view", 1)
        own, other = 2 * j, 2 * j + 1
        jobs[own] = dict(
            count=counts[own : own + 1], block=pull_of[own], place=place_of[own],
            weights=weights[j][0], images=chunks[j], width=width,
        )
        jobs[other] = dict(
            count=counts[other : other + 1], block=pull_of[other],
            weights=weights[j][1], bands=bands, width=width,
        )
    sums = pull([jobs[5], jobs[6]], after(where_of, picked), sums, blocks, half_rows, False)
    grad_points = pull([jobs[7]], where_of, sums, blocks, half_rows, True)

    grad = after(grad, chunks[0]).reshape(2, 2, width, grad.shape[1])
    grad = grad[0] + swap(grad[1], "feat", 1)
    grad = grad[0] + after(swap(grad[1], "feat", 2), near)
    rows = width // 2
    low = me % 2
    mine = lax.dynamic_slice_in_dim(grad, low * rows, rows, 0)
    other = lax.dynamic_slice_in_dim(grad, (1 - low) * rows, rows, 0)
    grad = mine + after(swap(other, "view", 1), marks[2])
    sent = grad.astype(jnp.bfloat16)
    grad = grad + after(swap(sent, "view", 2), marks[3]).astype(jnp.float32)
    sent = grad.astype(jnp.bfloat16)
    grad = grad + after(swap(sent, "view", 4), sums).astype(jnp.float32)
    grad = grad / (view_count * peers * GRID)
    far = swap(grad.astype(jnp.bfloat16), "view", 1).astype(jnp.float32)
    grad = in_order((low, grad), far)
    return (grad_points, grad)


def solution(mesh):
    size = mesh.shape
    paired = size["view"] == 8 and size["feat"] == 4
    placed = (
        P("view", "feat", None),
        P("feat", None),
        P("feat", "view", None),
        P("view", None, None, None),
        P("view", None, None),
        P("view", None),
        P("view", None),
    )
    return jax.shard_map(
        per_device if paired else per_device_listed,
        mesh=mesh,
        in_specs=placed,
        out_specs=(P("view", "feat", None), P("feat", None)),
        check_vma=False,
    )
```

```python
import jax
import jax.numpy as jnp
from jax import lax
from jax.experimental import pallas as pl
from jax.experimental.pallas import tpu as pltpu
from jax.sharding import PartitionSpec as P

GRID = 37
BAND = 2
BLOCK = 128
GROUP = 4


def slot_plan(owners, peer_count, capacity):
    total_requests = owners.shape[0]
    positions = jnp.arange(total_requests, dtype=jnp.int32)
    earlier = (owners[:, None] == owners[None, :]) & (positions[None, :] < positions[:, None])
    slot_rank = jnp.sum(earlier.astype(jnp.int32), axis=1)
    target = owners * capacity + slot_rank
    slot_ids = jnp.arange(peer_count * capacity, dtype=jnp.int32)
    matches = target[None, :] == slot_ids[:, None]
    source = jnp.sum(jnp.where(matches, positions[None, :], 0), axis=1)
    filled = jnp.any(matches, axis=1)
    return (target, source, filled)


def per_device_listed(points, head_weight, teacher, splat_weight, block_owner, block_local, block_row):
    peer_count = lax.axis_size("view")
    local_width = points.shape[1]
    view_count = splat_weight.shape[0]
    visible = splat_weight.shape[1]
    requests = view_count * visible
    capacity = max(3, (3 * requests + 2 * peer_count - 1) // (2 * peer_count))
    owners = block_owner.reshape(requests)
    local_ids = block_local.reshape(requests)
    target, source, filled = slot_plan(owners, peer_count, capacity)
    wanted = jnp.where(filled, jnp.take(local_ids, source), 0)
    columns = jnp.arange(GRID, dtype=jnp.int32)
    row_masks = [
        (block_row[:, :, None] + offset == columns[None, None, :]).astype(jnp.bfloat16)
        for offset in range(BAND)
    ]
    empty_bf = jnp.zeros((), jnp.bfloat16)
    asked_ids = lax.all_to_all(wanted, "view", split_axis=0, concat_axis=0, tiled=True)
    sent_rows = jnp.take(points, asked_ids, axis=0)
    arrived = lax.all_to_all(sent_rows, "view", split_axis=0, concat_axis=0, tiled=True)
    fetched = jnp.take(arrived, target, axis=0).reshape(view_count, visible, local_width, BLOCK)
    contrib = jnp.einsum(
        "vjcp,vjdp->vjcd", splat_weight, fetched, preferred_element_type=jnp.float32
    ).astype(jnp.bfloat16)
    rendered = jnp.zeros((view_count, GRID, GRID, local_width), jnp.float32)
    for offset in range(BAND):
        band_part = contrib[:, :, offset * GRID : (offset + 1) * GRID, :]
        rendered = rendered + jnp.einsum(
            "vjr,vjcd->vrcd", row_masks[offset], band_part, preferred_element_type=jnp.float32
        )
    rendered_rows = rendered.astype(jnp.bfloat16).reshape(view_count * GRID * GRID, local_width)
    pixel_rows = rendered_rows.shape[0]
    teacher_width = head_weight.shape[1]
    local_teacher = teacher.shape[0]
    contract_first = (((0,), (1,)), ((), ()))
    head_full = lax.all_gather(head_weight, "feat", axis=0, tiled=True)
    head_cols = lax.dynamic_slice_in_dim(
        head_full, lax.axis_index("feat") * local_teacher, local_teacher, 1
    )
    head_part = head_cols
    projected = lax.dot_general(
        head_part,
        lax.all_gather(rendered_rows, "feat", axis=1, tiled=True),
        contract_first,
        preferred_element_type=jnp.float32,
    )
    square_sum = lax.psum(jnp.sum(projected * projected, axis=0), "feat")
    scale_rows = jnp.sqrt(square_sum / teacher_width + 1e-06)
    normed = projected / scale_rows[None, :]
    target_feat = teacher.reshape(local_teacher, pixel_rows).astype(jnp.float32)
    residual = normed - target_feat
    row_dot = lax.psum(jnp.sum(residual * normed, axis=0), "feat")
    grad_proj = (
        (residual - normed * (row_dot / teacher_width)[None, :]) / scale_rows[None, :]
    ).astype(jnp.bfloat16)
    shard_part = lax.all_gather(grad_proj, "feat", axis=0, tiled=True)
    head_part = head_weight
    grad_image = lax.dot_general(
        shard_part, head_part, contract_first, preferred_element_type=jnp.float32
    )
    column_part = lax.dot_general(
        rendered_rows, shard_part, contract_first, preferred_element_type=jnp.float32
    )
    grad_head = column_part
    grad_image, grad_head = (grad_image, grad_head)
    head_grad = lax.psum(grad_head, "view") / (view_count * peer_count * GRID)
    grad_image = grad_image.astype(jnp.bfloat16).reshape(view_count, GRID, GRID, local_width)
    pieces = [
        jnp.einsum("vjr,vrcd->vjcd", row_mask, grad_image, preferred_element_type=jnp.float32)
        for row_mask in row_masks
    ]
    grad_contrib = jnp.concatenate(pieces, axis=2).astype(jnp.bfloat16)
    grad_block = jnp.einsum(
        "vjcp,vjcd->vjdp", splat_weight, grad_contrib, preferred_element_type=jnp.float32
    ).astype(jnp.bfloat16)
    grad_block = grad_block.reshape(requests, local_width, BLOCK)
    packed = jnp.where(filled[:, None, None], jnp.take(grad_block, source, axis=0), empty_bf)
    landed = lax.all_to_all(packed, "view", split_axis=0, concat_axis=0, tiled=True)
    summed = jax.ops.segment_sum(
        landed.astype(jnp.float32), asked_ids, num_segments=points.shape[0]
    )
    grad_points = summed.astype(jnp.bfloat16)
    return (grad_points, head_grad)


def price(us):
    return pl.CostEstimate(flops=int(us * 1e9), bytes_accessed=int(us * 2e6), transcendentals=0)


def call(body, out_shape, args, n_scalars, us, name, scratch=(), mib=12):
    smem = pl.BlockSpec(memory_space=pltpu.SMEM)
    vmem = pl.BlockSpec(memory_space=pltpu.VMEM)
    many = isinstance(out_shape, list)
    return pl.pallas_call(
        body,
        out_shape=out_shape,
        in_specs=[smem] * n_scalars + [vmem] * (len(args) - n_scalars),
        out_specs=[vmem] * len(out_shape) if many else vmem,
        scratch_shapes=list(scratch),
        compiler_params=pltpu.CompilerParams(vmem_limit_bytes=mib * 1024 * 1024),
        cost_estimate=price(us),
        name=name,
    )(*args)


def pack_weights(source, listed, peers, aligned):
    quarter = source.shape[0] // peers
    band_rows = listed.shape[1]
    tail = aligned - 16

    def body(source_ref, listed_ref, *outs):
        for k in range(peers):
            for i in range(quarter):
                outs[k][i, tail:aligned, :] = jnp.zeros((16, BLOCK), jnp.bfloat16)
                outs[k][i, 0:band_rows, :] = listed_ref[source_ref[k * quarter + i]]

    out = jax.ShapeDtypeStruct((quarter, aligned, BLOCK), jnp.bfloat16)
    return call(body, [out] * peers, (source, listed), 1, 3, "pack_weights")


def shifted(rows, start):
    rows = rows.astype(jnp.float32)
    rows = jnp.concatenate([rows, jnp.zeros((8, rows.shape[1]), jnp.float32)], axis=0)
    return pltpu.roll(rows, lax.rem(start, 8), 0)


def rows_at(start, band_rows):
    return pl.ds(pl.multiple_of((start // 8) * 8, 8), band_rows + 8)


def beside(first, second):
    lane = lax.broadcasted_iota(jnp.int32, (first.shape[0], 128), 1)
    second = pltpu.roll(second, 64, 1)
    middle = jnp.where(lane < 64, first[:, 128:256], second[:, 0:128])
    return jnp.concatenate([first[:, 0:128], middle, second[:, 128:256]], axis=1)


def apart(packed):
    return packed[:, 0:256], pltpu.roll(packed[:, 128:384], 192, 1)


def rounds(count, group):
    return (count + group - 1) // group


def spread(count, block, where, weight, points):
    slots, band_rows = weight.shape[:2]
    width = points.shape[1]

    def body(count_ref, block_ref, where_ref, weight_ref, points_ref, out_ref):
        blank = jnp.zeros((width, BLOCK), jnp.bfloat16)

        def group(step, carry):
            for t in range(2):
                pair = 2 * step + t
                one, two = 2 * pair, 2 * pair + 1
                weights = jnp.concatenate(
                    [weight_ref[where_ref[one]], weight_ref[where_ref[two]]], axis=1
                )
                blocks = jnp.concatenate(
                    [
                        jnp.concatenate([points_ref[block_ref[one]], blank], axis=1),
                        jnp.concatenate([blank, points_ref[block_ref[two]]], axis=1),
                    ],
                    axis=0,
                )
                out_ref[pair] = lax.dot_general(
                    weights, blocks, (((1,), (1,)), ((), ())), preferred_element_type=jnp.float32
                ).astype(jnp.bfloat16)
            return carry

        lax.fori_loop(0, rounds(count_ref[0], 4), group, 0)

    out = jax.ShapeDtypeStruct((slots // 2, band_rows, 2 * width), jnp.bfloat16)
    return call(body, out, (count, block, where, weight, points), 3, 0.1, "spread_blocks")


def render(count, block, place, where, other_count, other_place, weight, points, other, views, half_rows):
    width = points.shape[1]
    band_rows = weight.shape[1]

    def body(
        count_ref, block_ref, place_ref, where_ref, other_count_ref, other_place_ref,
        weight_ref, points_ref, other_ref, *rest
    ):
        out, acc = rest
        acc[...] = jnp.zeros_like(acc)

        def group(step, carry):
            parts = []
            for t in range(GROUP):
                slot = step * GROUP + t
                parts.append(
                    lax.dot_general(
                        shifted(weight_ref[where_ref[slot]], place_ref[slot]).astype(jnp.bfloat16),
                        points_ref[block_ref[slot]],
                        (((1,), (1,)), ((), ())),
                        preferred_element_type=jnp.float32,
                    )
                )
            for t in range(GROUP):
                acc[rows_at(place_ref[step * GROUP + t], band_rows), 0:width] += parts[t]
            return carry

        def other_group(step, carry):
            for t in range(2):
                pair = 2 * step + t
                for value, slot in zip(apart(other_ref[pair].astype(jnp.float32)), (2 * pair, 2 * pair + 1)):
                    start = other_place_ref[slot]
                    acc[rows_at(start, band_rows), :] += shifted(value, start)
            return carry

        lax.fori_loop(0, rounds(count_ref[0], GROUP), group, 0)
        lax.fori_loop(0, rounds(other_count_ref[0], 4), other_group, 0)
        for u in range(views):
            first = acc[2 * u * half_rows : (2 * u + 1) * half_rows, :]
            second = acc[(2 * u + 1) * half_rows : (2 * u + 2) * half_rows, :]
            out[u * half_rows : (u + 1) * half_rows, :] = beside(first, second).astype(out.dtype)

    images = jax.ShapeDtypeStruct((views * half_rows, 2 * width), jnp.bfloat16)
    args = (count, block, place, where, other_count, other_place, weight, points, other)
    scratch = [pltpu.VMEM((2 * views * half_rows + band_rows + 8, 256), jnp.float32)]
    return call(body, images, args, 6, 5, "render_blocks", scratch)


def unpack_images(image_refs, image, half_rows):
    views = [
        ref[i * half_rows : (i + 1) * half_rows, :]
        for ref in image_refs
        for i in range(ref.shape[0] // half_rows)
    ]
    for u, view in enumerate(views):
        first, second = apart(view.astype(jnp.float32))
        image[2 * u * half_rows : (2 * u + 1) * half_rows, :] = first
        image[(2 * u + 1) * half_rows : (2 * u + 2) * half_rows, :] = second


def pick(count, place, images, slots, band_rows, half_rows):
    pixels, packed = 2 * sum(part.shape[0] for part in images), images[0].shape[1]

    def body(count_ref, place_ref, *rest):
        image_refs, (out_ref, image) = rest[:-2], rest[-2:]
        unpack_images(image_refs, image, half_rows)
        image[pixels:, :] = jnp.zeros((band_rows + 8, 256), jnp.float32)

        def group(step, carry):
            for t in range(2):
                pair = 2 * step + t
                bands = []
                for slot in (2 * pair, 2 * pair + 1):
                    start = place_ref[slot]
                    rows = image[rows_at(start, band_rows), :]
                    back = lax.rem(band_rows + 8 - lax.rem(start, 8), band_rows + 8)
                    bands.append(pltpu.roll(rows, back, 0)[0:band_rows])
                out_ref[pair] = beside(*bands).astype(out_ref.dtype)
            return carry

        lax.fori_loop(0, rounds(count_ref[0], 4), group, 0)

    out = jax.ShapeDtypeStruct((slots // 2, band_rows, packed), jnp.bfloat16)
    scratch = [pltpu.VMEM((pixels + band_rows + 8, 256), jnp.float32)]
    return call(body, out, (count, place) + tuple(images), 2, 1, "pick_bands", scratch)


def pull(jobs, where, old, blocks, half_rows, last):
    band_rows = jobs[0]["weights"].shape[1]
    pixels = max([2 * sum(part.shape[0] for part in job.get("images", ())) for job in jobs])
    width = jobs[0]["width"]
    first = old is None
    tables, arrays, layout = [where], [], []
    for job in jobs:
        layout.append((len(tables), len(arrays), len(job.get("images", ()))))
        tables += [job["count"], job["block"]] + ([job["place"]] if "place" in job else [])
        arrays += [job["weights"]] + (list(job["images"]) if "place" in job else [job["bands"]])
    arrays += [] if first else [old]

    def body(*refs):
        where_ref = refs[0]
        array_refs = refs[len(tables) : len(tables) + len(arrays)]
        out_ref, image, *rest = refs[len(tables) + len(arrays) :]
        acc = rest[0] if last else out_ref
        acc[...] = jnp.zeros_like(acc) if first else array_refs[-1][...]

        for table, array, own in layout:
            count_ref, block_ref, weight_ref = refs[table], refs[table + 1], array_refs[array]
            place_ref, other_ref = refs[table + 2], array_refs[array + 1]
            if own:
                unpack_images(array_refs[array + 1 : array + 1 + own], image, half_rows)

            def group(step, carry):
                terms = []
                for t in range(GROUP):
                    slot = step * GROUP + t
                    start = place_ref[slot]
                    terms.append(
                        lax.dot_general(
                            image[rows_at(start, band_rows), 0:width].astype(jnp.bfloat16),
                            shifted(weight_ref[where_ref[slot]], start).astype(jnp.bfloat16),
                            (((0,), (0,)), ((), ())),
                            preferred_element_type=jnp.float32,
                        )
                    )
                for t in range(GROUP):
                    acc[block_ref[step * GROUP + t]] += terms[t]
                return carry

            def other_group(step, carry):
                terms = []
                for t in range(2):
                    pair = 2 * step + t
                    both = [weight_ref[where_ref[2 * pair + s]] for s in range(2)]
                    terms.append(
                        lax.dot_general(
                            other_ref[pair],
                            jnp.concatenate(both, axis=1),
                            (((0,), (0,)), ((), ())),
                            preferred_element_type=jnp.float32,
                        )
                    )
                for t in range(2):
                    pair = 2 * step + t
                    acc[block_ref[2 * pair]] += terms[t][0:width, 0:BLOCK]
                    acc[block_ref[2 * pair + 1]] += terms[t][width:, BLOCK:]
                return carry

            lax.fori_loop(0, rounds(count_ref[0], GROUP), group if own else other_group, 0)
        if last:
            out_ref[...] = acc[0:blocks].astype(out_ref.dtype)

    sums = (blocks + 1, width, BLOCK)
    out = jax.ShapeDtypeStruct((blocks, width, BLOCK), jnp.bfloat16)
    out = out if last else jax.ShapeDtypeStruct(sums, jnp.float32)
    scratch = [pltpu.VMEM((pixels + band_rows + 8, 256), jnp.float32)]
    scratch += [pltpu.VMEM(sums, jnp.float32)] if last else []
    us = 1
    return call(body, out, tuple(tables + arrays), len(tables), us, "pull_blocks", scratch, 24)


def loss_kernel(u, teacher_width, side_ref, head_ref, teacher_ref, *rest):
    parts_refs, image_refs, grad_ref = rest[0:4], rest[-5:-1], rest[-1]
    rows, packed = parts_refs[0].shape
    width = packed // 2
    lane = lax.broadcasted_iota(jnp.int32, (rows, packed), 1)
    head = head_ref[...]

    def halves_of(parts):
        halves = [[], []]
        for pair in range(2):
            one, two = (part.astype(jnp.float32) for part in parts[2 * pair : 2 * pair + 2])
            halves[0].append(jnp.where(lane < width, one, pltpu.roll(two, width, 1)))
            halves[1].append(jnp.where(lane < width, pltpu.roll(one, width, 1), two))
        return [jnp.concatenate(half, axis=1) for half in halves]

    halves = halves_of([ref[...] for ref in parts_refs])
    targets = halves_of([teacher_ref[side_ref[0] ^ g, u] for g in range(4)])
    rendered_all, grad_all, images = [], [], []
    for half in range(2):
        rendered = halves[half].astype(jnp.bfloat16)
        projected = jnp.dot(rendered, head, preferred_element_type=jnp.float32)
        square = jnp.sum(projected * projected, axis=1, keepdims=True)
        scale = jnp.sqrt(square / teacher_width + 1e-06)
        normed = projected / scale
        residual = normed - targets[half]
        inner = jnp.sum(residual * normed, axis=1, keepdims=True) / teacher_width
        grad_proj = ((residual - normed * inner) / scale).astype(jnp.bfloat16)
        images.append(
            lax.dot_general(grad_proj, head, (((1,), (1,)), ((), ())), preferred_element_type=jnp.float32)
        )
        rendered_all.append(rendered)
        grad_all.append(grad_proj)
    for pair in range(2):
        cols = slice(2 * pair * width, 2 * (pair + 1) * width)
        first, second = images[0][:, cols], images[1][:, cols]
        one = jnp.where(lane < width, first, pltpu.roll(second, width, 1))
        two = jnp.where(lane < width, pltpu.roll(first, width, 1), second)
        image_refs[2 * pair][...] = one.astype(jnp.bfloat16)
        image_refs[2 * pair + 1][...] = two.astype(jnp.bfloat16)
    grad = lax.dot_general(
        jnp.concatenate(rendered_all, axis=0),
        jnp.concatenate(grad_all, axis=0),
        (((0,), (0,)), ((), ())),
        preferred_element_type=jnp.float32,
    )
    grad_ref[...] = grad if len(rest) == 9 else grad + rest[4][...]


def loss(u, side, parts, head, teacher, grad):
    teacher_width = head.shape[1]
    outs = [jax.ShapeDtypeStruct(parts[0].shape, jnp.bfloat16)] * len(parts)
    outs += [jax.ShapeDtypeStruct(head.shape, jnp.float32)]
    body = lambda *refs: loss_kernel(u, teacher_width, *refs)
    args = (side, head, teacher) + tuple(parts) + (() if grad is None else (grad,))
    *images, grad = call(body, outs, args, 1, 3, "loss_rows", (), 20)
    return images, grad


def deal(side, terms, starts, sides, half_rows):
    rows = half_rows // sides

    def body(side_ref, *refs):
        for d in range(sides):
            here = (side_ref[0] ^ d) * rows
            value = 0.0
            for ref, start in zip(refs, starts):
                value = value + ref[pl.ds(pl.multiple_of(start + here, 16), rows), :].astype(jnp.float32)
            refs[len(terms) + d][...] = value.astype(jnp.bfloat16)

    out = jax.ShapeDtypeStruct((rows, terms[0].shape[1]), jnp.bfloat16)
    return call(body, [out] * sides, (side,) + tuple(terms), 1, 1, "deal_rows")


def gather(side, parts):
    rows, lanes = parts[0].shape

    def body(side_ref, *refs):
        for d in range(len(parts)):
            here = pl.ds(pl.multiple_of((side_ref[0] ^ d) * rows, 16), rows)
            refs[-1][here, :] = refs[d][...]

    out = jax.ShapeDtypeStruct((rows * len(parts), lanes), jnp.bfloat16)
    return call(body, out, (side,) + tuple(parts), 1, 1, "gather_rows")


def turn_teacher(side, teacher, sides, padded):
    views, width, pixels = teacher.shape
    half_rows = padded // 2
    rows = half_rows // sides
    whole = pixels // 128 * 128

    def body(side_ref, teacher_ref, *rest):
        outs, (across, turned) = rest[:sides], rest[sides:]
        for u in range(views):
            across[width:, :] = jnp.zeros((256 - width, padded), jnp.float32)
            across[0:width, whole:] = jnp.zeros((width, padded - whole), jnp.float32)
            across[0:width, 0:pixels] = teacher_ref[u].astype(jnp.float32)
            turned[...] = across[...].T
            for d in range(sides):
                start = pl.multiple_of((side_ref[0] ^ d) * rows, 16)
                first = turned[pl.ds(start, rows), :]
                second = turned[pl.ds(half_rows + start, rows), :]
                outs[d][u] = beside(first, second).astype(jnp.bfloat16)

    out = jax.ShapeDtypeStruct((views, rows, 2 * width), jnp.bfloat16)
    scratch = [pltpu.VMEM((256, padded), jnp.float32), pltpu.VMEM((padded, 256), jnp.float32)]
    return call(body, [out] * sides, (side, teacher), 1, 6, "turn_teacher", scratch)


def after(value, *earlier):
    return lax.optimization_barrier((value,) + earlier)[0]


def total(*terms):
    acc = terms[0].astype(jnp.float32)
    for term in terms[1:]:
        acc = acc + term.astype(jnp.float32)
    return acc.astype(jnp.bfloat16)


def in_order(own_first, other):
    index, mine = own_first
    return jnp.where(
        index == 0, jnp.concatenate([mine, other], 0), jnp.concatenate([other, mine], 0)
    )


def per_device(points, head_weight, teacher, splat_weight, block_owner, block_local, block_row):
    peers, sides = lax.axis_size("view"), lax.axis_size("feat")
    blocks, width = points.shape[0], points.shape[1]
    view_count, visible, band_rows = splat_weight.shape[:3]
    requests = view_count * visible
    capacity = max(3, (3 * requests + 2 * peers - 1) // (2 * peers))
    quarter = -(-capacity // sides)
    slots = quarter * sides
    pixels = teacher.shape[2]
    unit = 2 * sides * 16
    padded = -(-pixels // unit) * unit
    half_rows = padded // 2
    me, side = lax.axis_index("view"), lax.axis_index("feat")
    line, across, core = me // 2, side // 2, side % 2

    def hop(value, axis, pairs):
        return lax.ppermute(value, axis, pairs)

    def swap(value, axis, k):
        size = peers if axis == "view" else sides
        return hop(value, axis, [(i, i ^ k) for i in range(size)])

    def along(value, moves):
        return hop(value, "view", [(2 * a + y, 2 * b + y) for a, b in moves for y in range(2)])

    ints = jnp.int32
    owners = block_owner.reshape(requests)
    positions = jnp.arange(requests, dtype=ints)
    earlier = (owners[:, None] == owners[None, :]) & (positions[None, :] < positions[:, None])
    rank = jnp.sum(earlier.astype(ints), axis=1)
    peer_ids = me ^ jnp.arange(peers, dtype=ints)
    send_ranks = side * quarter + jnp.arange(quarter, dtype=ints)
    match = (owners[None, None, :] == peer_ids[:, None, None]) & (
        rank[None, None, :] == send_ranks[None, :, None]
    )
    source = jnp.sum(jnp.where(match, positions[None, None, :], 0), axis=2)
    aligned = -(-band_rows // 16) * 16
    listed = splat_weight.reshape(requests, band_rows, BLOCK)
    packed = pack_weights(source.reshape(peers * quarter), listed, peers, aligned)

    view_of = positions // visible
    start = view_of * padded + block_row.reshape(requests) * GRID
    told = jnp.stack([owners, rank, block_local.reshape(requests), start])
    heard = told[None]
    for k in (4, 2, 1):
        heard = jnp.concatenate([heard, swap(heard, "view", k)], axis=0)
    heard = heard.reshape((2, 2, 2) + told.shape).transpose(2, 1, 0, 3, 4).reshape((peers,) + told.shape)
    slot_ids = jnp.arange(slots, dtype=ints)

    def asked_of(owner, told):
        asked = (told[:, None, 0, :] == owner) & (told[:, None, 1, :] == slot_ids[None, :, None])
        filled = jnp.any(asked, axis=2)
        block = jnp.sum(jnp.where(asked, told[:, None, 2, :], 0), axis=2)
        place = jnp.sum(jnp.where(asked, told[:, None, 3, :], 0), axis=2)
        place = jnp.where(filled, place, view_count * padded)
        return jnp.sum(filled.astype(ints), axis=1), block, jnp.where(filled, block, blocks), place

    counts, block_of, pull_of, place_of = asked_of(me, heard)
    pair_counts, _, _, pair_places = asked_of(me ^ 1, heard[::2])
    turn = (slot_ids // quarter) ^ side
    turn = (turn % 2) * 2 + turn // 2
    where_of = turn * quarter + slot_ids % quarter

    weights, kept, given, arrived = {}, {}, {}, {}
    hops = []
    for j in (3, 2, 1, 0):
        got = []
        for k in (2 * j + 1, 2 * j):
            value = packed[k]
            got.append(swap(value, "view", k) if k else value)
        got = jnp.stack(got[::-1])
        if j >= 2:
            hops.append(got)
        else:
            got = after(got, given[3])
        got = jnp.concatenate([got, swap(got, "feat", 2)], axis=1)
        weights[j] = jnp.concatenate([got, swap(got, "feat", 1)], axis=1)
        k = 2 * j + 1
        given[j] = spread(counts[k : k + 1], block_of[k], where_of, weights[j][1], points)
        arrived[j] = given[j]
    arrived[3] = after(swap(given[3], "view", 1), given[2], weights[1], weights[0])
    for j in (3, 2, 1, 0):
        if j < 3:
            arrived[j] = swap(after(given[j], arrived[j + 1]), "view", 1)
        k = 2 * j
        kept[j] = render(
            counts[k : k + 1], block_of[k], place_of[k], where_of, pair_counts[j : j + 1], pair_places[j],
            weights[j][0], points, arrived[j], view_count, half_rows,
        )

    side_id = side.reshape(1).astype(ints)
    teacher = after(teacher.transpose(1, 0, 2), weights[0])
    target = turn_teacher(side_id, teacher, sides, padded)
    target = jnp.stack([swap(target[d], "feat", d) if d else target[d] for d in range(sides)])
    head_weight = after(head_weight, weights[0])
    head = jnp.concatenate([head_weight, swap(head_weight, "feat", 2)], axis=0)
    head = jnp.concatenate([head, swap(head, "feat", 1)], axis=0)

    far = along(kept[3], [(0, 1), (3, 2)])
    mid = total(kept[2], far)
    inward = along(mid, [(0, 1), (3, 2)])
    between = along(mid, [(1, 2), (2, 1)])
    back, grad, held = [], None, None
    for u in range(view_count):
        here = slice(u * half_rows, (u + 1) * half_rows)
        near = along(total(kept[1][here], between[here]), [(0, 1), (1, 0), (2, 3), (3, 2)])
        centre = along(total(kept[3][here], inward[here]), [(1, 2), (2, 1)])
        terms = (kept[0], near, centre)
        back.append(terms)
    middle = (line == 1) | (line == 2)
    images, nears, centres = [], [], []
    for u in range(view_count):
        terms = back[u]
        parts = deal(side_id, terms, (u * half_rows, 0, 0), sides, half_rows)
        parts = [swap(parts[d], "feat", d) if d else parts[d] for d in (0, 2, 1, 3)]
        if u:
            parts = after(parts, images[-1])
        parts, grad = loss(u, side_id, parts, head, target, grad)
        held = parts[0]
        parts = [swap(part, "feat", d) if d else part for d, part in zip((0, 2, 1, 3), parts)]
        parts = [parts[i] for i in (0, 2, 1, 3)]
        if u:
            parts = after(parts, nears[-1], centres[-1])
        images.append(gather(side_id, parts))
        nears.append(along(images[u], [(0, 1), (1, 0), (2, 3), (3, 2)]))
        centres.append(along(images[u], [(1, 2), (2, 1)]))
    near, centre = jnp.concatenate(nears, axis=0), jnp.concatenate(centres, axis=0)
    out_near = along(centre, [(1, 0), (2, 3)])
    cross = along(near, [(1, 2), (2, 1)])
    out_far = along(cross, [(1, 0), (2, 3)])
    chunks = [images, nears, [jnp.where(middle, cross, out_near)], [jnp.where(middle, centre, out_far)]]
    jobs, marks, bands, sums = {}, [], None, None
    for j in range(4):
        if j >= 2:
            ready = [jobs[k] for k in ((0, 1, 2), (3, 4))[j - 2]]
            sums = pull(ready, after(where_of, picked), sums, blocks, half_rows, False)
            if j == 3:
                chunks[j] = after(chunks[j], sums)
        picked = pick(pair_counts[j : j + 1], pair_places[j], chunks[j], slots, aligned, half_rows)
        marks.append(picked)
        bands = swap(picked if bands is None else after(picked, bands), "view", 1)
        own, other = 2 * j, 2 * j + 1
        jobs[own] = dict(
            count=counts[own : own + 1], block=pull_of[own], place=place_of[own],
            weights=weights[j][0], images=chunks[j], width=width,
        )
        jobs[other] = dict(
            count=counts[other : other + 1], block=pull_of[other],
            weights=weights[j][1], bands=bands, width=width,
        )
    sums = pull([jobs[5], jobs[6]], after(where_of, picked), sums, blocks, half_rows, False)
    grad_points = pull([jobs[7]], where_of, sums, blocks, half_rows, True)

    grad = after(grad, chunks[0]).reshape(2, 2, width, grad.shape[1])
    grad = grad[0] + swap(grad[1], "feat", 1)
    grad = grad[0] + after(swap(grad[1], "feat", 2), near)
    rows = width // 2
    low = me % 2
    mine = lax.dynamic_slice_in_dim(grad, low * rows, rows, 0)
    other = lax.dynamic_slice_in_dim(grad, (1 - low) * rows, rows, 0)
    grad = mine + after(swap(other, "view", 1), marks[2])
    sent = grad.astype(jnp.bfloat16)
    grad = grad + after(swap(sent, "view", 2), marks[3]).astype(jnp.float32)
    sent = grad.astype(jnp.bfloat16)
    grad = grad + after(swap(sent, "view", 4), sums).astype(jnp.float32)
    grad = grad / (view_count * peers * GRID)
    far = swap(grad.astype(jnp.bfloat16), "view", 1).astype(jnp.float32)
    grad = in_order((low, grad), far)
    return (grad_points, grad)


def solution(mesh):
    size = mesh.shape
    paired = size["view"] == 8 and size["feat"] == 4
    placed = (
        P("view", "feat", None),
        P("feat", None),
        P("feat", "view", None),
        P("view", None, None, None),
        P("view", None, None),
        P("view", None),
        P("view", None),
    )
    return jax.shard_map(
        per_device if paired else per_device_listed,
        mesh=mesh,
        in_specs=placed,
        out_specs=(P("view", "feat", None), P("feat", None)),
        check_vma=False,
    )
```

```python
import jax
import jax.numpy as jnp
from jax import lax
from jax.experimental import pallas as pl
from jax.experimental.pallas import tpu as pltpu
from jax.sharding import PartitionSpec as P

GRID = 37
BAND = 2
BLOCK = 128
GROUP = 4


def slot_plan(owners, peer_count, capacity):
    total_requests = owners.shape[0]
    positions = jnp.arange(total_requests, dtype=jnp.int32)
    earlier = (owners[:, None] == owners[None, :]) & (positions[None, :] < positions[:, None])
    slot_rank = jnp.sum(earlier.astype(jnp.int32), axis=1)
    target = owners * capacity + slot_rank
    slot_ids = jnp.arange(peer_count * capacity, dtype=jnp.int32)
    matches = target[None, :] == slot_ids[:, None]
    source = jnp.sum(jnp.where(matches, positions[None, :], 0), axis=1)
    filled = jnp.any(matches, axis=1)
    return (target, source, filled)


def per_device_listed(points, head_weight, teacher, splat_weight, block_owner, block_local, block_row):
    peer_count = lax.axis_size("view")
    local_width = points.shape[1]
    view_count = splat_weight.shape[0]
    visible = splat_weight.shape[1]
    requests = view_count * visible
    capacity = max(3, (3 * requests + 2 * peer_count - 1) // (2 * peer_count))
    owners = block_owner.reshape(requests)
    local_ids = block_local.reshape(requests)
    target, source, filled = slot_plan(owners, peer_count, capacity)
    wanted = jnp.where(filled, jnp.take(local_ids, source), 0)
    columns = jnp.arange(GRID, dtype=jnp.int32)
    row_masks = [
        (block_row[:, :, None] + offset == columns[None, None, :]).astype(jnp.bfloat16)
        for offset in range(BAND)
    ]
    empty_bf = jnp.zeros((), jnp.bfloat16)
    asked_ids = lax.all_to_all(wanted, "view", split_axis=0, concat_axis=0, tiled=True)
    sent_rows = jnp.take(points, asked_ids, axis=0)
    arrived = lax.all_to_all(sent_rows, "view", split_axis=0, concat_axis=0, tiled=True)
    fetched = jnp.take(arrived, target, axis=0).reshape(view_count, visible, local_width, BLOCK)
    contrib = jnp.einsum(
        "vjcp,vjdp->vjcd", splat_weight, fetched, preferred_element_type=jnp.float32
    ).astype(jnp.bfloat16)
    rendered = jnp.zeros((view_count, GRID, GRID, local_width), jnp.float32)
    for offset in range(BAND):
        band_part = contrib[:, :, offset * GRID : (offset + 1) * GRID, :]
        rendered = rendered + jnp.einsum(
            "vjr,vjcd->vrcd", row_masks[offset], band_part, preferred_element_type=jnp.float32
        )
    rendered_rows = rendered.astype(jnp.bfloat16).reshape(view_count * GRID * GRID, local_width)
    pixel_rows = rendered_rows.shape[0]
    teacher_width = head_weight.shape[1]
    local_teacher = teacher.shape[0]
    contract_first = (((0,), (1,)), ((), ()))
    head_full = lax.all_gather(head_weight, "feat", axis=0, tiled=True)
    head_cols = lax.dynamic_slice_in_dim(
        head_full, lax.axis_index("feat") * local_teacher, local_teacher, 1
    )
    head_part = head_cols
    projected = lax.dot_general(
        head_part,
        lax.all_gather(rendered_rows, "feat", axis=1, tiled=True),
        contract_first,
        preferred_element_type=jnp.float32,
    )
    square_sum = lax.psum(jnp.sum(projected * projected, axis=0), "feat")
    scale_rows = jnp.sqrt(square_sum / teacher_width + 1e-06)
    normed = projected / scale_rows[None, :]
    target_feat = teacher.reshape(local_teacher, pixel_rows).astype(jnp.float32)
    residual = normed - target_feat
    row_dot = lax.psum(jnp.sum(residual * normed, axis=0), "feat")
    grad_proj = (
        (residual - normed * (row_dot / teacher_width)[None, :]) / scale_rows[None, :]
    ).astype(jnp.bfloat16)
    shard_part = lax.all_gather(grad_proj, "feat", axis=0, tiled=True)
    head_part = head_weight
    grad_image = lax.dot_general(
        shard_part, head_part, contract_first, preferred_element_type=jnp.float32
    )
    column_part = lax.dot_general(
        rendered_rows, shard_part, contract_first, preferred_element_type=jnp.float32
    )
    grad_head = column_part
    grad_image, grad_head = (grad_image, grad_head)
    head_grad = lax.psum(grad_head, "view") / (view_count * peer_count * GRID)
    grad_image = grad_image.astype(jnp.bfloat16).reshape(view_count, GRID, GRID, local_width)
    pieces = [
        jnp.einsum("vjr,vrcd->vjcd", row_mask, grad_image, preferred_element_type=jnp.float32)
        for row_mask in row_masks
    ]
    grad_contrib = jnp.concatenate(pieces, axis=2).astype(jnp.bfloat16)
    grad_block = jnp.einsum(
        "vjcp,vjcd->vjdp", splat_weight, grad_contrib, preferred_element_type=jnp.float32
    ).astype(jnp.bfloat16)
    grad_block = grad_block.reshape(requests, local_width, BLOCK)
    packed = jnp.where(filled[:, None, None], jnp.take(grad_block, source, axis=0), empty_bf)
    landed = lax.all_to_all(packed, "view", split_axis=0, concat_axis=0, tiled=True)
    summed = jax.ops.segment_sum(
        landed.astype(jnp.float32), asked_ids, num_segments=points.shape[0]
    )
    grad_points = summed.astype(jnp.bfloat16)
    return (grad_points, head_grad)


def price(us):
    return pl.CostEstimate(flops=int(us * 1e9), bytes_accessed=int(us * 2e6), transcendentals=0)


def call(body, out_shape, args, n_scalars, us, name, scratch=(), mib=12):
    smem = pl.BlockSpec(memory_space=pltpu.SMEM)
    vmem = pl.BlockSpec(memory_space=pltpu.VMEM)
    many = isinstance(out_shape, list)
    return pl.pallas_call(
        body,
        out_shape=out_shape,
        in_specs=[smem] * n_scalars + [vmem] * (len(args) - n_scalars),
        out_specs=[vmem] * len(out_shape) if many else vmem,
        scratch_shapes=list(scratch),
        compiler_params=pltpu.CompilerParams(vmem_limit_bytes=mib * 1024 * 1024),
        cost_estimate=price(us),
        name=name,
    )(*args)


def pack_weights(source, listed, peers, aligned):
    quarter = source.shape[0] // peers
    band_rows = listed.shape[1]
    tail = aligned - 16

    def body(source_ref, listed_ref, *outs):
        for k in range(peers):
            for i in range(quarter):
                outs[k][i, tail:aligned, :] = jnp.zeros((16, BLOCK), jnp.bfloat16)
                outs[k][i, 0:band_rows, :] = listed_ref[source_ref[k * quarter + i]]

    out = jax.ShapeDtypeStruct((quarter, aligned, BLOCK), jnp.bfloat16)
    return call(body, [out] * peers, (source, listed), 1, 3, "pack_weights")


def shifted(rows, start):
    rows = rows.astype(jnp.float32)
    rows = jnp.concatenate([rows, jnp.zeros((8, rows.shape[1]), jnp.float32)], axis=0)
    return pltpu.roll(rows, lax.rem(start, 8), 0)


def rows_at(start, band_rows):
    return pl.ds(pl.multiple_of((start // 8) * 8, 8), band_rows + 8)


def beside(first, second):
    lane = lax.broadcasted_iota(jnp.int32, (first.shape[0], 128), 1)
    second = pltpu.roll(second, 64, 1)
    middle = jnp.where(lane < 64, first[:, 128:256], second[:, 0:128])
    return jnp.concatenate([first[:, 0:128], middle, second[:, 128:256]], axis=1)


def apart(packed):
    return packed[:, 0:256], pltpu.roll(packed[:, 128:384], 192, 1)


def rounds(count, group):
    return (count + group - 1) // group


def spread(count, block, where, weight, points):
    slots, band_rows = weight.shape[:2]
    width = points.shape[1]

    def body(count_ref, block_ref, where_ref, weight_ref, points_ref, out_ref):
        blank = jnp.zeros((width, BLOCK), jnp.bfloat16)

        def group(step, carry):
            for t in range(2):
                pair = 2 * step + t
                one, two = 2 * pair, 2 * pair + 1
                weights = jnp.concatenate(
                    [weight_ref[where_ref[one]], weight_ref[where_ref[two]]], axis=1
                )
                blocks = jnp.concatenate(
                    [
                        jnp.concatenate([points_ref[block_ref[one]], blank], axis=1),
                        jnp.concatenate([blank, points_ref[block_ref[two]]], axis=1),
                    ],
                    axis=0,
                )
                out_ref[pair] = lax.dot_general(
                    weights, blocks, (((1,), (1,)), ((), ())), preferred_element_type=jnp.float32
                ).astype(jnp.bfloat16)
            return carry

        lax.fori_loop(0, rounds(count_ref[0], 4), group, 0)

    out = jax.ShapeDtypeStruct((slots // 2, band_rows, 2 * width), jnp.bfloat16)
    return call(body, out, (count, block, where, weight, points), 3, 0.1, "spread_blocks")


def render(count, block, place, where, other_count, other_place, weight, points, other, views, half_rows):
    width = points.shape[1]
    band_rows = weight.shape[1]

    def body(
        count_ref, block_ref, place_ref, where_ref, other_count_ref, other_place_ref,
        weight_ref, points_ref, other_ref, *rest
    ):
        out, acc = rest
        acc[...] = jnp.zeros_like(acc)

        def group(step, carry):
            parts = []
            for t in range(GROUP):
                slot = step * GROUP + t
                parts.append(
                    lax.dot_general(
                        shifted(weight_ref[where_ref[slot]], place_ref[slot]).astype(jnp.bfloat16),
                        points_ref[block_ref[slot]],
                        (((1,), (1,)), ((), ())),
                        preferred_element_type=jnp.float32,
                    )
                )
            for t in range(GROUP):
                acc[rows_at(place_ref[step * GROUP + t], band_rows), 0:width] += parts[t]
            return carry

        def other_group(step, carry):
            for t in range(2):
                pair = 2 * step + t
                for value, slot in zip(apart(other_ref[pair].astype(jnp.float32)), (2 * pair, 2 * pair + 1)):
                    start = other_place_ref[slot]
                    acc[rows_at(start, band_rows), :] += shifted(value, start)
            return carry

        lax.fori_loop(0, rounds(count_ref[0], GROUP), group, 0)
        lax.fori_loop(0, rounds(other_count_ref[0], 4), other_group, 0)
        for u in range(views):
            first = acc[2 * u * half_rows : (2 * u + 1) * half_rows, :]
            second = acc[(2 * u + 1) * half_rows : (2 * u + 2) * half_rows, :]
            out[u * half_rows : (u + 1) * half_rows, :] = beside(first, second).astype(out.dtype)

    images = jax.ShapeDtypeStruct((views * half_rows, 2 * width), jnp.bfloat16)
    args = (count, block, place, where, other_count, other_place, weight, points, other)
    scratch = [pltpu.VMEM((2 * views * half_rows + band_rows + 8, 256), jnp.float32)]
    return call(body, images, args, 6, 5, "render_blocks", scratch)


def unpack_images(image_refs, image, half_rows):
    views = [
        ref[i * half_rows : (i + 1) * half_rows, :]
        for ref in image_refs
        for i in range(ref.shape[0] // half_rows)
    ]
    for u, view in enumerate(views):
        first, second = apart(view.astype(jnp.float32))
        image[2 * u * half_rows : (2 * u + 1) * half_rows, :] = first
        image[(2 * u + 1) * half_rows : (2 * u + 2) * half_rows, :] = second


def pick(count, place, images, slots, band_rows, half_rows):
    pixels, packed = 2 * sum(part.shape[0] for part in images), images[0].shape[1]

    def body(count_ref, place_ref, *rest):
        image_refs, (out_ref, image) = rest[:-2], rest[-2:]
        unpack_images(image_refs, image, half_rows)
        image[pixels:, :] = jnp.zeros((band_rows + 8, 256), jnp.float32)

        def group(step, carry):
            for t in range(2):
                pair = 2 * step + t
                bands = []
                for slot in (2 * pair, 2 * pair + 1):
                    start = place_ref[slot]
                    rows = image[rows_at(start, band_rows), :]
                    back = lax.rem(band_rows + 8 - lax.rem(start, 8), band_rows + 8)
                    bands.append(pltpu.roll(rows, back, 0)[0:band_rows])
                out_ref[pair] = beside(*bands).astype(out_ref.dtype)
            return carry

        lax.fori_loop(0, rounds(count_ref[0], 4), group, 0)

    out = jax.ShapeDtypeStruct((slots // 2, band_rows, packed), jnp.bfloat16)
    scratch = [pltpu.VMEM((pixels + band_rows + 8, 256), jnp.float32)]
    return call(body, out, (count, place) + tuple(images), 2, 1, "pick_bands", scratch)


def pull(jobs, where, old, blocks, half_rows, last):
    band_rows = jobs[0]["weights"].shape[1]
    pixels = max([2 * sum(part.shape[0] for part in job.get("images", ())) for job in jobs])
    width = jobs[0]["width"]
    first = old is None
    tables, arrays, layout = [where], [], []
    for job in jobs:
        layout.append((len(tables), len(arrays), len(job.get("images", ()))))
        tables += [job["count"], job["block"]] + ([job["place"]] if "place" in job else [])
        arrays += [job["weights"]] + (list(job["images"]) if "place" in job else [job["bands"]])
    arrays += [] if first else [old]

    def body(*refs):
        where_ref = refs[0]
        array_refs = refs[len(tables) : len(tables) + len(arrays)]
        out_ref, image, *rest = refs[len(tables) + len(arrays) :]
        acc = rest[0] if last else out_ref
        acc[...] = jnp.zeros_like(acc) if first else array_refs[-1][...]

        for table, array, own in layout:
            count_ref, block_ref, weight_ref = refs[table], refs[table + 1], array_refs[array]
            place_ref, other_ref = refs[table + 2], array_refs[array + 1]
            if own:
                unpack_images(array_refs[array + 1 : array + 1 + own], image, half_rows)

            def group(step, carry):
                terms = []
                for t in range(GROUP):
                    slot = step * GROUP + t
                    start = place_ref[slot]
                    terms.append(
                        lax.dot_general(
                            image[rows_at(start, band_rows), 0:width].astype(jnp.bfloat16),
                            shifted(weight_ref[where_ref[slot]], start).astype(jnp.bfloat16),
                            (((0,), (0,)), ((), ())),
                            preferred_element_type=jnp.float32,
                        )
                    )
                for t in range(GROUP):
                    acc[block_ref[step * GROUP + t]] += terms[t]
                return carry

            def other_group(step, carry):
                terms = []
                for t in range(2):
                    pair = 2 * step + t
                    both = [weight_ref[where_ref[2 * pair + s]] for s in range(2)]
                    terms.append(
                        lax.dot_general(
                            other_ref[pair],
                            jnp.concatenate(both, axis=1),
                            (((0,), (0,)), ((), ())),
                            preferred_element_type=jnp.float32,
                        )
                    )
                for t in range(2):
                    pair = 2 * step + t
                    acc[block_ref[2 * pair]] += terms[t][0:width, 0:BLOCK]
                    acc[block_ref[2 * pair + 1]] += terms[t][width:, BLOCK:]
                return carry

            lax.fori_loop(0, rounds(count_ref[0], GROUP), group if own else other_group, 0)
        if last:
            out_ref[...] = acc[0:blocks].astype(out_ref.dtype)

    sums = (blocks + 1, width, BLOCK)
    out = jax.ShapeDtypeStruct((blocks, width, BLOCK), jnp.bfloat16)
    out = out if last else jax.ShapeDtypeStruct(sums, jnp.float32)
    scratch = [pltpu.VMEM((pixels + band_rows + 8, 256), jnp.float32)]
    scratch += [pltpu.VMEM(sums, jnp.float32)] if last else []
    us = 1
    return call(body, out, tuple(tables + arrays), len(tables), us, "pull_blocks", scratch, 24)


def loss_kernel(u, teacher_width, half_rows, side_ref, head_ref, teacher_ref, *rest):
    parts_refs, image_refs, grad_ref = rest[0:4], rest[-5:-1], rest[-1]
    rows, packed = parts_refs[0].shape
    width = packed // 2
    lane = lax.broadcasted_iota(jnp.int32, (rows, packed), 1)
    head = head_ref[...]

    def halves_of(parts):
        halves = [[], []]
        for pair in range(2):
            one, two = (part.astype(jnp.float32) for part in parts[2 * pair : 2 * pair + 2])
            halves[0].append(jnp.where(lane < width, one, pltpu.roll(two, width, 1)))
            halves[1].append(jnp.where(lane < width, pltpu.roll(one, width, 1), two))
        return [jnp.concatenate(half, axis=1) for half in halves]

    halves = halves_of([ref[...] for ref in parts_refs])
    targets = halves_of([teacher_ref[side_ref[0] ^ g, u] for g in range(4)])
    twice = side_ref[0] * rows - first_row(side_ref[0], half_rows, 4)
    counted = lax.broadcasted_iota(jnp.int32, (rows, 1), 0) >= twice
    rendered_all, grad_all, images = [], [], []
    for half in range(2):
        rendered = halves[half].astype(jnp.bfloat16)
        projected = jnp.dot(rendered, head, preferred_element_type=jnp.float32)
        square = jnp.sum(projected * projected, axis=1, keepdims=True)
        scale = jnp.sqrt(square / teacher_width + 1e-06)
        normed = projected / scale
        residual = normed - targets[half]
        inner = jnp.sum(residual * normed, axis=1, keepdims=True) / teacher_width
        grad_proj = ((residual - normed * inner) / scale).astype(jnp.bfloat16)
        images.append(
            lax.dot_general(grad_proj, head, (((1,), (1,)), ((), ())), preferred_element_type=jnp.float32)
        )
        rendered_all.append(jnp.where(counted, rendered, jnp.zeros_like(rendered)))
        grad_all.append(grad_proj)
    for pair in range(2):
        cols = slice(2 * pair * width, 2 * (pair + 1) * width)
        first, second = images[0][:, cols], images[1][:, cols]
        one = jnp.where(lane < width, first, pltpu.roll(second, width, 1))
        two = jnp.where(lane < width, pltpu.roll(first, width, 1), second)
        image_refs[2 * pair][...] = one.astype(jnp.bfloat16)
        image_refs[2 * pair + 1][...] = two.astype(jnp.bfloat16)
    grad = lax.dot_general(
        jnp.concatenate(rendered_all, axis=0),
        jnp.concatenate(grad_all, axis=0),
        (((0,), (0,)), ((), ())),
        preferred_element_type=jnp.float32,
    )
    grad_ref[...] = grad if len(rest) == 9 else grad + rest[4][...]


def loss(u, side, parts, head, teacher, grad, half_rows):
    teacher_width = head.shape[1]
    outs = [jax.ShapeDtypeStruct(parts[0].shape, jnp.bfloat16)] * len(parts)
    outs += [jax.ShapeDtypeStruct(head.shape, jnp.float32)]
    body = lambda *refs: loss_kernel(u, teacher_width, half_rows, *refs)
    args = (side, head, teacher) + tuple(parts) + (() if grad is None else (grad,))
    *images, grad = call(body, outs, args, 1, 3, "loss_rows", (), 20)
    return images, grad


def share_of(half_rows, sides):
    return -(-half_rows // (16 * sides)) * 16


def first_row(side, half_rows, sides):
    rows = share_of(half_rows, sides)
    return jnp.minimum(side * rows, half_rows - rows)


def deal(side, terms, starts, sides, half_rows):
    rows = share_of(half_rows, sides)

    def body(side_ref, *refs):
        for d in range(sides):
            here = first_row(side_ref[0] ^ d, half_rows, sides)
            value = 0.0
            for ref, start in zip(refs, starts):
                value = value + ref[pl.ds(pl.multiple_of(start + here, 16), rows), :].astype(jnp.float32)
            refs[len(terms) + d][...] = value.astype(jnp.bfloat16)

    out = jax.ShapeDtypeStruct((rows, terms[0].shape[1]), jnp.bfloat16)
    return call(body, [out] * sides, (side,) + tuple(terms), 1, 1, "deal_rows")


def gather(side, parts, half_rows):
    rows, lanes = parts[0].shape

    def body(side_ref, *refs):
        for d in range(len(parts)):
            start = first_row(side_ref[0] ^ d, half_rows, len(parts))
            here = pl.ds(pl.multiple_of(start, 16), rows)
            refs[-1][here, :] = refs[d][...]

    out = jax.ShapeDtypeStruct((half_rows, lanes), jnp.bfloat16)
    return call(body, out, (side,) + tuple(parts), 1, 1, "gather_rows")


def turn_teacher(side, teacher, sides, padded):
    views, width, pixels = teacher.shape
    half_rows = padded // 2
    rows = share_of(half_rows, sides)
    whole = pixels // 128 * 128
    lanes = -(-padded // 128) * 128

    def body(side_ref, teacher_ref, *rest):
        outs, (across, turned) = rest[:sides], rest[sides:]
        for u in range(views):
            across[width:, :] = jnp.zeros((256 - width, lanes), jnp.float32)
            across[0:width, whole:] = jnp.zeros((width, lanes - whole), jnp.float32)
            across[0:width, 0:pixels] = teacher_ref[u].astype(jnp.float32)
            turned[...] = across[...].T
            for d in range(sides):
                start = pl.multiple_of(first_row(side_ref[0] ^ d, half_rows, sides), 16)
                first = turned[pl.ds(start, rows), :]
                second = turned[pl.ds(half_rows + start, rows), :]
                outs[d][u] = beside(first, second).astype(jnp.bfloat16)

    out = jax.ShapeDtypeStruct((views, rows, 2 * width), jnp.bfloat16)
    scratch = [pltpu.VMEM((256, lanes), jnp.float32), pltpu.VMEM((lanes, 256), jnp.float32)]
    return call(body, [out] * sides, (side, teacher), 1, 6, "turn_teacher", scratch)


def after(value, *earlier):
    return lax.optimization_barrier((value,) + earlier)[0]


def total(*terms):
    acc = terms[0].astype(jnp.float32)
    for term in terms[1:]:
        acc = acc + term.astype(jnp.float32)
    return acc.astype(jnp.bfloat16)


def in_order(own_first, other):
    index, mine = own_first
    return jnp.where(
        index == 0, jnp.concatenate([mine, other], 0), jnp.concatenate([other, mine], 0)
    )


def per_device(points, head_weight, teacher, splat_weight, block_owner, block_local, block_row):
    peers, sides = lax.axis_size("view"), lax.axis_size("feat")
    blocks, width = points.shape[0], points.shape[1]
    view_count, visible, band_rows = splat_weight.shape[:3]
    requests = view_count * visible
    capacity = max(3, (3 * requests + 2 * peers - 1) // (2 * peers))
    quarter = -(-capacity // sides)
    slots = quarter * sides
    pixels = teacher.shape[2]
    half_rows = -(-pixels // 32) * 16
    padded = 2 * half_rows
    me, side = lax.axis_index("view"), lax.axis_index("feat")
    line, across, core = me // 2, side // 2, side % 2

    def hop(value, axis, pairs):
        return lax.ppermute(value, axis, pairs)

    def swap(value, axis, k):
        size = peers if axis == "view" else sides
        return hop(value, axis, [(i, i ^ k) for i in range(size)])

    def along(value, moves):
        return hop(value, "view", [(2 * a + y, 2 * b + y) for a, b in moves for y in range(2)])

    ints = jnp.int32
    owners = block_owner.reshape(requests)
    positions = jnp.arange(requests, dtype=ints)
    earlier = (owners[:, None] == owners[None, :]) & (positions[None, :] < positions[:, None])
    rank = jnp.sum(earlier.astype(ints), axis=1)
    peer_ids = me ^ jnp.arange(peers, dtype=ints)
    send_ranks = side * quarter + jnp.arange(quarter, dtype=ints)
    match = (owners[None, None, :] == peer_ids[:, None, None]) & (
        rank[None, None, :] == send_ranks[None, :, None]
    )
    source = jnp.sum(jnp.where(match, positions[None, None, :], 0), axis=2)
    aligned = -(-band_rows // 16) * 16
    listed = splat_weight.reshape(requests, band_rows, BLOCK)
    packed = pack_weights(source.reshape(peers * quarter), listed, peers, aligned)

    view_of = positions // visible
    start = view_of * padded + block_row.reshape(requests) * GRID
    told = jnp.stack([owners, rank, block_local.reshape(requests), start])
    heard = told[None]
    for k in (4, 2, 1):
        heard = jnp.concatenate([heard, swap(heard, "view", k)], axis=0)
    heard = heard.reshape((2, 2, 2) + told.shape).transpose(2, 1, 0, 3, 4).reshape((peers,) + told.shape)
    slot_ids = jnp.arange(slots, dtype=ints)

    def asked_of(owner, told):
        asked = (told[:, None, 0, :] == owner) & (told[:, None, 1, :] == slot_ids[None, :, None])
        filled = jnp.any(asked, axis=2)
        block = jnp.sum(jnp.where(asked, told[:, None, 2, :], 0), axis=2)
        place = jnp.sum(jnp.where(asked, told[:, None, 3, :], 0), axis=2)
        place = jnp.where(filled, place, view_count * padded)
        return jnp.sum(filled.astype(ints), axis=1), block, jnp.where(filled, block, blocks), place

    counts, block_of, pull_of, place_of = asked_of(me, heard)
    pair_counts, _, _, pair_places = asked_of(me ^ 1, heard[::2])
    turn = (slot_ids // quarter) ^ side
    turn = (turn % 2) * 2 + turn // 2
    where_of = turn * quarter + slot_ids % quarter

    weights, kept, given, arrived = {}, {}, {}, {}
    hops = []
    for j in (3, 2, 1, 0):
        got = []
        for k in (2 * j + 1, 2 * j):
            value = packed[k]
            got.append(swap(value, "view", k) if k else value)
        got = jnp.stack(got[::-1])
        if j >= 2:
            hops.append(got)
        else:
            got = after(got, given[3])
        got = jnp.concatenate([got, swap(got, "feat", 2)], axis=1)
        weights[j] = jnp.concatenate([got, swap(got, "feat", 1)], axis=1)
        k = 2 * j + 1
        given[j] = spread(counts[k : k + 1], block_of[k], where_of, weights[j][1], points)
        arrived[j] = given[j]
    arrived[3] = after(swap(given[3], "view", 1), given[2], weights[1], weights[0])
    for j in (3, 2, 1, 0):
        if j < 3:
            arrived[j] = swap(after(given[j], arrived[j + 1]), "view", 1)
        k = 2 * j
        kept[j] = render(
            counts[k : k + 1], block_of[k], place_of[k], where_of, pair_counts[j : j + 1], pair_places[j],
            weights[j][0], points, arrived[j], view_count, half_rows,
        )

    side_id = side.reshape(1).astype(ints)
    teacher = after(teacher.transpose(1, 0, 2), weights[0])
    target = turn_teacher(side_id, teacher, sides, padded)
    target = jnp.stack([swap(target[d], "feat", d) if d else target[d] for d in range(sides)])
    head_weight = after(head_weight, weights[0])
    head = jnp.concatenate([head_weight, swap(head_weight, "feat", 2)], axis=0)
    head = jnp.concatenate([head, swap(head, "feat", 1)], axis=0)

    far = along(kept[3], [(0, 1), (3, 2)])
    mid = total(kept[2], far)
    inward = along(mid, [(0, 1), (3, 2)])
    between = along(mid, [(1, 2), (2, 1)])
    back, grad, held = [], None, None
    for u in range(view_count):
        here = slice(u * half_rows, (u + 1) * half_rows)
        near = along(total(kept[1][here], between[here]), [(0, 1), (1, 0), (2, 3), (3, 2)])
        centre = along(total(kept[3][here], inward[here]), [(1, 2), (2, 1)])
        terms = (kept[0], near, centre)
        back.append(terms)
    middle = (line == 1) | (line == 2)
    images, nears, centres = [], [], []
    for u in range(view_count):
        terms = back[u]
        parts = deal(side_id, terms, (u * half_rows, 0, 0), sides, half_rows)
        parts = [swap(parts[d], "feat", d) if d else parts[d] for d in (0, 2, 1, 3)]
        if u:
            parts = after(parts, images[-1])
        parts, grad = loss(u, side_id, parts, head, target, grad, half_rows)
        held = parts[0]
        parts = [swap(part, "feat", d) if d else part for d, part in zip((0, 2, 1, 3), parts)]
        parts = [parts[i] for i in (0, 2, 1, 3)]
        if u:
            parts = after(parts, nears[-1], centres[-1])
        images.append(gather(side_id, parts, half_rows))
        nears.append(along(images[u], [(0, 1), (1, 0), (2, 3), (3, 2)]))
        centres.append(along(images[u], [(1, 2), (2, 1)]))
    near, centre = jnp.concatenate(nears, axis=0), jnp.concatenate(centres, axis=0)
    out_near = along(centre, [(1, 0), (2, 3)])
    cross = along(near, [(1, 2), (2, 1)])
    out_far = along(cross, [(1, 0), (2, 3)])
    chunks = [images, nears, [jnp.where(middle, cross, out_near)], [jnp.where(middle, centre, out_far)]]
    jobs, marks, bands, sums = {}, [], None, None
    for j in range(4):
        if j >= 2:
            ready = [jobs[k] for k in ((0, 1, 2), (3, 4))[j - 2]]
            sums = pull(ready, after(where_of, picked), sums, blocks, half_rows, False)
            if j == 3:
                chunks[j] = after(chunks[j], sums)
        picked = pick(pair_counts[j : j + 1], pair_places[j], chunks[j], slots, aligned, half_rows)
        marks.append(picked)
        bands = swap(picked if bands is None else after(picked, bands), "view", 1)
        own, other = 2 * j, 2 * j + 1
        jobs[own] = dict(
            count=counts[own : own + 1], block=pull_of[own], place=place_of[own],
            weights=weights[j][0], images=chunks[j], width=width,
        )
        jobs[other] = dict(
            count=counts[other : other + 1], block=pull_of[other],
            weights=weights[j][1], bands=bands, width=width,
        )
    sums = pull([jobs[5], jobs[6]], after(where_of, picked), sums, blocks, half_rows, False)
    grad_points = pull([jobs[7]], where_of, sums, blocks, half_rows, True)

    grad = after(grad, chunks[0]).reshape(2, 2, width, grad.shape[1])
    grad = grad[0] + swap(grad[1], "feat", 1)
    grad = grad[0] + after(swap(grad[1], "feat", 2), near)
    rows = width // 2
    low = me % 2
    mine = lax.dynamic_slice_in_dim(grad, low * rows, rows, 0)
    other = lax.dynamic_slice_in_dim(grad, (1 - low) * rows, rows, 0)
    grad = mine + after(swap(other, "view", 1), marks[2])
    sent = grad.astype(jnp.bfloat16)
    grad = grad + after(swap(sent, "view", 2), marks[3]).astype(jnp.float32)
    sent = grad.astype(jnp.bfloat16)
    grad = grad + after(swap(sent, "view", 4), sums).astype(jnp.float32)
    grad = grad / (view_count * peers * GRID)
    far = swap(after(grad.astype(jnp.bfloat16), bands), "view", 1).astype(jnp.float32)
    grad = in_order((low, grad), far)
    return (grad_points, grad)


def solution(mesh):
    size = mesh.shape
    paired = size["view"] == 8 and size["feat"] == 4
    placed = (
        P("view", "feat", None),
        P("feat", None),
        P("feat", "view", None),
        P("view", None, None, None),
        P("view", None, None),
        P("view", None),
        P("view", None),
    )
    return jax.shard_map(
        per_device if paired else per_device_listed,
        mesh=mesh,
        in_specs=placed,
        out_specs=(P("view", "feat", None), P("feat", None)),
        check_vma=False,
    )
```

```python
import jax
import jax.numpy as jnp
from jax import lax
from jax.experimental import pallas as pl
from jax.experimental.pallas import tpu as pltpu
from jax.sharding import PartitionSpec as P

GRID = 37
BAND = 2
BLOCK = 128
GROUP = 4


def slot_plan(owners, peer_count, capacity):
    total_requests = owners.shape[0]
    positions = jnp.arange(total_requests, dtype=jnp.int32)
    earlier = (owners[:, None] == owners[None, :]) & (positions[None, :] < positions[:, None])
    slot_rank = jnp.sum(earlier.astype(jnp.int32), axis=1)
    target = owners * capacity + slot_rank
    slot_ids = jnp.arange(peer_count * capacity, dtype=jnp.int32)
    matches = target[None, :] == slot_ids[:, None]
    source = jnp.sum(jnp.where(matches, positions[None, :], 0), axis=1)
    filled = jnp.any(matches, axis=1)
    return (target, source, filled)


def per_device_listed(points, head_weight, teacher, splat_weight, block_owner, block_local, block_row):
    peer_count = lax.axis_size("view")
    local_width = points.shape[1]
    view_count = splat_weight.shape[0]
    visible = splat_weight.shape[1]
    requests = view_count * visible
    capacity = max(3, (3 * requests + 2 * peer_count - 1) // (2 * peer_count))
    owners = block_owner.reshape(requests)
    local_ids = block_local.reshape(requests)
    target, source, filled = slot_plan(owners, peer_count, capacity)
    wanted = jnp.where(filled, jnp.take(local_ids, source), 0)
    columns = jnp.arange(GRID, dtype=jnp.int32)
    row_masks = [
        (block_row[:, :, None] + offset == columns[None, None, :]).astype(jnp.bfloat16)
        for offset in range(BAND)
    ]
    empty_bf = jnp.zeros((), jnp.bfloat16)
    asked_ids = lax.all_to_all(wanted, "view", split_axis=0, concat_axis=0, tiled=True)
    sent_rows = jnp.take(points, asked_ids, axis=0)
    arrived = lax.all_to_all(sent_rows, "view", split_axis=0, concat_axis=0, tiled=True)
    fetched = jnp.take(arrived, target, axis=0).reshape(view_count, visible, local_width, BLOCK)
    contrib = jnp.einsum(
        "vjcp,vjdp->vjcd", splat_weight, fetched, preferred_element_type=jnp.float32
    ).astype(jnp.bfloat16)
    rendered = jnp.zeros((view_count, GRID, GRID, local_width), jnp.float32)
    for offset in range(BAND):
        band_part = contrib[:, :, offset * GRID : (offset + 1) * GRID, :]
        rendered = rendered + jnp.einsum(
            "vjr,vjcd->vrcd", row_masks[offset], band_part, preferred_element_type=jnp.float32
        )
    rendered_rows = rendered.astype(jnp.bfloat16).reshape(view_count * GRID * GRID, local_width)
    pixel_rows = rendered_rows.shape[0]
    teacher_width = head_weight.shape[1]
    local_teacher = teacher.shape[0]
    contract_first = (((0,), (1,)), ((), ()))
    head_full = lax.all_gather(head_weight, "feat", axis=0, tiled=True)
    head_cols = lax.dynamic_slice_in_dim(
        head_full, lax.axis_index("feat") * local_teacher, local_teacher, 1
    )
    head_part = head_cols
    projected = lax.dot_general(
        head_part,
        lax.all_gather(rendered_rows, "feat", axis=1, tiled=True),
        contract_first,
        preferred_element_type=jnp.float32,
    )
    square_sum = lax.psum(jnp.sum(projected * projected, axis=0), "feat")
    scale_rows = jnp.sqrt(square_sum / teacher_width + 1e-06)
    normed = projected / scale_rows[None, :]
    target_feat = teacher.reshape(local_teacher, pixel_rows).astype(jnp.float32)
    residual = normed - target_feat
    row_dot = lax.psum(jnp.sum(residual * normed, axis=0), "feat")
    grad_proj = (
        (residual - normed * (row_dot / teacher_width)[None, :]) / scale_rows[None, :]
    ).astype(jnp.bfloat16)
    shard_part = lax.all_gather(grad_proj, "feat", axis=0, tiled=True)
    head_part = head_weight
    grad_image = lax.dot_general(
        shard_part, head_part, contract_first, preferred_element_type=jnp.float32
    )
    column_part = lax.dot_general(
        rendered_rows, shard_part, contract_first, preferred_element_type=jnp.float32
    )
    grad_head = column_part
    grad_image, grad_head = (grad_image, grad_head)
    head_grad = lax.psum(grad_head, "view") / (view_count * peer_count * GRID)
    grad_image = grad_image.astype(jnp.bfloat16).reshape(view_count, GRID, GRID, local_width)
    pieces = [
        jnp.einsum("vjr,vrcd->vjcd", row_mask, grad_image, preferred_element_type=jnp.float32)
        for row_mask in row_masks
    ]
    grad_contrib = jnp.concatenate(pieces, axis=2).astype(jnp.bfloat16)
    grad_block = jnp.einsum(
        "vjcp,vjcd->vjdp", splat_weight, grad_contrib, preferred_element_type=jnp.float32
    ).astype(jnp.bfloat16)
    grad_block = grad_block.reshape(requests, local_width, BLOCK)
    packed = jnp.where(filled[:, None, None], jnp.take(grad_block, source, axis=0), empty_bf)
    landed = lax.all_to_all(packed, "view", split_axis=0, concat_axis=0, tiled=True)
    summed = jax.ops.segment_sum(
        landed.astype(jnp.float32), asked_ids, num_segments=points.shape[0]
    )
    grad_points = summed.astype(jnp.bfloat16)
    return (grad_points, head_grad)


def price(us):
    return pl.CostEstimate(flops=int(us * 1e9), bytes_accessed=int(us * 2e6), transcendentals=0)


def call(body, out_shape, args, n_scalars, us, name, scratch=(), mib=12):
    smem = pl.BlockSpec(memory_space=pltpu.SMEM)
    vmem = pl.BlockSpec(memory_space=pltpu.VMEM)
    many = isinstance(out_shape, list)
    return pl.pallas_call(
        body,
        out_shape=out_shape,
        in_specs=[smem] * n_scalars + [vmem] * (len(args) - n_scalars),
        out_specs=[vmem] * len(out_shape) if many else vmem,
        scratch_shapes=list(scratch),
        compiler_params=pltpu.CompilerParams(vmem_limit_bytes=mib * 1024 * 1024),
        cost_estimate=price(us),
        name=name,
    )(*args)


def pack_weights(source, listed, peers, aligned):
    quarter = source.shape[0] // peers
    band_rows = listed.shape[1]
    tail = aligned - 16

    def body(source_ref, listed_ref, *outs):
        for k in range(peers):
            for i in range(quarter):
                outs[k][i, tail:aligned, :] = jnp.zeros((16, BLOCK), jnp.bfloat16)
                outs[k][i, 0:band_rows, :] = listed_ref[source_ref[k * quarter + i]]

    out = jax.ShapeDtypeStruct((quarter, aligned, BLOCK), jnp.bfloat16)
    return call(body, [out] * peers, (source, listed), 1, 3, "pack_weights")


def shifted(rows, start):
    rows = rows.astype(jnp.float32)
    rows = jnp.concatenate([rows, jnp.zeros((8, rows.shape[1]), jnp.float32)], axis=0)
    return pltpu.roll(rows, lax.rem(start, 8), 0)


def rows_at(start, band_rows):
    return pl.ds(pl.multiple_of((start // 8) * 8, 8), band_rows + 8)


def beside(first, second):
    lane = lax.broadcasted_iota(jnp.int32, (first.shape[0], 128), 1)
    second = pltpu.roll(second, 64, 1)
    middle = jnp.where(lane < 64, first[:, 128:256], second[:, 0:128])
    return jnp.concatenate([first[:, 0:128], middle, second[:, 128:256]], axis=1)


def apart(packed):
    return packed[:, 0:256], pltpu.roll(packed[:, 128:384], 192, 1)


def rounds(count, group):
    return (count + group - 1) // group


def spread(count, block, where, weight, points):
    slots, band_rows = weight.shape[:2]
    width = points.shape[1]

    def body(count_ref, block_ref, where_ref, weight_ref, points_ref, out_ref):
        blank = jnp.zeros((width, BLOCK), jnp.bfloat16)

        def group(step, carry):
            for t in range(2):
                pair = 2 * step + t
                one, two = 2 * pair, 2 * pair + 1
                weights = jnp.concatenate(
                    [weight_ref[where_ref[one]], weight_ref[where_ref[two]]], axis=1
                )
                blocks = jnp.concatenate(
                    [
                        jnp.concatenate([points_ref[block_ref[one]], blank], axis=1),
                        jnp.concatenate([blank, points_ref[block_ref[two]]], axis=1),
                    ],
                    axis=0,
                )
                out_ref[pair] = lax.dot_general(
                    weights, blocks, (((1,), (1,)), ((), ())), preferred_element_type=jnp.float32
                ).astype(jnp.bfloat16)
            return carry

        lax.fori_loop(0, rounds(count_ref[0], 4), group, 0)

    out = jax.ShapeDtypeStruct((slots // 2, band_rows, 2 * width), jnp.bfloat16)
    return call(body, out, (count, block, where, weight, points), 3, 0.1, "spread_blocks")


def render(count, block, place, where, other_count, other_place, weight, points, other, views, half_rows):
    width = points.shape[1]
    band_rows = weight.shape[1]

    def body(
        count_ref, block_ref, place_ref, where_ref, other_count_ref, other_place_ref,
        weight_ref, points_ref, other_ref, *rest
    ):
        out, acc = rest
        acc[...] = jnp.zeros_like(acc)

        def group(step, carry):
            parts = []
            for t in range(GROUP):
                slot = step * GROUP + t
                parts.append(
                    lax.dot_general(
                        shifted(weight_ref[where_ref[slot]], place_ref[slot]).astype(jnp.bfloat16),
                        points_ref[block_ref[slot]],
                        (((1,), (1,)), ((), ())),
                        preferred_element_type=jnp.float32,
                    )
                )
            for t in range(GROUP):
                acc[rows_at(place_ref[step * GROUP + t], band_rows), 0:width] += parts[t]
            return carry

        def other_group(step, carry):
            for t in range(2):
                pair = 2 * step + t
                for value, slot in zip(apart(other_ref[pair].astype(jnp.float32)), (2 * pair, 2 * pair + 1)):
                    start = other_place_ref[slot]
                    acc[rows_at(start, band_rows), :] += shifted(value, start)
            return carry

        lax.fori_loop(0, rounds(count_ref[0], GROUP), group, 0)
        lax.fori_loop(0, rounds(other_count_ref[0], 4), other_group, 0)
        for u in range(views):
            first = acc[2 * u * half_rows : (2 * u + 1) * half_rows, :]
            second = acc[(2 * u + 1) * half_rows : (2 * u + 2) * half_rows, :]
            out[u * half_rows : (u + 1) * half_rows, :] = beside(first, second).astype(out.dtype)

    images = jax.ShapeDtypeStruct((views * half_rows, 2 * width), jnp.bfloat16)
    args = (count, block, place, where, other_count, other_place, weight, points, other)
    scratch = [pltpu.VMEM((2 * views * half_rows + band_rows + 8, 256), jnp.float32)]
    return call(body, images, args, 6, 5, "render_blocks", scratch)


def unpack_images(image_refs, image, half_rows):
    views = [
        ref[i * half_rows : (i + 1) * half_rows, :]
        for ref in image_refs
        for i in range(ref.shape[0] // half_rows)
    ]
    for u, view in enumerate(views):
        first, second = apart(view.astype(jnp.float32))
        image[2 * u * half_rows : (2 * u + 1) * half_rows, :] = first
        image[(2 * u + 1) * half_rows : (2 * u + 2) * half_rows, :] = second


def pick(count, place, images, slots, band_rows, half_rows):
    pixels, packed = 2 * sum(part.shape[0] for part in images), images[0].shape[1]

    def body(count_ref, place_ref, *rest):
        image_refs, (out_ref, image) = rest[:-2], rest[-2:]
        unpack_images(image_refs, image, half_rows)
        image[pixels:, :] = jnp.zeros((band_rows + 8, 256), jnp.float32)

        def group(step, carry):
            for t in range(2):
                pair = 2 * step + t
                bands = []
                for slot in (2 * pair, 2 * pair + 1):
                    start = place_ref[slot]
                    rows = image[rows_at(start, band_rows), :]
                    back = lax.rem(band_rows + 8 - lax.rem(start, 8), band_rows + 8)
                    bands.append(pltpu.roll(rows, back, 0)[0:band_rows])
                out_ref[pair] = beside(*bands).astype(out_ref.dtype)
            return carry

        lax.fori_loop(0, rounds(count_ref[0], 4), group, 0)

    out = jax.ShapeDtypeStruct((slots // 2, band_rows, packed), jnp.bfloat16)
    scratch = [pltpu.VMEM((pixels + band_rows + 8, 256), jnp.float32)]
    return call(body, out, (count, place) + tuple(images), 2, 0.1, "pick_bands", scratch)


def pull(jobs, where, old, blocks, half_rows, last):
    band_rows = jobs[0]["weights"].shape[1]
    pixels = max([2 * sum(part.shape[0] for part in job.get("images", ())) for job in jobs])
    width = jobs[0]["width"]
    first = old is None
    tables, arrays, layout = [where], [], []
    for job in jobs:
        layout.append((len(tables), len(arrays), len(job.get("images", ()))))
        tables += [job["count"], job["block"]] + ([job["place"]] if "place" in job else [])
        arrays += [job["weights"]] + (list(job["images"]) if "place" in job else [job["bands"]])
    arrays += [] if first else [old]

    def body(*refs):
        where_ref = refs[0]
        array_refs = refs[len(tables) : len(tables) + len(arrays)]
        out_ref, image, *rest = refs[len(tables) + len(arrays) :]
        acc = rest[0] if last else out_ref
        acc[...] = jnp.zeros_like(acc) if first else array_refs[-1][...]

        for table, array, own in layout:
            count_ref, block_ref, weight_ref = refs[table], refs[table + 1], array_refs[array]
            place_ref, other_ref = refs[table + 2], array_refs[array + 1]
            if own:
                unpack_images(array_refs[array + 1 : array + 1 + own], image, half_rows)

            def group(step, carry):
                terms = []
                for t in range(GROUP):
                    slot = step * GROUP + t
                    start = place_ref[slot]
                    terms.append(
                        lax.dot_general(
                            image[rows_at(start, band_rows), 0:width].astype(jnp.bfloat16),
                            shifted(weight_ref[where_ref[slot]], start).astype(jnp.bfloat16),
                            (((0,), (0,)), ((), ())),
                            preferred_element_type=jnp.float32,
                        )
                    )
                for t in range(GROUP):
                    acc[block_ref[step * GROUP + t]] += terms[t]
                return carry

            def other_group(step, carry):
                terms = []
                for t in range(2):
                    pair = 2 * step + t
                    both = [weight_ref[where_ref[2 * pair + s]] for s in range(2)]
                    terms.append(
                        lax.dot_general(
                            other_ref[pair],
                            jnp.concatenate(both, axis=1),
                            (((0,), (0,)), ((), ())),
                            preferred_element_type=jnp.float32,
                        )
                    )
                for t in range(2):
                    pair = 2 * step + t
                    acc[block_ref[2 * pair]] += terms[t][0:width, 0:BLOCK]
                    acc[block_ref[2 * pair + 1]] += terms[t][width:, BLOCK:]
                return carry

            lax.fori_loop(0, rounds(count_ref[0], GROUP), group if own else other_group, 0)
        if last:
            out_ref[...] = acc[0:blocks].astype(out_ref.dtype)

    sums = (blocks + 1, width, BLOCK)
    out = jax.ShapeDtypeStruct((blocks, width, BLOCK), jnp.bfloat16)
    out = out if last else jax.ShapeDtypeStruct(sums, jnp.float32)
    scratch = [pltpu.VMEM((pixels + band_rows + 8, 256), jnp.float32)]
    scratch += [pltpu.VMEM(sums, jnp.float32)] if last else []
    us = 0.1
    return call(body, out, tuple(tables + arrays), len(tables), us, "pull_blocks", scratch, 24)


def loss_kernel(u, teacher_width, half_rows, side_ref, head_ref, teacher_ref, *rest):
    parts_refs, image_refs, grad_ref = rest[0:4], rest[-5:-1], rest[-1]
    rows, packed = parts_refs[0].shape
    width = packed // 2
    lane = lax.broadcasted_iota(jnp.int32, (rows, packed), 1)
    head = head_ref[...]

    def halves_of(parts):
        halves = [[], []]
        for pair in range(2):
            one, two = (part.astype(jnp.float32) for part in parts[2 * pair : 2 * pair + 2])
            halves[0].append(jnp.where(lane < width, one, pltpu.roll(two, width, 1)))
            halves[1].append(jnp.where(lane < width, pltpu.roll(one, width, 1), two))
        return [jnp.concatenate(half, axis=1) for half in halves]

    halves = halves_of([ref[...] for ref in parts_refs])
    targets = halves_of([teacher_ref[side_ref[0] ^ g, u] for g in range(4)])
    twice = side_ref[0] * rows - first_row(side_ref[0], half_rows, 4)
    counted = lax.broadcasted_iota(jnp.int32, (rows, 1), 0) >= twice
    rendered_all, grad_all, images = [], [], []
    for half in range(2):
        rendered = halves[half].astype(jnp.bfloat16)
        projected = jnp.dot(rendered, head, preferred_element_type=jnp.float32)
        square = jnp.sum(projected * projected, axis=1, keepdims=True)
        scale = jnp.sqrt(square / teacher_width + 1e-06)
        normed = projected / scale
        residual = normed - targets[half]
        inner = jnp.sum(residual * normed, axis=1, keepdims=True) / teacher_width
        grad_proj = ((residual - normed * inner) / scale).astype(jnp.bfloat16)
        images.append(
            lax.dot_general(grad_proj, head, (((1,), (1,)), ((), ())), preferred_element_type=jnp.float32)
        )
        rendered_all.append(jnp.where(counted, rendered, jnp.zeros_like(rendered)))
        grad_all.append(grad_proj)
    for pair in range(2):
        cols = slice(2 * pair * width, 2 * (pair + 1) * width)
        first, second = images[0][:, cols], images[1][:, cols]
        one = jnp.where(lane < width, first, pltpu.roll(second, width, 1))
        two = jnp.where(lane < width, pltpu.roll(first, width, 1), second)
        image_refs[2 * pair][...] = one.astype(jnp.bfloat16)
        image_refs[2 * pair + 1][...] = two.astype(jnp.bfloat16)
    grad = lax.dot_general(
        jnp.concatenate(rendered_all, axis=0),
        jnp.concatenate(grad_all, axis=0),
        (((0,), (0,)), ((), ())),
        preferred_element_type=jnp.float32,
    )
    grad_ref[...] = grad if len(rest) == 9 else grad + rest[4][...]


def loss(u, side, parts, head, teacher, grad, half_rows):
    teacher_width = head.shape[1]
    outs = [jax.ShapeDtypeStruct(parts[0].shape, jnp.bfloat16)] * len(parts)
    outs += [jax.ShapeDtypeStruct(head.shape, jnp.float32)]
    body = lambda *refs: loss_kernel(u, teacher_width, half_rows, *refs)
    args = (side, head, teacher) + tuple(parts) + (() if grad is None else (grad,))
    *images, grad = call(body, outs, args, 1, 3, "loss_rows", (), 20)
    return images, grad


def share_of(half_rows, sides):
    return -(-half_rows // (16 * sides)) * 16


def first_row(side, half_rows, sides):
    rows = share_of(half_rows, sides)
    return jnp.minimum(side * rows, half_rows - rows)


def deal(side, terms, starts, sides, half_rows):
    rows = share_of(half_rows, sides)

    def body(side_ref, *refs):
        for d in range(sides):
            here = first_row(side_ref[0] ^ d, half_rows, sides)
            value = 0.0
            for ref, start in zip(refs, starts):
                value = value + ref[pl.ds(pl.multiple_of(start + here, 16), rows), :].astype(jnp.float32)
            refs[len(terms) + d][...] = value.astype(jnp.bfloat16)

    out = jax.ShapeDtypeStruct((rows, terms[0].shape[1]), jnp.bfloat16)
    return call(body, [out] * sides, (side,) + tuple(terms), 1, 1, "deal_rows")


def gather(side, parts, half_rows):
    rows, lanes = parts[0].shape

    def body(side_ref, *refs):
        for d in range(len(parts)):
            start = first_row(side_ref[0] ^ d, half_rows, len(parts))
            here = pl.ds(pl.multiple_of(start, 16), rows)
            refs[-1][here, :] = refs[d][...]

    out = jax.ShapeDtypeStruct((half_rows, lanes), jnp.bfloat16)
    return call(body, out, (side,) + tuple(parts), 1, 1, "gather_rows")


def turn_teacher(side, teacher, sides, padded):
    views, width, pixels = teacher.shape
    half_rows = padded // 2
    rows = share_of(half_rows, sides)
    whole = pixels // 128 * 128
    lanes = -(-padded // 128) * 128

    def body(side_ref, teacher_ref, *rest):
        outs, (across, turned) = rest[:sides], rest[sides:]
        for u in range(views):
            across[width:, :] = jnp.zeros((256 - width, lanes), jnp.float32)
            across[0:width, whole:] = jnp.zeros((width, lanes - whole), jnp.float32)
            across[0:width, 0:pixels] = teacher_ref[u].astype(jnp.float32)
            turned[...] = across[...].T
            for d in range(sides):
                start = pl.multiple_of(first_row(side_ref[0] ^ d, half_rows, sides), 16)
                first = turned[pl.ds(start, rows), :]
                second = turned[pl.ds(half_rows + start, rows), :]
                outs[d][u] = beside(first, second).astype(jnp.bfloat16)

    out = jax.ShapeDtypeStruct((views, rows, 2 * width), jnp.bfloat16)
    scratch = [pltpu.VMEM((256, lanes), jnp.float32), pltpu.VMEM((lanes, 256), jnp.float32)]
    return call(body, [out] * sides, (side, teacher), 1, 6, "turn_teacher", scratch)


def after(value, *earlier):
    return lax.optimization_barrier((value,) + earlier)[0]


def total(*terms):
    acc = terms[0].astype(jnp.float32)
    for term in terms[1:]:
        acc = acc + term.astype(jnp.float32)
    return acc.astype(jnp.bfloat16)


def in_order(own_first, other):
    index, mine = own_first
    return jnp.where(
        index == 0, jnp.concatenate([mine, other], 0), jnp.concatenate([other, mine], 0)
    )


def per_device(points, head_weight, teacher, splat_weight, block_owner, block_local, block_row):
    peers, sides = lax.axis_size("view"), lax.axis_size("feat")
    blocks, width = points.shape[0], points.shape[1]
    view_count, visible, band_rows = splat_weight.shape[:3]
    requests = view_count * visible
    capacity = max(3, (3 * requests + 2 * peers - 1) // (2 * peers))
    quarter = -(-capacity // sides)
    slots = quarter * sides
    pixels = teacher.shape[2]
    half_rows = -(-pixels // 32) * 16
    padded = 2 * half_rows
    me, side = lax.axis_index("view"), lax.axis_index("feat")
    line, across, core = me // 2, side // 2, side % 2

    def hop(value, axis, pairs):
        return lax.ppermute(value, axis, pairs)

    def swap(value, axis, k):
        size = peers if axis == "view" else sides
        return hop(value, axis, [(i, i ^ k) for i in range(size)])

    def along(value, moves):
        return hop(value, "view", [(2 * a + y, 2 * b + y) for a, b in moves for y in range(2)])

    ints = jnp.int32
    owners = block_owner.reshape(requests)
    positions = jnp.arange(requests, dtype=ints)
    earlier = (owners[:, None] == owners[None, :]) & (positions[None, :] < positions[:, None])
    rank = jnp.sum(earlier.astype(ints), axis=1)
    peer_ids = me ^ jnp.arange(peers, dtype=ints)
    send_ranks = side * quarter + jnp.arange(quarter, dtype=ints)
    match = (owners[None, None, :] == peer_ids[:, None, None]) & (
        rank[None, None, :] == send_ranks[None, :, None]
    )
    source = jnp.sum(jnp.where(match, positions[None, None, :], 0), axis=2)
    aligned = -(-band_rows // 16) * 16
    listed = splat_weight.reshape(requests, band_rows, BLOCK)
    packed = pack_weights(source.reshape(peers * quarter), listed, peers, aligned)

    view_of = positions // visible
    start = view_of * padded + block_row.reshape(requests) * GRID
    told = jnp.stack([owners, rank, block_local.reshape(requests), start])
    heard = told[None]
    for k in (4, 2, 1):
        heard = jnp.concatenate([heard, swap(heard, "view", k)], axis=0)
    heard = heard.reshape((2, 2, 2) + told.shape).transpose(2, 1, 0, 3, 4).reshape((peers,) + told.shape)
    slot_ids = jnp.arange(slots, dtype=ints)

    def asked_of(owner, told):
        asked = (told[:, None, 0, :] == owner) & (told[:, None, 1, :] == slot_ids[None, :, None])
        filled = jnp.any(asked, axis=2)
        block = jnp.sum(jnp.where(asked, told[:, None, 2, :], 0), axis=2)
        place = jnp.sum(jnp.where(asked, told[:, None, 3, :], 0), axis=2)
        place = jnp.where(filled, place, view_count * padded)
        return jnp.sum(filled.astype(ints), axis=1), block, jnp.where(filled, block, blocks), place

    counts, block_of, pull_of, place_of = asked_of(me, heard)
    pair_counts, _, _, pair_places = asked_of(me ^ 1, heard[::2])
    turn = (slot_ids // quarter) ^ side
    turn = (turn % 2) * 2 + turn // 2
    where_of = turn * quarter + slot_ids % quarter

    weights, kept, given, arrived = {}, {}, {}, {}
    for j in (3, 2, 1, 0):
        got = []
        for k in (2 * j + 1, 2 * j):
            value = packed[k]
            got.append(swap(value, "view", k) if k else value)
        got = jnp.stack(got[::-1])
        if j < 2:
            got = after(got, given[3])
        got = jnp.concatenate([got, swap(got, "feat", 2)], axis=1)
        weights[j] = jnp.concatenate([got, swap(got, "feat", 1)], axis=1)
        k = 2 * j + 1
        given[j] = spread(counts[k : k + 1], block_of[k], where_of, weights[j][1], points)
        arrived[j] = given[j]
    side_id = side.reshape(1).astype(ints)
    teacher = after(teacher.transpose(1, 0, 2), weights[0])
    target = turn_teacher(side_id, teacher, sides, padded)
    target = jnp.stack([swap(target[d], "feat", d) if d else target[d] for d in range(sides)])
    head_weight = after(head_weight, weights[0])
    head = jnp.concatenate([head_weight, swap(head_weight, "feat", 2)], axis=0)
    head = jnp.concatenate([head, swap(head, "feat", 1)], axis=0)

    arrived[3] = after(swap(given[3], "view", 1), given[2], weights[1], weights[0])
    for j in (3, 2, 1, 0):
        if j < 3:
            arrived[j] = swap(after(given[j], arrived[j + 1]), "view", 1)
        k = 2 * j
        kept[j] = render(
            counts[k : k + 1], block_of[k], place_of[k], where_of, pair_counts[j : j + 1], pair_places[j],
            weights[j][0], after(points, *(head,)) if j == 1 else points, arrived[j], view_count, half_rows,
        )

    far = along(kept[3], [(0, 1), (3, 2)])
    mid = total(kept[2], far)
    inward = along(mid, [(0, 1), (3, 2)])
    between = along(mid, [(1, 2), (2, 1)])
    back, grad, held = [], None, None
    for u in range(view_count):
        here = slice(u * half_rows, (u + 1) * half_rows)
        near = along(total(kept[1][here], between[here]), [(0, 1), (1, 0), (2, 3), (3, 2)])
        centre = along(total(kept[3][here], inward[here]), [(1, 2), (2, 1)])
        terms = (kept[0], near, centre)
        back.append(terms)
    middle = (line == 1) | (line == 2)
    images, nears, centres = [], [], []
    for u in range(view_count):
        terms = back[u]
        parts = deal(side_id, terms, (u * half_rows, 0, 0), sides, half_rows)
        parts = [swap(parts[d], "feat", d) if d else parts[d] for d in (0, 2, 1, 3)]
        if u:
            parts = after(parts, images[-1])
        parts, grad = loss(u, side_id, parts, head, target, grad, half_rows)
        held = parts[0]
        parts = [swap(part, "feat", d) if d else part for d, part in zip((0, 2, 1, 3), parts)]
        parts = [parts[i] for i in (0, 2, 1, 3)]
        if u:
            parts = after(parts, nears[-1], centres[-1])
        images.append(gather(side_id, parts, half_rows))
        nears.append(along(images[u], [(0, 1), (1, 0), (2, 3), (3, 2)]))
        centres.append(along(images[u], [(1, 2), (2, 1)]))
    near, centre = jnp.concatenate(nears, axis=0), jnp.concatenate(centres, axis=0)
    out_near = along(centre, [(1, 0), (2, 3)])
    cross = along(near, [(1, 2), (2, 1)])
    out_far = along(cross, [(1, 0), (2, 3)])
    chunks = [images, nears, [jnp.where(middle, cross, out_near)], [jnp.where(middle, centre, out_far)]]
    jobs, marks, bands, sums = {}, [], None, None
    for j in range(4):
        if j >= 2:
            ready = [jobs[k] for k in ((0, 1, 2), (3, 4))[j - 2]]
            sums = pull(ready, after(where_of, picked), sums, blocks, half_rows, False)
            if j == 3:
                chunks[j] = after(chunks[j], sums)
        picked = pick(pair_counts[j : j + 1], pair_places[j], chunks[j], slots, aligned, half_rows)
        marks.append(picked)
        bands = swap(picked if bands is None else after(picked, bands), "view", 1)
        own, other = 2 * j, 2 * j + 1
        jobs[own] = dict(
            count=counts[own : own + 1], block=pull_of[own], place=place_of[own],
            weights=weights[j][0], images=chunks[j], width=width,
        )
        jobs[other] = dict(
            count=counts[other : other + 1], block=pull_of[other],
            weights=weights[j][1], bands=bands, width=width,
        )
    sums = pull([jobs[5], jobs[6]], after(where_of, picked), sums, blocks, half_rows, False)
    grad_points = pull([jobs[7]], where_of, sums, blocks, half_rows, True)

    grad = after(grad, chunks[0]).reshape(2, 2, width, grad.shape[1])
    grad = grad[0] + swap(grad[1], "feat", 1)
    grad = grad[0] + after(swap(grad[1], "feat", 2), near)
    rows = width // 2
    low = me % 2
    mine = lax.dynamic_slice_in_dim(grad, low * rows, rows, 0)
    other = lax.dynamic_slice_in_dim(grad, (1 - low) * rows, rows, 0)
    grad = mine + after(swap(other, "view", 1), marks[2])
    sent = grad.astype(jnp.bfloat16)
    grad = grad + after(swap(sent, "view", 2), marks[3]).astype(jnp.float32)
    sent = grad.astype(jnp.bfloat16)
    grad = grad + after(swap(sent, "view", 4), sums).astype(jnp.float32)
    grad = grad / (view_count * peers * GRID)
    far = swap(after(grad.astype(jnp.bfloat16), bands), "view", 1).astype(jnp.float32)
    grad = in_order((low, grad), far)
    return (grad_points, grad)


def solution(mesh):
    size = mesh.shape
    paired = size["view"] == 8 and size["feat"] == 4
    placed = (
        P("view", "feat", None),
        P("feat", None),
        P("feat", "view", None),
        P("view", None, None, None),
        P("view", None, None),
        P("view", None),
        P("view", None),
    )
    return jax.shard_map(
        per_device if paired else per_device_listed,
        mesh=mesh,
        in_specs=placed,
        out_specs=(P("view", "feat", None), P("feat", None)),
        check_vma=False,
    )
```

```python
import jax
import jax.numpy as jnp
from jax import lax
from jax.experimental import pallas as pl
from jax.experimental.pallas import tpu as pltpu
from jax.sharding import PartitionSpec as P

GRID = 37
BAND = 2
BLOCK = 128
GROUP = 4


def slot_plan(owners, peer_count, capacity):
    total_requests = owners.shape[0]
    positions = jnp.arange(total_requests, dtype=jnp.int32)
    earlier = (owners[:, None] == owners[None, :]) & (positions[None, :] < positions[:, None])
    slot_rank = jnp.sum(earlier.astype(jnp.int32), axis=1)
    target = owners * capacity + slot_rank
    slot_ids = jnp.arange(peer_count * capacity, dtype=jnp.int32)
    matches = target[None, :] == slot_ids[:, None]
    source = jnp.sum(jnp.where(matches, positions[None, :], 0), axis=1)
    filled = jnp.any(matches, axis=1)
    return (target, source, filled)


def per_device_listed(points, head_weight, teacher, splat_weight, block_owner, block_local, block_row):
    peer_count = lax.axis_size("view")
    local_width = points.shape[1]
    view_count = splat_weight.shape[0]
    visible = splat_weight.shape[1]
    requests = view_count * visible
    capacity = max(3, (3 * requests + 2 * peer_count - 1) // (2 * peer_count))
    owners = block_owner.reshape(requests)
    local_ids = block_local.reshape(requests)
    target, source, filled = slot_plan(owners, peer_count, capacity)
    wanted = jnp.where(filled, jnp.take(local_ids, source), 0)
    columns = jnp.arange(GRID, dtype=jnp.int32)
    row_masks = [
        (block_row[:, :, None] + offset == columns[None, None, :]).astype(jnp.bfloat16)
        for offset in range(BAND)
    ]
    empty_bf = jnp.zeros((), jnp.bfloat16)
    asked_ids = lax.all_to_all(wanted, "view", split_axis=0, concat_axis=0, tiled=True)
    sent_rows = jnp.take(points, asked_ids, axis=0)
    arrived = lax.all_to_all(sent_rows, "view", split_axis=0, concat_axis=0, tiled=True)
    fetched = jnp.take(arrived, target, axis=0).reshape(view_count, visible, local_width, BLOCK)
    contrib = jnp.einsum(
        "vjcp,vjdp->vjcd", splat_weight, fetched, preferred_element_type=jnp.float32
    ).astype(jnp.bfloat16)
    rendered = jnp.zeros((view_count, GRID, GRID, local_width), jnp.float32)
    for offset in range(BAND):
        band_part = contrib[:, :, offset * GRID : (offset + 1) * GRID, :]
        rendered = rendered + jnp.einsum(
            "vjr,vjcd->vrcd", row_masks[offset], band_part, preferred_element_type=jnp.float32
        )
    rendered_rows = rendered.astype(jnp.bfloat16).reshape(view_count * GRID * GRID, local_width)
    pixel_rows = rendered_rows.shape[0]
    teacher_width = head_weight.shape[1]
    local_teacher = teacher.shape[0]
    contract_first = (((0,), (1,)), ((), ()))
    head_full = lax.all_gather(head_weight, "feat", axis=0, tiled=True)
    head_cols = lax.dynamic_slice_in_dim(
        head_full, lax.axis_index("feat") * local_teacher, local_teacher, 1
    )
    head_part = head_cols
    projected = lax.dot_general(
        head_part,
        lax.all_gather(rendered_rows, "feat", axis=1, tiled=True),
        contract_first,
        preferred_element_type=jnp.float32,
    )
    square_sum = lax.psum(jnp.sum(projected * projected, axis=0), "feat")
    scale_rows = jnp.sqrt(square_sum / teacher_width + 1e-06)
    normed = projected / scale_rows[None, :]
    target_feat = teacher.reshape(local_teacher, pixel_rows).astype(jnp.float32)
    residual = normed - target_feat
    row_dot = lax.psum(jnp.sum(residual * normed, axis=0), "feat")
    grad_proj = (
        (residual - normed * (row_dot / teacher_width)[None, :]) / scale_rows[None, :]
    ).astype(jnp.bfloat16)
    shard_part = lax.all_gather(grad_proj, "feat", axis=0, tiled=True)
    head_part = head_weight
    grad_image = lax.dot_general(
        shard_part, head_part, contract_first, preferred_element_type=jnp.float32
    )
    column_part = lax.dot_general(
        rendered_rows, shard_part, contract_first, preferred_element_type=jnp.float32
    )
    grad_head = column_part
    grad_image, grad_head = (grad_image, grad_head)
    head_grad = lax.psum(grad_head, "view") / (view_count * peer_count * GRID)
    grad_image = grad_image.astype(jnp.bfloat16).reshape(view_count, GRID, GRID, local_width)
    pieces = [
        jnp.einsum("vjr,vrcd->vjcd", row_mask, grad_image, preferred_element_type=jnp.float32)
        for row_mask in row_masks
    ]
    grad_contrib = jnp.concatenate(pieces, axis=2).astype(jnp.bfloat16)
    grad_block = jnp.einsum(
        "vjcp,vjcd->vjdp", splat_weight, grad_contrib, preferred_element_type=jnp.float32
    ).astype(jnp.bfloat16)
    grad_block = grad_block.reshape(requests, local_width, BLOCK)
    packed = jnp.where(filled[:, None, None], jnp.take(grad_block, source, axis=0), empty_bf)
    landed = lax.all_to_all(packed, "view", split_axis=0, concat_axis=0, tiled=True)
    summed = jax.ops.segment_sum(
        landed.astype(jnp.float32), asked_ids, num_segments=points.shape[0]
    )
    grad_points = summed.astype(jnp.bfloat16)
    return (grad_points, head_grad)


def price(us):
    return pl.CostEstimate(flops=int(us * 1e9), bytes_accessed=int(us * 2e6), transcendentals=0)


def call(body, out_shape, args, n_scalars, us, name, scratch=(), mib=12):
    smem = pl.BlockSpec(memory_space=pltpu.SMEM)
    vmem = pl.BlockSpec(memory_space=pltpu.VMEM)
    many = isinstance(out_shape, list)
    return pl.pallas_call(
        body,
        out_shape=out_shape,
        in_specs=[smem] * n_scalars + [vmem] * (len(args) - n_scalars),
        out_specs=[vmem] * len(out_shape) if many else vmem,
        scratch_shapes=list(scratch),
        compiler_params=pltpu.CompilerParams(vmem_limit_bytes=mib * 1024 * 1024),
        cost_estimate=price(us),
        name=name,
    )(*args)


def pack_weights(source, listed, peers, aligned):
    quarter = source.shape[0] // peers
    band_rows = listed.shape[1]
    tail = aligned - 16

    def body(source_ref, listed_ref, *outs):
        for k in range(peers):
            for i in range(quarter):
                outs[k][i, tail:aligned, :] = jnp.zeros((16, BLOCK), jnp.bfloat16)
                outs[k][i, 0:band_rows, :] = listed_ref[source_ref[k * quarter + i]]

    out = jax.ShapeDtypeStruct((quarter, aligned, BLOCK), jnp.bfloat16)
    return call(body, [out] * peers, (source, listed), 1, 3, "pack_weights")


def shifted(rows, start):
    rows = rows.astype(jnp.float32)
    rows = jnp.concatenate([rows, jnp.zeros((8, rows.shape[1]), jnp.float32)], axis=0)
    return pltpu.roll(rows, lax.rem(start, 8), 0)


def rows_at(start, band_rows):
    return pl.ds(pl.multiple_of((start // 8) * 8, 8), band_rows + 8)


def beside(first, second):
    lane = lax.broadcasted_iota(jnp.int32, (first.shape[0], 128), 1)
    second = pltpu.roll(second, 64, 1)
    middle = jnp.where(lane < 64, first[:, 128:256], second[:, 0:128])
    return jnp.concatenate([first[:, 0:128], middle, second[:, 128:256]], axis=1)


def apart(packed):
    return packed[:, 0:256], pltpu.roll(packed[:, 128:384], 192, 1)


def rounds(count, group):
    return (count + group - 1) // group


def spread(count, block, where, weight, points):
    slots, band_rows = weight.shape[:2]
    width = points.shape[1]

    def body(count_ref, block_ref, where_ref, weight_ref, points_ref, out_ref):
        blank = jnp.zeros((width, BLOCK), jnp.bfloat16)

        def group(step, carry):
            for t in range(2):
                pair = 2 * step + t
                one, two = 2 * pair, 2 * pair + 1
                weights = jnp.concatenate(
                    [weight_ref[where_ref[one]], weight_ref[where_ref[two]]], axis=1
                )
                blocks = jnp.concatenate(
                    [
                        jnp.concatenate([points_ref[block_ref[one]], blank], axis=1),
                        jnp.concatenate([blank, points_ref[block_ref[two]]], axis=1),
                    ],
                    axis=0,
                )
                out_ref[pair] = lax.dot_general(
                    weights, blocks, (((1,), (1,)), ((), ())), preferred_element_type=jnp.float32
                ).astype(jnp.bfloat16)
            return carry

        lax.fori_loop(0, rounds(count_ref[0], 4), group, 0)

    out = jax.ShapeDtypeStruct((slots // 2, band_rows, 2 * width), jnp.bfloat16)
    return call(body, out, (count, block, where, weight, points), 3, 0.1, "spread_blocks")


def render(count, block, place, where, other_count, other_place, weight, points, other, views, half_rows):
    width = points.shape[1]
    band_rows = weight.shape[1]

    def body(
        count_ref, block_ref, place_ref, where_ref, other_count_ref, other_place_ref,
        weight_ref, points_ref, other_ref, *rest
    ):
        out, acc = rest
        acc[...] = jnp.zeros_like(acc)

        def group(step, carry):
            parts = []
            for t in range(GROUP):
                slot = step * GROUP + t
                parts.append(
                    lax.dot_general(
                        shifted(weight_ref[where_ref[slot]], place_ref[slot]).astype(jnp.bfloat16),
                        points_ref[block_ref[slot]],
                        (((1,), (1,)), ((), ())),
                        preferred_element_type=jnp.float32,
                    )
                )
            for t in range(GROUP):
                acc[rows_at(place_ref[step * GROUP + t], band_rows), 0:width] += parts[t]
            return carry

        def other_group(step, carry):
            for t in range(2):
                pair = 2 * step + t
                for value, slot in zip(apart(other_ref[pair].astype(jnp.float32)), (2 * pair, 2 * pair + 1)):
                    start = other_place_ref[slot]
                    acc[rows_at(start, band_rows), :] += shifted(value, start)
            return carry

        lax.fori_loop(0, rounds(count_ref[0], GROUP), group, 0)
        lax.fori_loop(0, rounds(other_count_ref[0], 4), other_group, 0)
        for u in range(views):
            first = acc[2 * u * half_rows : (2 * u + 1) * half_rows, :]
            second = acc[(2 * u + 1) * half_rows : (2 * u + 2) * half_rows, :]
            out[u * half_rows : (u + 1) * half_rows, :] = beside(first, second).astype(out.dtype)

    images = jax.ShapeDtypeStruct((views * half_rows, 2 * width), jnp.bfloat16)
    args = (count, block, place, where, other_count, other_place, weight, points, other)
    scratch = [pltpu.VMEM((2 * views * half_rows + band_rows + 8, 256), jnp.float32)]
    return call(body, images, args, 6, 5, "render_blocks", scratch)


def unpack_images(image_refs, image, half_rows):
    views = [
        ref[i * half_rows : (i + 1) * half_rows, :]
        for ref in image_refs
        for i in range(ref.shape[0] // half_rows)
    ]
    for u, view in enumerate(views):
        first, second = apart(view.astype(jnp.float32))
        image[2 * u * half_rows : (2 * u + 1) * half_rows, :] = first
        image[(2 * u + 1) * half_rows : (2 * u + 2) * half_rows, :] = second


def pick(count, place, images, slots, band_rows, half_rows):
    pixels, packed = 2 * sum(part.shape[0] for part in images), images[0].shape[1]

    def body(count_ref, place_ref, *rest):
        image_refs, (out_ref, image) = rest[:-2], rest[-2:]
        unpack_images(image_refs, image, half_rows)
        image[pixels:, :] = jnp.zeros((band_rows + 8, 256), jnp.float32)

        def group(step, carry):
            for t in range(2):
                pair = 2 * step + t
                bands = []
                for slot in (2 * pair, 2 * pair + 1):
                    start = place_ref[slot]
                    rows = image[rows_at(start, band_rows), :]
                    back = lax.rem(band_rows + 8 - lax.rem(start, 8), band_rows + 8)
                    bands.append(pltpu.roll(rows, back, 0)[0:band_rows])
                out_ref[pair] = beside(*bands).astype(out_ref.dtype)
            return carry

        lax.fori_loop(0, rounds(count_ref[0], 4), group, 0)

    out = jax.ShapeDtypeStruct((slots // 2, band_rows, packed), jnp.bfloat16)
    scratch = [pltpu.VMEM((pixels + band_rows + 8, 256), jnp.float32)]
    return call(body, out, (count, place) + tuple(images), 2, 0.1, "pick_bands", scratch)


def pull(jobs, where, old, blocks, half_rows, last):
    band_rows = jobs[0]["weights"].shape[1]
    pixels = max([2 * sum(part.shape[0] for part in job.get("images", ())) for job in jobs])
    width = jobs[0]["width"]
    first = old is None
    tables, arrays, layout = [where], [], []
    for job in jobs:
        layout.append((len(tables), len(arrays), len(job.get("images", ()))))
        tables += [job["count"], job["block"]] + ([job["place"]] if "place" in job else [])
        arrays += [job["weights"]] + (list(job["images"]) if "place" in job else [job["bands"]])
    arrays += [] if first else [old]

    def body(*refs):
        where_ref = refs[0]
        array_refs = refs[len(tables) : len(tables) + len(arrays)]
        out_ref, image, *rest = refs[len(tables) + len(arrays) :]
        acc = rest[0] if last else out_ref
        acc[...] = jnp.zeros_like(acc) if first else array_refs[-1][...]

        for table, array, own in layout:
            count_ref, block_ref, weight_ref = refs[table], refs[table + 1], array_refs[array]
            place_ref, other_ref = refs[table + 2], array_refs[array + 1]
            if own:
                unpack_images(array_refs[array + 1 : array + 1 + own], image, half_rows)

            def group(step, carry):
                terms = []
                for t in range(GROUP):
                    slot = step * GROUP + t
                    start = place_ref[slot]
                    terms.append(
                        lax.dot_general(
                            image[rows_at(start, band_rows), 0:width].astype(jnp.bfloat16),
                            shifted(weight_ref[where_ref[slot]], start).astype(jnp.bfloat16),
                            (((0,), (0,)), ((), ())),
                            preferred_element_type=jnp.float32,
                        )
                    )
                for t in range(GROUP):
                    acc[block_ref[step * GROUP + t]] += terms[t]
                return carry

            def other_group(step, carry):
                terms = []
                for t in range(2):
                    pair = 2 * step + t
                    both = [weight_ref[where_ref[2 * pair + s]] for s in range(2)]
                    terms.append(
                        lax.dot_general(
                            other_ref[pair],
                            jnp.concatenate(both, axis=1),
                            (((0,), (0,)), ((), ())),
                            preferred_element_type=jnp.float32,
                        )
                    )
                for t in range(2):
                    pair = 2 * step + t
                    acc[block_ref[2 * pair]] += terms[t][0:width, 0:BLOCK]
                    acc[block_ref[2 * pair + 1]] += terms[t][width:, BLOCK:]
                return carry

            lax.fori_loop(0, rounds(count_ref[0], GROUP), group if own else other_group, 0)
        if last:
            out_ref[...] = acc[0:blocks].astype(out_ref.dtype)

    sums = (blocks + 1, width, BLOCK)
    out = jax.ShapeDtypeStruct((blocks, width, BLOCK), jnp.bfloat16)
    out = out if last else jax.ShapeDtypeStruct(sums, jnp.float32)
    scratch = [pltpu.VMEM((pixels + band_rows + 8, 256), jnp.float32)]
    scratch += [pltpu.VMEM(sums, jnp.float32)] if last else []
    us = 0.1
    return call(body, out, tuple(tables + arrays), len(tables), us, "pull_blocks", scratch, 24)


def loss_kernel(u, teacher_width, half_rows, side_ref, head_ref, teacher_ref, *rest):
    parts_refs, image_refs, grad_ref = rest[0:4], rest[-5:-1], rest[-1]
    rows, packed = parts_refs[0].shape
    width = packed // 2
    lane = lax.broadcasted_iota(jnp.int32, (rows, packed), 1)
    head = head_ref[...]

    def halves_of(parts):
        halves = [[], []]
        for pair in range(2):
            one, two = (part.astype(jnp.float32) for part in parts[2 * pair : 2 * pair + 2])
            halves[0].append(jnp.where(lane < width, one, pltpu.roll(two, width, 1)))
            halves[1].append(jnp.where(lane < width, pltpu.roll(one, width, 1), two))
        return [jnp.concatenate(half, axis=1) for half in halves]

    halves = halves_of([ref[...] for ref in parts_refs])
    targets = halves_of([teacher_ref[side_ref[0] ^ g, u] for g in range(4)])
    twice = side_ref[0] * rows - first_row(side_ref[0], half_rows, 4)
    counted = lax.broadcasted_iota(jnp.int32, (rows, 1), 0) >= twice
    rendered_all, grad_all, images = [], [], []
    for half in range(2):
        rendered = halves[half].astype(jnp.bfloat16)
        projected = jnp.dot(rendered, head, preferred_element_type=jnp.float32)
        square = jnp.sum(projected * projected, axis=1, keepdims=True)
        scale = jnp.sqrt(square / teacher_width + 1e-06)
        normed = projected / scale
        residual = normed - targets[half]
        inner = jnp.sum(residual * normed, axis=1, keepdims=True) / teacher_width
        grad_proj = ((residual - normed * inner) / scale).astype(jnp.bfloat16)
        images.append(
            lax.dot_general(grad_proj, head, (((1,), (1,)), ((), ())), preferred_element_type=jnp.float32)
        )
        rendered_all.append(jnp.where(counted, rendered, jnp.zeros_like(rendered)))
        grad_all.append(grad_proj)
    for pair in range(2):
        cols = slice(2 * pair * width, 2 * (pair + 1) * width)
        first, second = images[0][:, cols], images[1][:, cols]
        one = jnp.where(lane < width, first, pltpu.roll(second, width, 1))
        two = jnp.where(lane < width, pltpu.roll(first, width, 1), second)
        image_refs[2 * pair][...] = one.astype(jnp.bfloat16)
        image_refs[2 * pair + 1][...] = two.astype(jnp.bfloat16)
    grad = lax.dot_general(
        jnp.concatenate(rendered_all, axis=0),
        jnp.concatenate(grad_all, axis=0),
        (((0,), (0,)), ((), ())),
        preferred_element_type=jnp.float32,
    )
    grad_ref[...] = grad if len(rest) == 9 else grad + rest[4][...]


def loss(u, side, parts, head, teacher, grad, half_rows):
    teacher_width = head.shape[1]
    outs = [jax.ShapeDtypeStruct(parts[0].shape, jnp.bfloat16)] * len(parts)
    outs += [jax.ShapeDtypeStruct(head.shape, jnp.float32)]
    body = lambda *refs: loss_kernel(u, teacher_width, half_rows, *refs)
    args = (side, head, teacher) + tuple(parts) + (() if grad is None else (grad,))
    *images, grad = call(body, outs, args, 1, 3, "loss_rows", (), 20)
    return images, grad


def share_of(half_rows, sides):
    return -(-half_rows // (16 * sides)) * 16


def first_row(side, half_rows, sides):
    rows = share_of(half_rows, sides)
    return jnp.minimum(side * rows, half_rows - rows)


def deal(side, terms, starts, sides, half_rows):
    rows = share_of(half_rows, sides)

    def body(side_ref, *refs):
        for d in range(sides):
            here = first_row(side_ref[0] ^ d, half_rows, sides)
            value = 0.0
            for ref, start in zip(refs, starts):
                value = value + ref[pl.ds(pl.multiple_of(start + here, 16), rows), :].astype(jnp.float32)
            refs[len(terms) + d][...] = value.astype(jnp.bfloat16)

    out = jax.ShapeDtypeStruct((rows, terms[0].shape[1]), jnp.bfloat16)
    return call(body, [out] * sides, (side,) + tuple(terms), 1, 3, "deal_rows")


def gather(side, parts, half_rows):
    rows, lanes = parts[0].shape

    def body(side_ref, *refs):
        for d in range(len(parts)):
            start = first_row(side_ref[0] ^ d, half_rows, len(parts))
            here = pl.ds(pl.multiple_of(start, 16), rows)
            refs[-1][here, :] = refs[d][...]

    out = jax.ShapeDtypeStruct((half_rows, lanes), jnp.bfloat16)
    return call(body, out, (side,) + tuple(parts), 1, 3, "gather_rows")


def turn_teacher(side, teacher, sides, padded):
    views, width, pixels = teacher.shape
    half_rows = padded // 2
    rows = share_of(half_rows, sides)
    whole = pixels // 128 * 128
    lanes = -(-padded // 128) * 128

    def body(side_ref, teacher_ref, *rest):
        outs, (across, turned) = rest[:sides], rest[sides:]
        for u in range(views):
            across[width:, :] = jnp.zeros((256 - width, lanes), jnp.float32)
            across[0:width, whole:] = jnp.zeros((width, lanes - whole), jnp.float32)
            across[0:width, 0:pixels] = teacher_ref[u].astype(jnp.float32)
            turned[...] = across[...].T
            for d in range(sides):
                start = pl.multiple_of(first_row(side_ref[0] ^ d, half_rows, sides), 16)
                first = turned[pl.ds(start, rows), :]
                second = turned[pl.ds(half_rows + start, rows), :]
                outs[d][u] = beside(first, second).astype(jnp.bfloat16)

    out = jax.ShapeDtypeStruct((views, rows, 2 * width), jnp.bfloat16)
    scratch = [pltpu.VMEM((256, lanes), jnp.float32), pltpu.VMEM((lanes, 256), jnp.float32)]
    return call(body, [out] * sides, (side, teacher), 1, 6, "turn_teacher", scratch)


def after(value, *earlier):
    return lax.optimization_barrier((value,) + earlier)[0]


def total(*terms):
    acc = terms[0].astype(jnp.float32)
    for term in terms[1:]:
        acc = acc + term.astype(jnp.float32)
    return acc.astype(jnp.bfloat16)


def in_order(own_first, other):
    index, mine = own_first
    return jnp.where(
        index == 0, jnp.concatenate([mine, other], 0), jnp.concatenate([other, mine], 0)
    )


def per_device(points, head_weight, teacher, splat_weight, block_owner, block_local, block_row):
    peers, sides = lax.axis_size("view"), lax.axis_size("feat")
    blocks, width = points.shape[0], points.shape[1]
    view_count, visible, band_rows = splat_weight.shape[:3]
    requests = view_count * visible
    capacity = max(3, (3 * requests + 2 * peers - 1) // (2 * peers))
    quarter = -(-capacity // sides)
    slots = quarter * sides
    pixels = teacher.shape[2]
    half_rows = -(-pixels // 32) * 16
    padded = 2 * half_rows
    me, side = lax.axis_index("view"), lax.axis_index("feat")
    line, across, core = me // 2, side // 2, side % 2

    def hop(value, axis, pairs):
        return lax.ppermute(value, axis, pairs)

    def swap(value, axis, k):
        size = peers if axis == "view" else sides
        return hop(value, axis, [(i, i ^ k) for i in range(size)])

    def along(value, moves):
        return hop(value, "view", [(2 * a + y, 2 * b + y) for a, b in moves for y in range(2)])

    ints = jnp.int32
    owners = block_owner.reshape(requests)
    positions = jnp.arange(requests, dtype=ints)
    earlier = (owners[:, None] == owners[None, :]) & (positions[None, :] < positions[:, None])
    rank = jnp.sum(earlier.astype(ints), axis=1)
    peer_ids = me ^ jnp.arange(peers, dtype=ints)
    send_ranks = side * quarter + jnp.arange(quarter, dtype=ints)
    match = (owners[None, None, :] == peer_ids[:, None, None]) & (
        rank[None, None, :] == send_ranks[None, :, None]
    )
    source = jnp.sum(jnp.where(match, positions[None, None, :], 0), axis=2)
    aligned = -(-band_rows // 16) * 16
    listed = splat_weight.reshape(requests, band_rows, BLOCK)
    packed = pack_weights(source.reshape(peers * quarter), listed, peers, aligned)

    view_of = positions // visible
    start = view_of * padded + block_row.reshape(requests) * GRID
    told = jnp.stack([owners, rank, block_local.reshape(requests), start])
    heard = told[None]
    for k in (4, 2, 1):
        heard = jnp.concatenate([heard, swap(heard, "view", k)], axis=0)
    heard = heard.reshape((2, 2, 2) + told.shape).transpose(2, 1, 0, 3, 4).reshape((peers,) + told.shape)
    slot_ids = jnp.arange(slots, dtype=ints)

    def asked_of(owner, told):
        asked = (told[:, None, 0, :] == owner) & (told[:, None, 1, :] == slot_ids[None, :, None])
        filled = jnp.any(asked, axis=2)
        block = jnp.sum(jnp.where(asked, told[:, None, 2, :], 0), axis=2)
        place = jnp.sum(jnp.where(asked, told[:, None, 3, :], 0), axis=2)
        place = jnp.where(filled, place, view_count * padded)
        return jnp.sum(filled.astype(ints), axis=1), block, jnp.where(filled, block, blocks), place

    counts, block_of, pull_of, place_of = asked_of(me, heard)
    pair_counts, _, _, pair_places = asked_of(me ^ 1, heard[::2])
    turn = (slot_ids // quarter) ^ side
    turn = (turn % 2) * 2 + turn // 2
    where_of = turn * quarter + slot_ids % quarter

    weights, kept, given, arrived = {}, {}, {}, {}
    for j in (3, 2, 1, 0):
        got = []
        for k in (2 * j + 1, 2 * j):
            value = packed[k]
            got.append(swap(value, "view", k) if k else value)
        got = jnp.stack(got[::-1])
        if j < 2:
            got = after(got, given[3])
        got = jnp.concatenate([got, swap(got, "feat", 2)], axis=1)
        weights[j] = jnp.concatenate([got, swap(got, "feat", 1)], axis=1)
        k = 2 * j + 1
        given[j] = spread(counts[k : k + 1], block_of[k], where_of, weights[j][1], points)
        arrived[j] = given[j]
    side_id = side.reshape(1).astype(ints)
    teacher = after(teacher.transpose(1, 0, 2), weights[0])
    target = turn_teacher(side_id, teacher, sides, padded)
    target = jnp.stack([swap(target[d], "feat", d) if d else target[d] for d in range(sides)])
    head_weight = after(head_weight, weights[0])
    head = jnp.concatenate([head_weight, swap(head_weight, "feat", 2)], axis=0)
    head = jnp.concatenate([head, swap(head, "feat", 1)], axis=0)

    arrived[3] = after(swap(given[3], "view", 1), given[2], weights[1], weights[0])
    for j in (3, 2, 1, 0):
        if j < 3:
            arrived[j] = swap(after(given[j], arrived[j + 1]), "view", 1)
        k = 2 * j
        kept[j] = render(
            counts[k : k + 1], block_of[k], place_of[k], where_of, pair_counts[j : j + 1], pair_places[j],
            weights[j][0], after(points, *(head,)) if j == 1 else points, arrived[j], view_count, half_rows,
        )

    far = along(kept[3], [(0, 1), (3, 2)])
    mid = total(kept[2], far)
    inward = along(mid, [(0, 1), (3, 2)])
    between = along(mid, [(1, 2), (2, 1)])
    back, grad, held = [], None, None
    for u in range(view_count):
        here = slice(u * half_rows, (u + 1) * half_rows)
        near = along(total(kept[1][here], between[here]), [(0, 1), (1, 0), (2, 3), (3, 2)])
        centre = along(total(kept[3][here], inward[here]), [(1, 2), (2, 1)])
        terms = (kept[0], near, centre)
        back.append(terms)
    middle = (line == 1) | (line == 2)
    images, nears, centres = [], [], []
    for u in range(view_count):
        terms = back[u]
        parts = deal(side_id, terms, (u * half_rows, 0, 0), sides, half_rows)
        parts = [swap(parts[d], "feat", d) if d else parts[d] for d in (0, 2, 1, 3)]
        if u:
            parts = after(parts, images[-1])
        parts, grad = loss(u, side_id, parts, head, target, grad, half_rows)
        held = parts[0]
        parts = [swap(part, "feat", d) if d else part for d, part in zip((0, 2, 1, 3), parts)]
        parts = [parts[i] for i in (0, 2, 1, 3)]
        if u:
            parts = after(parts, nears[-1], centres[-1])
        images.append(gather(side_id, parts, half_rows))
        nears.append(along(images[u], [(0, 1), (1, 0), (2, 3), (3, 2)]))
        centres.append(along(images[u], [(1, 2), (2, 1)]))
    near, centre = jnp.concatenate(nears, axis=0), jnp.concatenate(centres, axis=0)
    out_near = along(centre, [(1, 0), (2, 3)])
    cross = along(near, [(1, 2), (2, 1)])
    out_far = along(cross, [(1, 0), (2, 3)])
    chunks = [images, nears, [jnp.where(middle, cross, out_near)], [jnp.where(middle, centre, out_far)]]
    jobs, marks, bands, sums = {}, [], None, None
    for j in range(4):
        if j >= 2:
            ready = [jobs[k] for k in ((0, 1, 2), (3, 4))[j - 2]]
            sums = pull(ready, after(where_of, picked), sums, blocks, half_rows, False)
            if j == 3:
                chunks[j] = after(chunks[j], sums)
        picked = pick(pair_counts[j : j + 1], pair_places[j], chunks[j], slots, aligned, half_rows)
        marks.append(picked)
        bands = swap(picked if bands is None else after(picked, bands), "view", 1)
        own, other = 2 * j, 2 * j + 1
        jobs[own] = dict(
            count=counts[own : own + 1], block=pull_of[own], place=place_of[own],
            weights=weights[j][0], images=chunks[j], width=width,
        )
        jobs[other] = dict(
            count=counts[other : other + 1], block=pull_of[other],
            weights=weights[j][1], bands=bands, width=width,
        )
    sums = pull([jobs[5], jobs[6]], after(where_of, picked), sums, blocks, half_rows, False)
    grad_points = pull([jobs[7]], where_of, sums, blocks, half_rows, True)

    grad = after(grad, chunks[0]).reshape(2, 2, width, grad.shape[1])
    grad = grad[0] + swap(grad[1], "feat", 1)
    grad = grad[0] + after(swap(grad[1], "feat", 2), near)
    rows = width // 2
    low = me % 2
    mine = lax.dynamic_slice_in_dim(grad, low * rows, rows, 0)
    other = lax.dynamic_slice_in_dim(grad, (1 - low) * rows, rows, 0)
    grad = mine + after(swap(other.astype(jnp.bfloat16), "view", 1), marks[2]).astype(jnp.float32)
    sent = grad.astype(jnp.bfloat16)
    grad = grad + after(swap(sent, "view", 2), marks[3]).astype(jnp.float32)
    sent = grad.astype(jnp.bfloat16)
    grad = grad + after(swap(sent, "view", 4), sums).astype(jnp.float32)
    grad = grad / (view_count * peers * GRID)
    far = swap(after(grad.astype(jnp.bfloat16), bands), "view", 1).astype(jnp.float32)
    grad = in_order((low, grad), far)
    return (grad_points, grad)


def solution(mesh):
    size = mesh.shape
    paired = size["view"] == 8 and size["feat"] == 4
    placed = (
        P("view", "feat", None),
        P("feat", None),
        P("feat", "view", None),
        P("view", None, None, None),
        P("view", None, None),
        P("view", None),
        P("view", None),
    )
    return jax.shard_map(
        per_device if paired else per_device_listed,
        mesh=mesh,
        in_specs=placed,
        out_specs=(P("view", "feat", None), P("feat", None)),
        check_vma=False,
    )
```
